32 devices in a mesh: dp: 8 (over y, x, core), rows: 4 (over z).
Axes of the slice: x: 2, y: 2, z: 4, core: 2. Of those that a mesh axis runs over, the one named last changes fastest.
Arguments:
- tokens: bfloat16 [32, 28, 70, 384], P('dp', 'rows'), may hold values from -6 to 6
- heights: int32 [32], P('dp'), may hold values from 1 to 4, as said below
- conv_weight: bfloat16 [4, 3, 3, 384], replicated, may hold values from -2 to 2
- conv_bias: bfloat16 [4, 384], replicated, may hold values from -1.5 to 1.5
- norm_gain: bfloat16 [4, 384], replicated, may hold values from 0.5 to 1.5
- norm_shift: bfloat16 [4, 384], replicated, may hold values from -1 to 1
- mix_weight: bfloat16 [2, 384, 1152], replicated, may hold values from -0.3125 to 0.3125
- window_bias: bfloat16 [768], replicated, may hold values from -1.5 to 1.5
- channel_bias: bfloat16 [1152], replicated, may hold values from -0.5 to 0.5
- out_weight: bfloat16 [2, 384, 384], replicated, may hold values from -0.875 to 0.875
- out_bias: bfloat16 [2, 384], replicated, may hold values from -1.5 to 1.5
- up_weight: bfloat16 [2, 384, 1536], replicated, may hold values from -0.3125 to 0.3125
- up_bias: bfloat16 [2, 1536], replicated, may hold values from -1.5 to 1.5
- down_weight: bfloat16 [2, 1536, 384], replicated, may hold values from -0.15625 to 0.15625
- down_bias: bfloat16 [2, 384], replicated, may hold values from -1.5 to 1.5
- cotangent: bfloat16 [32, 28, 70, 384], P('dp', 'rows'), may hold values from -6 to 6
Outputs:
- result: bfloat16 [32, 28, 70, 384], P('dp', 'rows')
- tokens_grad: float32 [32, 28, 70, 384], P('dp', 'rows')
- conv_weight_grad: float32 [4, 3, 3, 384], replicated
- conv_bias_grad: float32 [4, 384], replicated
- norm_gain_grad: float32 [4, 384], replicated
- norm_shift_grad: float32 [3, 384], replicated
- final_shift_grad: float32 [384], replicated
- mix_weight_grad: float32 [2, 384, 1152], replicated
- window_bias_grad: float32 [768], replicated
- channel_bias_grad: float32 [1152], replicated
- out_weight_grad: float32 [2, 384, 384], replicated
- out_bias_grad: float32 [2, 384], replicated
- up_weight_grad: float32 [2, 384, 1536], replicated
- up_bias_grad: float32 [2, 1536], replicated
- down_weight_grad: float32 [2, 1536, 384], replicated
- down_bias_grad: float32 [2, 384], replicated
The draws below stay inside these ranges and needn't reach their ends.
Inputs may be any that keep to these rules, and one draw needn't show every extreme that they name: `heights`: in each block of 4 images of one index of dp, one image is 4 window rows tall.
All inputs are finite; a program needn't handle non-finite values.
Results may differ from the reference program's by a relative error of at most 0.019.
Values may be sent and summed in bfloat16 or wider, within the bound.
No kernel may reach another device: no remote copies, remote signals or barrier semaphores. Data moves between devices by JAX's collectives and lax.ppermute only.
A program may use at most 320 MiB of HBM per device.

```python
import jax
import jax.numpy as jnp
from jax import lax

HEADS = 12
HEAD_DIM = 32
FF = 1536
C = 384
IMG_DEV = 4
WIDTH = 70
WROWS = 4
HEIGHT = 28
IMAGES = 32


def draw_heights(key, part):
    key = jax.random.fold_in(key, 7)
    base_key, choose_key = jax.random.split(key)
    base_rows = jax.random.randint(base_key, (IMAGES,), 1, WROWS + 1)
    chosen_slot = jax.random.randint(choose_key, (IMAGES // IMG_DEV,), 0, IMG_DEV)
    slot_index = jnp.arange(IMAGES) % IMG_DEV
    chosen = slot_index == jnp.repeat(chosen_slot, IMG_DEV)
    return jnp.where(chosen, WROWS, base_rows).astype(jnp.int32)


def steps_of(rng, extent, pieces, low, high):
    def one(axis_at, blocks):
        steps = jax.random.uniform(jax.random.fold_in(jax.random.fold_in(rng, 6), axis_at), (blocks,), jnp.float32, low / len(pieces), high / len(pieces))
        return jnp.repeat(jnp.exp(steps), extent[axis_at] // blocks).reshape((-1,) + (1,) * (len(extent) - axis_at - 1))

    level = one(*pieces[0])
    for cut in pieces[1:]:
        level = level * one(*cut)
    return level


def gaussian(own_key, shape, scale, bound, pieces=(), kind=jnp.bfloat16):
    factor_of = steps_of(own_key, shape, pieces, -0.22, 0.18) if pieces else 1.0
    values = jax.random.normal(own_key, shape, jnp.float32) * scale * factor_of
    return jnp.minimum(jnp.maximum(values, -bound), bound).astype(kind)


def setup_inputs(seed: int = 0) -> dict:
    key_list = jax.random.split(jax.random.key(seed), 17)
    tokens = gaussian(key_list[0], (IMAGES, HEIGHT, WIDTH, C), 1.0, 6.0, ((0, 8), (1, 4)))
    heights = draw_heights(jax.random.fold_in(key_list[16], 71), 0)
    conv_weight = gaussian(key_list[2], (4, 3, 3, C), 9 ** -0.5, 2.0)
    conv_bias = gaussian(key_list[3], (4, C), 0.3, 1.5)
    norm_gain = jnp.clip(1.0 + 0.1 * jax.random.normal(key_list[4], (4, C), jnp.float32), 0.5, 1.5).astype(jnp.bfloat16)
    norm_shift = gaussian(key_list[5], (4, C), 0.2, 1.0)
    mix_weight = gaussian(key_list[6], (2, C, 3 * C), C ** -0.5, 0.3125)
    window_bias = gaussian(key_list[7], (2 * C,), 0.3, 1.5)
    channel_bias = gaussian(key_list[8], (3 * C,), 0.1, 0.5)
    out_weight = gaussian(key_list[9], (2, C, C), (C // 8) ** -0.5, 0.875)
    out_bias = gaussian(key_list[10], (2, C), 0.3, 1.5)
    up_weight = gaussian(key_list[11], (2, C, FF), C ** -0.5, 0.3125)
    up_bias = gaussian(key_list[12], (2, FF), 0.3, 1.5)
    down_weight = gaussian(key_list[13], (2, FF, C), FF ** -0.5, 0.15625)
    down_bias = gaussian(key_list[14], (2, C), 0.3, 1.5)
    cotangent = gaussian(key_list[15], (IMAGES, HEIGHT, WIDTH, C), 1.0, 6.0, ((0, 8), (1, 4)))
    return {"tokens": tokens, "heights": heights, "conv_weight": conv_weight, "conv_bias": conv_bias, "norm_gain": norm_gain, "norm_shift": norm_shift, "mix_weight": mix_weight, "window_bias": window_bias, "channel_bias": channel_bias, "out_weight": out_weight, "out_bias": out_bias, "up_weight": up_weight, "up_bias": up_bias, "down_weight": down_weight, "down_bias": down_bias, "cotangent": cotangent}


@jax.custom_vjp
def low(v):
    return lax.optimization_barrier(v.astype(jnp.bfloat16)).astype(jnp.float32)

@jax.custom_vjp
def low_back(v):
    return v

def low_keep(v):
    return (low(v), None)

def low_pass(kept, grad):
    return (grad,)

def back_keep(v):
    return (v, None)

def back_low(kept, grad):
    return (low(grad),)
low.defvjp(low_keep, low_pass)
low_back.defvjp(back_keep, back_low)
HIGH = lax.Precision.HIGHEST
EPS = 1e-05

def dense(left, right):
    return jnp.dot(left, right, preferred_element_type=jnp.float32, precision=HIGH)

def layer_norm(value, gain, shift):
    centre = value - lax.optimization_barrier(jnp.mean(value, axis=-1, keepdims=True))
    spread = lax.optimization_barrier(jnp.mean(centre * centre, axis=-1, keepdims=True))
    return centre * lax.rsqrt(spread + EPS) * gain + shift

def depthwise(field, weight):
    height, width = (field.shape[0], field.shape[1])
    padded = jnp.pad(field, ((1, 1), (1, 1), (0, 0)))
    total = jnp.zeros_like(field)
    for row_off in range(3):
        for col_off in range(3):
            total = total + padded[row_off:row_off + height, col_off:col_off + width] * weight[row_off, col_off]
    return total

def position_step(value, weight, bias, region):
    return region * (value + low_back(depthwise(low(value), weight)) + bias)

def to_windows(flat, height, width):
    blocks = flat.reshape(height // 7, 7, width // 7, 7, HEADS, HEAD_DIM)
    return blocks.transpose(0, 2, 4, 1, 3, 5).reshape(-1, HEADS, 49, HEAD_DIM)

def from_windows(windows, height, width):
    blocks = windows.reshape(height // 7, width // 7, HEADS, 7, 7, HEAD_DIM)
    return blocks.transpose(0, 3, 1, 4, 2, 5).reshape(height * width, HEADS * HEAD_DIM)

def window_branch(normed, weight, bias_full, height, width):
    chans = normed.shape[-1]
    mixed = low(low_back(dense(normed, weight)) + bias_full)
    query = to_windows(mixed[:, :chans], height, width)
    key = to_windows(mixed[:, chans:2 * chans], height, width)
    value = to_windows(mixed[:, 2 * chans:], height, width)
    scores = low_back(jnp.einsum('nhqd,nhkd->nhqk', query, key, precision=HIGH) * HEAD_DIM ** (-0.5))
    probs = low(jax.nn.softmax(scores, axis=-1))
    attended = low(low_back(jnp.einsum('nhqk,nhkd->nhqd', probs, value, precision=HIGH)))
    return from_windows(attended, height, width)

def channel_branch(normed, weight, bias, keep_flat, scale):
    chans = normed.shape[-1]
    mixed = low(low_back(dense(normed, weight)) + bias).reshape(-1, 3, HEADS, HEAD_DIM)
    query = mixed[:, 0]
    key = mixed[:, 1] * keep_flat
    value = mixed[:, 2]
    gram = jnp.einsum('thd,the->hde', key, value, precision=HIGH)
    weights = low(jax.nn.softmax(low_back(gram * scale), axis=-1))
    attended = low(low_back(jnp.einsum('hde,the->thd', weights, query, precision=HIGH)))
    return attended.reshape(-1, chans)

def feed_forward(normed, up_w, up_b, down_w, down_b):
    hidden = low(jax.nn.gelu(low_back(dense(normed, up_w)) + up_b, approximate=False))
    return low_back(dense(hidden, down_w)) + down_b

def block(image, params, region, scale):
    conv_w, conv_b, gain, shift, mix_w, win_b, chan_b, out_w, out_b, up_w, up_b, down_w, down_b = params
    height, width, chans = image.shape
    keep_flat = jnp.broadcast_to(region, (height, width, 1)).reshape(-1, 1, 1)
    bias_full = jnp.concatenate([win_b[:chans], jnp.zeros((chans,), jnp.float32), win_b[chans:]])
    state = region * image
    state = position_step(state, conv_w[0], conv_b[0], region)
    normed = low(layer_norm(state, gain[0], shift[0])).reshape(-1, chans)
    branch = window_branch(normed, mix_w[0], bias_full, height, width)
    state = region * (state + (low_back(dense(branch, out_w[0])) + out_b[0]).reshape(state.shape))
    state = position_step(state, conv_w[1], conv_b[1], region)
    normed = low(layer_norm(state, gain[1], shift[1])).reshape(-1, chans)
    state = region * (state + feed_forward(normed, up_w[0], up_b[0], down_w[0], down_b[0]).reshape(state.shape))
    state = position_step(state, conv_w[2], conv_b[2], region)
    normed = low(layer_norm(state, gain[2], shift[2])).reshape(-1, chans)
    branch = channel_branch(normed, mix_w[1], chan_b, keep_flat, scale)
    state = region * (state + (low_back(dense(branch, out_w[1])) + out_b[1]).reshape(state.shape))
    state = position_step(state, conv_w[3], conv_b[3], region)
    normed = low(layer_norm(state, gain[3], shift[3])).reshape(-1, chans)
    state = region * (state + feed_forward(normed, up_w[1], up_b[1], down_w[1], down_b[1]).reshape(state.shape))
    return state

def reference(tokens, heights, conv_weight, conv_bias, norm_gain, norm_shift, mix_weight, window_bias, channel_bias, out_weight, out_bias, up_weight, up_bias, down_weight, down_bias, cotangent):
    params = tuple((item.astype(jnp.float32) for item in (conv_weight, conv_bias, norm_gain, norm_shift, mix_weight, window_bias, channel_bias, out_weight, out_bias, up_weight, up_bias, down_weight, down_bias)))
    row_index = jnp.arange(HEIGHT, dtype=jnp.int32)

    def one_image(totals, item):
        image, image_cot, level = item
        region = (row_index < level * 7).astype(jnp.float32)[:, None, None]
        scale = lax.rsqrt((level * 7 * WIDTH).astype(jnp.float32))

        def forward(image_value, weights):
            return block(image_value, weights, region, scale)
        output, pull = jax.vjp(forward, image.astype(jnp.float32), params)
        image_grad, weight_grads = pull(image_cot.astype(jnp.float32))
        totals = jax.tree.map(jnp.add, totals, weight_grads)
        return (totals, (output.astype(jnp.bfloat16), image_grad))
    zeros = jax.tree.map(jnp.zeros_like, params)
    totals, outputs = lax.scan(one_image, zeros, (tokens, cotangent, heights))
    result, tokens_grad = outputs
    return (result, tokens_grad, totals[0], totals[1], totals[2], totals[3][:3], totals[3][3], totals[4], totals[5], totals[6], totals[7], totals[8], totals[9], totals[10], totals[11], totals[12])
```

```python
import functools

import jax
import jax.numpy as jnp
from jax import lax
from jax.experimental import pallas as pl
from jax.experimental.pallas import tpu as pltpu
from jax.sharding import Mesh
from jax.sharding import PartitionSpec as P

HEADS = 12
HEAD_DIM = 32
EPS = 1e-05
WIN = 7
SLOT = 64
LANES = 128
F32 = jnp.float32
BF16 = jnp.bfloat16
SCALE = HEAD_DIM ** (-0.5)
LOG2E = 1.4426950408889634
ROOT_HALF = 0.7071067811865476
VMEM_LIMIT = 58 * 1024 * 1024
SMALL_ROWS = 256


def dot(left, right):
    return jnp.dot(left, right, preferred_element_type=F32)


def dot_nt(left, right):
    return lax.dot_general(left, right, (((1,), (1,)), ((), ())), preferred_element_type=F32)


def dot_tn(left, right):
    return lax.dot_general(left, right, (((0,), (0,)), ((), ())), preferred_element_type=F32)


def low(value):
    return value.astype(BF16).astype(F32)


def fold(value):
    rows, cols = value.shape
    return jnp.sum(value.reshape(rows // 8, 8, cols), axis=0)


def loop(count, step, body):
    for at in range(0, count, step):
        body(at)


def lane_tiles(chans):
    return [slice(t, t + LANES) for t in range(0, chans, LANES)]


def gelu_parts(value):
    size = jnp.abs(value)
    t = 1.0 / (1.0 + (0.3275911 * ROOT_HALF) * size)
    poly = t * (
        0.127414796
        + t * (-0.142248368 + t * (0.7107068705 + t * (-0.7265760135 + t * 0.5307027145)))
    )
    bell = jnp.exp2(value * value * (-0.5 * LOG2E))
    tail = poly * bell
    cdf = jnp.where(value >= 0.0, 1.0 - tail, tail)
    return value * cdf, cdf + value * bell * 0.3989422804014327


def norm_of(value, gain, shift):
    centre = value - jnp.mean(value, axis=-1, keepdims=True)
    spread = jnp.mean(centre * centre, axis=-1, keepdims=True)
    return centre * lax.rsqrt(spread + EPS) * gain + shift


def norm_back(value, gain, normed_grad):
    centre = value - jnp.mean(value, axis=-1, keepdims=True)
    inv = lax.rsqrt(jnp.mean(centre * centre, axis=-1, keepdims=True) + EPS)
    unit = centre * inv
    unit_grad = normed_grad * gain
    first = jnp.mean(unit_grad, axis=-1, keepdims=True)
    second = jnp.mean(unit_grad * unit, axis=-1, keepdims=True)
    return inv * (unit_grad - first - unit * second), normed_grad * unit


def fill_source(src, main, prev, after, halo, step, steps, width):
    rows = main.shape[0]
    src[pl.ds(0, width), :] = jnp.where(step == 0, halo[0:width, :], low(prev[...]))
    src[pl.ds(rows + width, width), :] = jnp.where(
        step == steps - 1, halo[width : 2 * width, :], low(after[...])
    )

    def body(at):
        src[pl.ds(at + width, 2 * width), :] = low(main[pl.ds(at, 2 * width), :])

    loop(rows // (2 * width) * 2 * width, 2 * width, body)
    if rows % (2 * width):
        at = rows - width
        src[pl.ds(at + width, width), :] = low(main[pl.ds(at, width), :])


def conv_tile(src, vec, at, tile, width, lanes, flipped):
    rows = [src[pl.ds(at + width * d, tile), lanes] for d in range(3)]
    sums = []
    for col in range(3):
        total = None
        for row in range(3):
            k = (2 - row) * 3 + (2 - col) if flipped else row * 3 + col
            term = rows[row] * vec[k : k + 1, lanes]
            total = term if total is None else total + term
        sums.append(total)
    return sums[1] + pltpu.roll(sums[0], 1, 0) + pltpu.roll(sums[2], tile - 1, 0), rows


def conv_weight_tile(acc, rows, field, tile, lanes):
    shifted = [pltpu.roll(field, 1, 0), field, pltpu.roll(field, tile - 1, 0)]
    for row in range(3):
        for col in range(3):
            k = row * 3 + col
            acc[8 * k : 8 * k + 8, lanes] += fold(shifted[col] * rows[2 - row])


def block_heads(part):
    lane = lax.broadcasted_iota(jnp.int32, part.shape, 1)
    zero = jnp.zeros_like(part)
    return jnp.concatenate(
        [jnp.where(lane // HEAD_DIM == h, part, zero) for h in range(LANES // HEAD_DIM)], axis=0
    )


def window_forward_kernel(
    tok, prev, after, halo, mask, vec, mix, mix_b, out_w, gather, x1, nw, mw, ow, x2, src, keep, probs
):
    step, steps = pl.program_id(0), pl.num_programs(0)
    rows, width, chans = tok.shape
    src[pl.ds(0, width), :] = jnp.where(step == 0, halo[0:width, :], prev[0].astype(F32))
    src[pl.ds((rows + 1) * width, width), :] = jnp.where(
        step == steps - 1, halo[width : 2 * width, :], after[0].astype(F32)
    )
    for i in range(rows):
        src[pl.ds((i + 1) * width, width), :] = tok[i].astype(F32)

    def conv_body(at):
        region = mask[pl.ds(at, width), :]
        for lanes in lane_tiles(chans):
            got, near = conv_tile(src, vec, at, width, width, lanes, False)
            x1[pl.ds(at, width), lanes] = region * (near[1] + got + vec[9:10, lanes])

    loop(rows * width, width, conv_body)

    normed = norm_of(x1[...], vec[10:11, :], vec[11:12, :]).astype(BF16)
    normed = dot(gather[...], normed).astype(BF16)
    nw[...] = normed
    mw[...] = (dot(normed, mix[...]) + mix_b[...]).astype(BF16)
    windows = nw.shape[0] // SLOT
    lane = lax.broadcasted_iota(jnp.int32, (SLOT, LANES), 1)
    left = lane < SLOT
    real = lane % SLOT < WIN * WIN
    ones = (
        lax.broadcasted_iota(jnp.int32, (4 * SLOT, LANES), 0) // SLOT
        == lax.broadcasted_iota(jnp.int32, (4 * SLOT, LANES), 1) // HEAD_DIM
    ).astype(BF16)
    floor = -1e30

    places = [(at, lanes) for at in range(0, windows * SLOT, SLOT) for lanes in lane_tiles(chans)]
    for n, (at, lanes) in enumerate(places):
        query = mw[at : at + SLOT, lanes]
        key = mw[at : at + SLOT, chans + lanes.start : chans + lanes.stop]
        scores = dot_nt(query, block_heads(key))
        for half in range(2):
            part = jnp.where(real, scores[:, half * LANES : (half + 1) * LANES], floor)
            top_l = jnp.max(jnp.where(left, part, floor), axis=1, keepdims=True)
            top_r = jnp.max(jnp.where(left, floor, part), axis=1, keepdims=True)
            top = jnp.where(left, top_l, top_r)
            raised = jnp.exp2((part - top) * (SCALE * LOG2E)).astype(BF16)
            probs[n * SLOT : (n + 1) * SLOT, half * LANES : (half + 1) * LANES] = raised
    for n, (at, lanes) in enumerate(places):
        value = mw[at : at + SLOT, 2 * chans + lanes.start : 2 * chans + lanes.stop]
        both = dot(
            probs[n * SLOT : (n + 1) * SLOT, :], jnp.concatenate([block_heads(value), ones], axis=1)
        )
        ow[at : at + SLOT, lanes] = (both[:, :LANES] / both[:, LANES:]).astype(BF16)
    merged = dot_tn(gather[...], ow[...]).astype(BF16)
    keep[...] = dot(merged, out_w[...])

    def out_body(at):
        region = mask[pl.ds(at, width), :]
        for lanes in lane_tiles(chans):
            x2[pl.ds(at, width), lanes] = region * (
                x1[pl.ds(at, width), lanes] + keep[pl.ds(at, width), lanes] + vec[12:13, lanes]
            )

    loop(rows * width, width, out_body)


def conv_forward(main, prev, after, halo, mask, vec, out, src, width):
    step, steps = pl.program_id(0), pl.num_programs(0)
    rows, chans = main.shape
    fill_source(src, main, prev, after, halo, step, steps, width)
    tile = 2 * width

    def body(at):
        region = mask[pl.ds(at, tile), :]
        for lanes in lane_tiles(chans):
            got, _ = conv_tile(src, vec, at, tile, width, lanes, False)
            out[pl.ds(at, tile), lanes] = region * (
                main[pl.ds(at, tile), lanes] + got + vec[9:10, lanes]
            )

    loop(rows, tile, body)


def norm_forward(value, vec, out):
    out[...] = norm_of(value[...], vec[10:11, :], vec[11:12, :]).astype(BF16)


def mlp_body(normed, up_w, up_b, down_w, hidden, slope, keep):
    rows = normed.shape[0]
    for at in range(0, up_w.shape[1], 256):
        cols = slice(at, at + 256)
        pre = dot(normed[...], up_w[:, cols]) + up_b[:, cols]
        for row in range(0, rows, 144):
            act, der = gelu_parts(pre[row : row + 144])
            hidden[row : row + 144, cols] = act.astype(BF16)
            slope[row : row + 144, cols] = der.astype(BF16)
        part = dot(hidden[:, cols], down_w[cols, :])
        if at == 0:
            keep[...] = part
        else:
            keep[...] += part


def add_residual(state, branch, mask, vec, out):
    chans = state.shape[1]

    def body(at):
        region = mask[pl.ds(at, 144), :]
        for lanes in lane_tiles(chans):
            out[pl.ds(at, 144), lanes] = (
                region
                * (state[pl.ds(at, 144), lanes] + branch[pl.ds(at, 144), lanes] + vec[12:13, lanes])
            ).astype(out.dtype)

    loop(state.shape[0], 144, body)


def mlp_forward_kernel(
    main, prev, after, halo, mask, vec, up_w, up_b, down_w, x3, x4, normed, hidden, slope, src, keep
):
    width = prev.shape[0]
    conv_forward(main, prev, after, halo, mask, vec, x3, src, width)
    norm_forward(x3, vec, normed)
    mlp_body(normed, up_w, up_b, down_w, hidden, slope, keep)
    add_residual(x3, keep, mask, vec, x4)


def norm_backward(state, normed_grad, grad, vec, small, out, gain_row):
    part = normed_grad[...]
    back, scaled = norm_back(state[...], vec[10:11, :], part)
    out[...] = grad[...].astype(F32) + back
    small[gain_row : gain_row + 8, :] += fold(scaled)
    small[gain_row + 8 : gain_row + 16, :] += fold(part)


def mlp_down_back(rounded, normed, hidden, slope, pre_grad, up_w, down_w, up_g, up_bg, down_g):
    rows = rounded.shape[0]
    for at in range(0, up_w.shape[1], 256):
        cols = slice(at, at + 256)
        hidden_grad = dot_nt(rounded[...], down_w[cols, :])
        total = None
        for row in range(0, rows, 144):
            part = hidden_grad[row : row + 144] * slope[row : row + 144, cols].astype(F32)
            pre_grad[row : row + 144, cols] = part.astype(BF16)
            total = fold(part) if total is None else total + fold(part)
        up_bg[:, cols] += total
        up_g[:, cols] += dot_tn(normed[...], pre_grad[:, cols])
        down_g[cols, :] += dot_tn(hidden[:, cols], rounded[...])


def mlp_both(normed, cot, up_w, up_b, down_w, hidden, pre_grad, up_g, up_bg, down_g):
    rows = normed.shape[0]
    for at in range(0, up_w.shape[1], 256):
        cols = slice(at, at + 256)
        pre = dot(normed[...], up_w[:, cols]) + up_b[:, cols]
        hidden_grad = dot_nt(cot[...], down_w[cols, :])
        total = None
        for row in range(0, rows, 144):
            act, der = gelu_parts(pre[row : row + 144])
            hidden[row : row + 144, cols] = act.astype(BF16)
            part = hidden_grad[row : row + 144] * der
            pre_grad[row : row + 144, cols] = part.astype(BF16)
            total = fold(part) if total is None else total + fold(part)
        up_bg[:, cols] += total
        up_g[:, cols] += dot_tn(normed[...], pre_grad[:, cols])
        down_g[cols, :] += dot_tn(hidden[:, cols], cot[...])


def column_blocks(source, chans):
    return [source.at[:, col : col + chans] for col in range(0, source.shape[1], chans)]


def spread(core, kept, sent, blocks):
    half = kept.shape[0]
    for flag in range(2):

        @pl.when(core[0] == flag)
        def _():
            at = 0
            for block in blocks:
                rows = block.shape[0]
                cuts = [0, rows] if not at < half < at + rows else [0, half - at, rows]
                for low_cut, high_cut in zip(cuts, cuts[1:]):
                    start = at + low_cut
                    target = kept if (start >= half) == (flag == 1) else sent
                    start = start % half
                    target[start : start + high_cut - low_cut, :] = block[
                        low_cut:high_cut, :
                    ].astype(BF16)
                at += rows


def last_step():
    return pl.program_id(0) == pl.num_programs(0) - 1


def zero_first(*refs):
    @pl.when(pl.program_id(0) == 0)
    def _():
        for ref in refs:
            ref[...] = jnp.zeros_like(ref)


def last_mlp_kernel(
    main, prev, after, halo, mask, vec, up_w, up_b, down_w, cot,
    result, grad, packed, up_bg, small,
    src, x7, keep, back, normed, hidden, pre_grad, up_g, down_g,
):
    width = prev.shape[0]
    zero_first(up_g, up_bg, down_g, small)
    conv_forward(main, prev, after, halo, mask, vec, x7, src, width)
    norm_forward(x7, vec, normed)
    mlp_both(normed, cot, up_w, up_b, down_w, hidden, pre_grad, up_g, up_bg, down_g)
    keep[...] = dot(hidden[...], down_w[...])
    back[...] = dot_nt(pre_grad[...], up_w[...])
    add_residual(x7, keep, mask, vec, result)
    small[0:8, :] += fold(cot[...].astype(F32))
    norm_backward(x7, back, cot, vec, small, grad, 8)

    @pl.when(last_step())
    def _():
        at = 0
        for block in column_blocks(up_g, packed.shape[1]) + [down_g]:
            packed[at : at + block.shape[0], :] = block[...].astype(BF16)
            at += block.shape[0]


def conv_backward(main, prev, after, halo, mask, vec, field, out, conv_g, small, src, width):
    step, steps = pl.program_id(0), pl.num_programs(0)
    rows, chans = main.shape
    fill_source(src, main, prev, after, halo, step, steps, width)
    tile = 72

    def body(at):
        region = mask[pl.ds(at, tile), :]
        for lanes in lane_tiles(chans):
            got, near = conv_tile(src, vec, at, tile, width, lanes, True)
            grad = main[pl.ds(at, tile), lanes]
            out[pl.ds(at, tile), lanes] = (region * (grad + got)).astype(out.dtype)
            conv_weight_tile(conv_g, near, low(field[pl.ds(at, tile), lanes]), tile, lanes)
            small[0:8, lanes] += fold(grad)

    loop(rows, tile, body)


def fold_rows(source, small, row):
    def body(at):
        small[row : row + 8, :] += fold(source[pl.ds(at, 72), :])

    loop(source.shape[0], 72, body)


def channel_mix_kernel(
    main, prev, after, halo, mask, vec, mix, mix_b, x5, normed, mixed, gram, src
):
    width = prev.shape[0]
    chans = main.shape[1]
    zero_first(gram)
    conv_forward(main, prev, after, halo, mask, vec, x5, src, width)
    norm_forward(x5, vec, normed)
    rows = main.shape[0]
    for part in range(3):
        cols = slice(part * chans, (part + 1) * chans)
        got = dot(normed[...], mix[:, cols]) + mix_b[:, cols]
        if part == 1:
            got = got * jnp.concatenate([mask[...]] * (chans // LANES), axis=1)
        mixed[:, cols] = got.astype(BF16)
    for t, lanes in enumerate(lane_tiles(chans)):
        gram[t] += dot_tn(
            mixed[:, chans + lanes.start : chans + lanes.stop],
            mixed[:, 2 * chans + lanes.start : 2 * chans + lanes.stop],
        )


def same_head():
    row = lax.broadcasted_iota(jnp.int32, (LANES, LANES), 0)
    col = lax.broadcasted_iota(jnp.int32, (LANES, LANES), 1)
    return row // HEAD_DIM == col // HEAD_DIM


def channel_weights(gram, scale):
    own = same_head()
    logits = jnp.where(own, gram * scale, -1e30)
    top = jnp.max(logits, axis=1, keepdims=True)
    raised = jnp.where(own, jnp.exp(logits - top), 0.0)
    return raised / jnp.sum(raised, axis=1, keepdims=True)


def channel_out_kernel(mixed, gram, scale, x5, mask, vec, out_w, o2, x6, keep):
    chans = x5.shape[1]
    for t, lanes in enumerate(lane_tiles(chans)):
        weights = channel_weights(gram[t], scale[0:1, :]).astype(BF16)
        o2[:, lanes] = dot_nt(mixed[:, lanes], weights).astype(BF16)
    keep[...] = dot(o2[...], out_w[...])
    add_residual(x5, keep, mask, vec, x6)


def channel_grad_kernel(
    main, prev, after, halo, mask, vec, x6, mixed, o2, out_w,
    grad, attended_grad, weights_g, packed, conv_g, small, src, rounded, out_g,
):
    width = prev.shape[0]
    chans = main.shape[1]
    zero_first(weights_g, out_g, conv_g, small)
    conv_backward(main, prev, after, halo, mask, vec, x6, grad, conv_g, small, src, width)
    rounded[...] = grad[...].astype(BF16)
    fold_rows(grad, small, 8)
    out_g[...] += dot_tn(o2[...], rounded[...])
    attended_grad[...] = dot_nt(rounded[...], out_w[...]).astype(BF16)
    for t, lanes in enumerate(lane_tiles(chans)):
        weights_g[t] += dot_tn(attended_grad[:, lanes], mixed[:, lanes])

    @pl.when(last_step())
    def _():
        packed[...] = out_g[...].astype(BF16)


def channel_back_kernel(
    attended_grad, mixed, gram, weights_g, scale, normed, x5, g6, mask, vec, mix,
    grad, packed, mix_bg, small, mixed_grad, keep, mix_g,
):
    chans = x5.shape[1]
    zero_first(mix_g, mix_bg, small)
    own = same_head()
    wide = mask[...]
    for t, lanes in enumerate(lane_tiles(chans)):
        weights = channel_weights(gram[t], scale[0:1, :])
        back = jnp.where(own, weights_g[t], 0.0)
        logit = weights * (back - jnp.sum(back * weights, axis=1, keepdims=True))
        logit = logit.astype(BF16)
        key = slice(chans + lanes.start, chans + lanes.stop)
        val = slice(2 * chans + lanes.start, 2 * chans + lanes.stop)
        query_grad = dot(attended_grad[:, lanes], weights.astype(BF16))
        key_grad = dot_nt(mixed[:, val], logit) * scale[0:1, :] * wide
        value_grad = dot(mixed[:, key], logit) * scale[0:1, :]
        for cols, part in ((lanes, query_grad), (key, key_grad), (val, value_grad)):
            mix_bg[:, cols] += fold(part)
            mixed_grad[:, cols] = part.astype(BF16)
    for part in range(3):
        cols = slice(part * chans, (part + 1) * chans)
        mix_g[part * chans : (part + 1) * chans, :] += dot_tn(normed[...], mixed_grad[:, cols])
    keep[...] = dot_nt(mixed_grad[...], mix[...])
    norm_backward(x5, keep, g6, vec, small, grad, 0)

    @pl.when(last_step())
    def _():
        packed[...] = mix_g[...].astype(BF16)


def mlp_back_kernel(
    main, prev, after, halo, mask, vec_conv, vec, x4, x3, normed, hidden, slope, up_w, down_w, mlp1, mix1, out1, core,
    grad, kept, sent, up_bg, conv_g, small,
    src, g4, rounded, keep, pre_grad, up_g, down_g,
):
    width = prev.shape[0]
    zero_first(up_g, up_bg, down_g, conv_g, small)
    conv_backward(main, prev, after, halo, mask, vec_conv, x4, g4, conv_g, small, src, width)
    rounded[...] = g4[...].astype(BF16)
    fold_rows(g4, small, 8)
    mlp_down_back(rounded, normed, hidden, slope, pre_grad, up_w, down_w, up_g, up_bg, down_g)
    keep[...] = dot_nt(pre_grad[...], up_w[...])
    norm_backward(x3, keep, g4, vec, small, grad, 16)

    @pl.when(last_step())
    def _():
        spread(core, kept, sent, [mlp1, mix1, out1] + column_blocks(up_g, kept.shape[1]) + [down_g])


def window_back_kernel(
    main, prev, after, halo, mask, vec_conv, vec, x2, x1, nw, mw, ow, mix, out_w, gather,
    grad, packed, mix_bg, conv_g, small,
    src, mix_g, out_g, g2, gw, dow, dmw, keep, probs, slopes,
):
    width = prev.shape[0]
    chans = main.shape[1]
    zero_first(mix_g, mix_bg, out_g, conv_g, small)
    conv_backward(main, prev, after, halo, mask, vec_conv, x2, g2, conv_g, small, src, width)
    fold_rows(g2, small, 8)
    gw[...] = dot(gather[...], g2[...].astype(BF16)).astype(BF16)
    out_g[...] += dot_tn(ow[...], gw[...])
    dow[...] = dot_nt(gw[...], out_w[...]).astype(BF16)
    windows = nw.shape[0] // SLOT
    real = lax.broadcasted_iota(jnp.int32, (SLOT, 4 * SLOT), 0) < WIN * WIN
    head = lax.broadcasted_iota(jnp.int32, (SLOT, LANES), 1) // HEAD_DIM

    places = [(at, lanes) for at in range(0, windows * SLOT, SLOT) for lanes in lane_tiles(chans)]
    for n, (at, lanes) in enumerate(places):
        rows = slice(at, at + SLOT)
        query = mw[rows, lanes]
        key = mw[rows, chans + lanes.start : chans + lanes.stop]
        value = mw[rows, 2 * chans + lanes.start : 2 * chans + lanes.stop]
        scores = jnp.where(real, dot_nt(key, block_heads(query)), -1e30)
        top = jnp.max(scores, axis=0, keepdims=True)
        raised = jnp.exp2((scores - top) * (SCALE * LOG2E))
        share = raised * (1.0 / jnp.sum(raised, axis=0, keepdims=True))
        share_grad = dot_nt(value, block_heads(dow[rows, lanes]))
        inner = jnp.sum(share_grad * share, axis=0, keepdims=True)
        probs[n * SLOT : (n + 1) * SLOT, :] = share.astype(BF16)
        slopes[n * SLOT : (n + 1) * SLOT, :] = (share * (share_grad - inner)).astype(BF16)
    for n, (at, lanes) in enumerate(places):
        rows = slice(at, at + SLOT)
        key_cols = slice(chans + lanes.start, chans + lanes.stop)
        value_cols = slice(2 * chans + lanes.start, 2 * chans + lanes.stop)
        share, slope = probs[n * SLOT : (n + 1) * SLOT, :], slopes[n * SLOT : (n + 1) * SLOT, :]
        value_grad = dot(share, block_heads(dow[rows, lanes]))
        key_grad = dot(slope, block_heads(mw[rows, lanes])) * SCALE
        full = dot_tn(slope, mw[rows, key_cols])
        query_grad = jnp.zeros((SLOT, LANES), F32)
        for h in range(LANES // HEAD_DIM):
            query_grad = jnp.where(head == h, full[h * SLOT : (h + 1) * SLOT], query_grad)
        query_grad = query_grad * SCALE
        for cols, part in ((lanes, query_grad), (key_cols, key_grad), (value_cols, value_grad)):
            dmw[rows, cols] = part.astype(BF16)
            mix_bg[:, cols] += fold(part)
    for part in range(3):
        cols = slice(part * chans, (part + 1) * chans)
        mix_g[part * chans : (part + 1) * chans, :] += dot_tn(nw[...], dmw[:, cols])
    normed_grad = dot_nt(dmw[...], mix[...]).astype(BF16)
    keep[...] = dot_tn(gather[...], normed_grad)
    norm_backward(x1, keep, g2, vec, small, grad, 16)

    @pl.when(last_step())
    def _():
        packed[: 3 * chans, :] = mix_g[...].astype(BF16)
        packed[3 * chans :, :] = out_g[...].astype(BF16)


def token_grad_kernel(main, prev, after, halo, mask, vec, field, out, conv_g, small, src):
    width = prev.shape[0]
    zero_first(conv_g, small)
    conv_backward(main, prev, after, halo, mask, vec, field, out, conv_g, small, src, width)


def call(kernel, steps, ins, outs, scratch, cost, after=()):
    count = len(ins)

    def body(*refs):
        kernel(*refs[:count], *refs[count + len(after) :])

    def spec(block, index):
        if block is None:
            return pl.BlockSpec(memory_space=pltpu.SMEM)
        fixed = tuple(0 for _ in block)
        if index is None:
            return pl.BlockSpec(block, lambda i: fixed, pipeline_mode=pl.Buffered(1))
        return pl.BlockSpec(block, index)

    def out_spec(block, index):
        fixed = tuple(0 for _ in block)
        return pl.BlockSpec(block, (lambda i: fixed) if index is None else index)

    return pl.pallas_call(
        body,
        grid=(steps,),
        in_specs=[spec(block, index) for _, block, index in ins]
        + [pl.BlockSpec(memory_space=pl.ANY) for _ in after],
        out_specs=[out_spec(block, index) for _, _, block, index in outs],
        out_shape=[jax.ShapeDtypeStruct(shape, dtype) for shape, dtype, _, _ in outs],
        scratch_shapes=[pltpu.VMEM(shape, dtype) for shape, dtype in scratch],
        compiler_params=pltpu.CompilerParams(vmem_limit_bytes=VMEM_LIMIT),
        cost_estimate=pl.CostEstimate(flops=1, bytes_accessed=1, transcendentals=0),
    )(*[array for array, _, _ in ins], *after)


def gather_matrix(cols, width):
    windows = cols // WIN
    slot = jnp.arange(windows * SLOT, dtype=jnp.int32)[:, None]
    window, inside = slot // SLOT, slot % SLOT
    source = inside // WIN * width + window * WIN + inside % WIN
    patch = jnp.arange(WIN * width, dtype=jnp.int32)[None, :]
    return ((source == patch) & (inside < WIN * WIN)).astype(BF16)


def image_block(x0, cot, tok_halo, mask, scale, halo_of, across, weights, cols, core, send_result, share_cores, share_planes):
    conv_w, conv_b, gain, shift, mix_w, win_b, chan_b, out_w, out_b, up_w, up_b, down_w, down_b = weights
    height, width, chans = x0.shape
    tokens = height * width
    ff = up_w.shape[2]
    vec_of = [
        jnp.concatenate(
            [
                conv_w[k].reshape(9, chans),
                conv_b[k : k + 1],
                gain[k : k + 1],
                shift[k : k + 1],
                (out_b if k % 2 == 0 else down_b)[k // 2 : k // 2 + 1],
                jnp.zeros((3, chans), BF16),
            ],
            axis=0,
        ).astype(F32)
        for k in range(4)
    ]
    bias0 = jnp.concatenate([win_b[:chans], jnp.zeros((chans,), BF16), win_b[chans:]])
    bias0 = bias0.astype(F32)[None]
    bias1 = chan_b.astype(F32)[None]
    up_bias = up_b.astype(F32)
    gather = gather_matrix(cols, width)
    wrows = cols // WIN * SLOT
    unit = WIN * width
    units = height // WIN
    chunk = 2 * unit if units % 2 == 0 else unit
    chunks = tokens // chunk

    def near(array, rows):
        per = rows // width
        return [
            (array, (rows, chans), lambda i: (i, 0)),
            (array, (width, chans), lambda i: (jnp.maximum(i * per - 1, 0), 0)),
            (array, (width, chans), lambda i: (jnp.minimum(i * per + per, height - 1), 0)),
            (halo_of(array), (2 * width, chans), None),
        ]

    def rows_in(array, rows):
        return (array, (rows, array.shape[1]), lambda i: (i, 0))

    def whole(array):
        return (array, array.shape, None)

    def rows_out(cols_, dtype, rows=chunk, total=tokens):
        return ((total, cols_), dtype, (rows, cols_), lambda i: (i, 0))

    def sums(*shape, dtype=F32):
        return (shape, dtype, shape, None)

    def vec(k):
        return whole(vec_of[k])

    scalar = (core, None, None)

    dense = 2 * tokens * chans
    x1, nw, mw, ow, x2 = call(
        window_forward_kernel,
        units,
        [
            (x0, (WIN, width, chans), lambda i: (i, 0, 0)),
            (x0, (1, width, chans), lambda i: (jnp.maximum(i * WIN - 1, 0), 0, 0)),
            (x0, (1, width, chans), lambda i: (jnp.minimum(i * WIN + WIN, height - 1), 0, 0)),
            whole(tok_halo),
            rows_in(mask, unit),
            vec(0),
            whole(mix_w[0]),
            whole(bias0),
            whole(out_w[0]),
            whole(gather),
        ],
        [
            rows_out(chans, F32, unit),
            rows_out(chans, BF16, wrows, units * wrows),
            rows_out(3 * chans, BF16, wrows, units * wrows),
            rows_out(chans, BF16, wrows, units * wrows),
            rows_out(chans, F32, unit),
        ],
        [
            ((unit + 2 * width, chans), F32),
            ((unit, chans), F32),
            ((wrows * chans // LANES, 4 * SLOT), BF16),
        ],
        dense * 4 * chans,
    )
    x3, x4, n1, h1, s1 = call(
        mlp_forward_kernel,
        chunks,
        near(x2, chunk) + [rows_in(mask, chunk), vec(1), whole(up_w[0]), whole(up_bias[0:1]), whole(down_w[0])],
        [
            rows_out(chans, F32),
            rows_out(chans, F32),
            rows_out(chans, BF16),
            rows_out(ff, BF16),
            rows_out(ff, BF16),
        ],
        [((chunk + 2 * width, chans), F32), ((chunk, chans), F32)],
        dense * 2 * ff,
    )
    x5, n2, m2, gram = call(
        channel_mix_kernel,
        chunks,
        near(x4, chunk) + [rows_in(mask, chunk), vec(2), whole(mix_w[1]), whole(bias1)],
        [
            rows_out(chans, F32),
            rows_out(chans, BF16),
            rows_out(3 * chans, BF16),
            sums(chans // LANES, LANES, LANES),
        ],
        [((chunk + 2 * width, chans), F32)],
        dense * 3 * chans,
    )
    gram = across(gram)
    o2, x6 = call(
        channel_out_kernel,
        chunks,
        [
            rows_in(m2, chunk),
            whole(gram),
            whole(scale),
            rows_in(x5, chunk),
            rows_in(mask, chunk),
            vec(2),
            whole(out_w[1]),
        ],
        [rows_out(chans, BF16), rows_out(chans, F32)],
        [((chunk, chans), F32)],
        dense * 2 * chans,
    )
    result, g7, mlp1, up_bg1, small7 = call(
        last_mlp_kernel,
        chunks,
        near(x6, chunk)
        + [
            rows_in(mask, chunk),
            vec(3),
            whole(up_w[1]),
            whole(up_bias[1:2]),
            whole(down_w[1]),
            rows_in(cot, chunk),
        ],
        [
            rows_out(chans, BF16),
            rows_out(chans, F32),
            sums(2 * ff, chans, dtype=BF16),
            sums(8, ff),
            sums(24, chans),
        ],
        [
            ((chunk + 2 * width, chans), F32),
            ((chunk, chans), F32),
            ((chunk, chans), F32),
            ((chunk, chans), F32),
            ((chunk, chans), BF16),
            ((chunk, ff), BF16),
            ((chunk, ff), BF16),
            ((chans, ff), F32),
            ((ff, chans), F32),
        ],
        dense * 6 * ff,
    )
    result = send_result(result)
    g6, do2, weights_g, out1, conv_g3, small6 = call(
        channel_grad_kernel,
        chunks,
        near(g7, chunk)
        + [
            rows_in(mask, chunk),
            vec(3),
            rows_in(x6, chunk),
            (m2, (chunk, chans), lambda i: (i, 0)),
            rows_in(o2, chunk),
            whole(out_w[1]),
        ],
        [
            rows_out(chans, F32),
            rows_out(chans, BF16),
            sums(chans // LANES, LANES, LANES),
            sums(chans, chans, dtype=BF16),
            sums(72, chans),
            sums(16, chans),
        ],
        [((chunk + 2 * width, chans), F32), ((chunk, chans), BF16), ((chans, chans), F32)],
        dense * 3 * chans,
    )
    weights_g = across(weights_g)
    g5, mix1, mix_bg1, small5 = call(
        channel_back_kernel,
        chunks,
        [
            rows_in(do2, chunk),
            rows_in(m2, chunk),
            whole(gram),
            whole(weights_g),
            whole(scale),
            rows_in(n2, chunk),
            rows_in(x5, chunk),
            rows_in(g6, chunk),
            rows_in(mask, chunk),
            vec(2),
            whole(mix_w[1]),
        ],
        [
            rows_out(chans, F32),
            sums(3 * chans, chans, dtype=BF16),
            sums(8, 3 * chans),
            sums(16, chans),
        ],
        [((chunk, 3 * chans), BF16), ((chunk, chans), F32), ((3 * chans, chans), F32)],
        dense * 7 * chans,
    )
    g3, kept0, sent0, up_bg0, conv_g2, small3 = call(
        mlp_back_kernel,
        chunks,
        near(g5, chunk)
        + [
            rows_in(mask, chunk),
            vec(2),
            vec(1),
            rows_in(x4, chunk),
            rows_in(x3, chunk),
            rows_in(n1, chunk),
            rows_in(h1, chunk),
            rows_in(s1, chunk),
            whole(up_w[0]),
            whole(down_w[0]),
            whole(mlp1),
            whole(mix1),
            whole(out1),
            scalar,
        ],
        [
            rows_out(chans, F32),
            sums(2 * ff + 2 * chans, chans, dtype=BF16),
            sums(2 * ff + 2 * chans, chans, dtype=BF16),
            sums(8, ff),
            sums(72, chans),
            sums(32, chans),
        ],
        [
            ((chunk + 2 * width, chans), F32),
            ((chunk, chans), F32),
            ((chunk, chans), BF16),
            ((chunk, chans), F32),
            ((chunk, ff), BF16),
            ((chans, ff), F32),
            ((ff, chans), F32),
        ],
        dense * 4 * ff,
        after=(result,),
    )
    mid = share_planes(share_cores(kept0, sent0))
    g1, win0, mix_bg0, conv_g1, small1 = call(
        window_back_kernel,
        units,
        near(g3, unit)
        + [
            rows_in(mask, unit),
            vec(1),
            vec(0),
            rows_in(x2, unit),
            rows_in(x1, unit),
            rows_in(nw, wrows),
            rows_in(mw, wrows),
            rows_in(ow, wrows),
            whole(mix_w[0]),
            whole(out_w[0]),
            whole(gather),
        ],
        [
            rows_out(chans, F32, unit),
            sums(4 * chans, chans, dtype=BF16),
            sums(8, 3 * chans),
            sums(72, chans),
            sums(32, chans),
        ],
        [
            ((unit + 2 * width, chans), F32),
            ((3 * chans, chans), F32),
            ((chans, chans), F32),
            ((unit, chans), F32),
            ((wrows, chans), BF16),
            ((wrows, chans), BF16),
            ((wrows, 3 * chans), BF16),
            ((unit, chans), F32),
            ((wrows * chans // LANES, 4 * SLOT), BF16),
            ((wrows * chans // LANES, 4 * SLOT), BF16),
        ],
        dense * 16 * chans,
    )
    x0_flat = x0.reshape(tokens, chans)
    tokens_grad, conv_g0, small0 = call(
        token_grad_kernel,
        chunks,
        near(g1, chunk) + [rows_in(mask, chunk), vec(0), rows_in(x0_flat, chunk)],
        [rows_out(chans, BF16), sums(72, chans), sums(8, chans)],
        [((chunk + 2 * width, chans), F32)],
        dense * 30,
        after=(mid,),
    )

    sums0 = (conv_g0, conv_g1, conv_g2, conv_g3, small0, small1, small3, small5, small6, small7)
    bias_sums = (mix_bg0, mix_bg1, up_bg0, up_bg1)
    kept, sent = fold_small(core, win0, sums0 + bias_sums, chans)
    return result, tokens_grad, mid, kept, sent


def small_kernel(
    core, win0, conv0, conv1, conv2, conv3, s0, s1, s3, s5, s6, s7, mix0, mix1, up0, up1,
    kept, sent, rows,
):
    chans = rows.shape[1]
    rows[...] = jnp.zeros_like(rows)
    place = 0

    def put(part):
        nonlocal place
        rows[place : place + 1, :] = jnp.sum(part, axis=0, keepdims=True)
        place += 1

    for conv in (conv0, conv1, conv2, conv3):
        for k in range(9):
            put(conv[8 * k : 8 * k + 8, :])
    for ref, at in (
        (s0, 0), (s1, 0), (s3, 0), (s6, 0),
        (s1, 16), (s3, 16), (s5, 0), (s7, 8),
        (s1, 24), (s3, 24), (s5, 8), (s7, 16),
        (s1, 8), (s6, 8), (s3, 8), (s7, 0),
    ):
        put(ref[at : at + 8, :])
    for ref in (mix0, mix1, up0, up1):
        for col in range(0, ref.shape[1], chans):
            put(ref[:, col : col + chans])
    spread(core, kept, sent, [win0, rows])


def fold_small(core, win0, parts, chans):
    half = (win0.shape[0] + SMALL_ROWS) // 2
    return pl.pallas_call(
        small_kernel,
        in_specs=[pl.BlockSpec(memory_space=pltpu.SMEM)]
        + [pl.BlockSpec(memory_space=pltpu.VMEM)] * (1 + len(parts)),
        out_shape=[jax.ShapeDtypeStruct((half, chans), BF16)] * 2,
        scratch_shapes=[pltpu.VMEM((SMALL_ROWS, chans), F32)],
        compiler_params=pltpu.CompilerParams(vmem_limit_bytes=VMEM_LIMIT),
    )(core, win0, *parts)


def reader(first, second):
    half = first.shape[0]

    def read(at, count):
        parts = []
        if at < half:
            parts.append(first[at : min(at + count, half), :].astype(F32))
        if at + count > half:
            parts.append(second[max(at - half, 0) : at + count - half, :].astype(F32))
        return parts[0] if len(parts) == 1 else jnp.concatenate(parts, axis=0)

    return read


def put_attention(read, mix_w, out_w):
    chans = out_w.shape[1]
    for k in range(3):
        mix_w[0, :, k * chans : (k + 1) * chans] = read(k * chans, chans)
    out_w[0] = read(3 * chans, chans)


def put_feed(read, at, up_w, down_w):
    chans = down_w.shape[2]
    blocks = up_w.shape[2] // chans
    for k in range(blocks):
        up_w[0, :, k * chans : (k + 1) * chans] = read(at + k * chans, chans)
    for k in range(blocks):
        down_w[0, k * chans : (k + 1) * chans, :] = read(at + (blocks + k) * chans, chans)


def feed_kernel(core, mid_a, mid_b, mix_w, out_w, up_w, down_w):
    layer = pl.program_id(0)
    chans = mid_a.shape[1]
    feed_rows = 2 * up_w.shape[2]
    for flag in range(2):
        mid = reader(*((mid_a, mid_b) if flag == 0 else (mid_b, mid_a)))

        @pl.when((core[0] == flag) & (layer == 0))
        def _():
            put_feed(mid, feed_rows + 4 * chans, up_w, down_w)

        @pl.when((core[0] == flag) & (layer == 1))
        def _():
            put_attention(lambda at, count: mid(feed_rows + at, count), mix_w, out_w)
            put_feed(mid, 0, up_w, down_w)


def late_kernel(
    core, late_a, late_b, mix_in, out_in,
    mix_w, out_w, conv_w, conv_b, gain, shift, last_shift, win_b, chan_b, out_b, up_b, down_b,
    rows,
):
    chans = late_a.shape[1]
    blocks = up_b.shape[1] // chans
    for flag in range(2):
        late = reader(*((late_a, late_b) if flag == 0 else (late_b, late_a)))

        @pl.when(core[0] == flag)
        def _():
            put_attention(late, mix_w, out_w)
            rows[...] = late(4 * chans, SMALL_ROWS)

    at = 0
    for k in range(4):
        for i in range(3):
            conv_w[k, i] = rows[at : at + 3, :]
            at += 3
    for ref in (conv_b, gain):
        ref[...] = rows[at : at + 4, :]
        at += 4
    shift[...] = rows[at : at + 3, :]
    last_shift[...] = rows[at + 3 : at + 4, :]
    at += 4
    for ref in (out_b, down_b):
        ref[...] = rows[at : at + 2, :]
        at += 2
    win_b[0:1, :] = rows[at : at + 1, :]
    win_b[1:2, :] = rows[at + 2 : at + 3, :]
    chan_b[...] = rows[at + 3 : at + 6, :]
    at += 6
    for k in range(2):
        for i in range(blocks):
            up_b[k : k + 1, i * chans : (i + 1) * chans] = rows[at : at + 1, :]
            at += 1


def feed_grads(core, mid, chans, ff):
    mix_shape, out_shape = (2, chans, 3 * chans), (2, chans, chans)
    up_shape, down_shape = (2, chans, ff), (2, ff, chans)
    return pl.pallas_call(
        feed_kernel,
        grid=(2,),
        in_specs=[pl.BlockSpec(memory_space=pltpu.SMEM)]
        + [pl.BlockSpec(x.shape, lambda i: (0, 0), pipeline_mode=pl.Buffered(1)) for x in mid],
        out_specs=[pl.BlockSpec((1,) + x[1:], lambda i: (1, 0, 0)) for x in (mix_shape, out_shape)]
        + [pl.BlockSpec((1,) + x[1:], lambda i: (i, 0, 0)) for x in (up_shape, down_shape)],
        out_shape=[jax.ShapeDtypeStruct(x, F32) for x in (mix_shape, out_shape, up_shape, down_shape)],
        compiler_params=pltpu.CompilerParams(vmem_limit_bytes=VMEM_LIMIT),
    )(core, *mid)


def assemble(result, tokens_grad, core, late, feed):
    mix_w, out_w, up_w, down_w = feed
    _, chans, ff = up_w.shape
    smem = pl.BlockSpec(memory_space=pltpu.SMEM)
    shapes = [
        (4, 3, 3, chans), (4, chans), (4, chans), (3, chans), (1, chans),
        (2, chans), (3, chans), (2, chans), (2, ff), (2, chans),
    ]

    def fixed(shape):
        return pl.BlockSpec(shape, lambda i: (0,) * len(shape))

    mix_w, out_w, conv_w, conv_b, gain, shift, last_shift, win_b, chan_b, out_b, up_b, down_b = pl.pallas_call(
        late_kernel,
        grid=(1,),
        in_specs=[smem] + [fixed(x.shape) for x in late] + [pl.BlockSpec(memory_space=pl.ANY)] * 2,
        out_specs=[fixed((1,) + x[1:]) for x in (mix_w.shape, out_w.shape)] + [fixed(x) for x in shapes],
        out_shape=[jax.ShapeDtypeStruct(x, F32) for x in (mix_w.shape, out_w.shape, *shapes)],
        input_output_aliases={3: 0, 4: 1},
        scratch_shapes=[pltpu.VMEM((SMALL_ROWS, chans), F32)],
        compiler_params=pltpu.CompilerParams(vmem_limit_bytes=VMEM_LIMIT),
    )(core, *late, mix_w, out_w)
    return (
        result, tokens_grad, conv_w, conv_b, gain, shift, last_shift.reshape(-1), mix_w,
        win_b.reshape(-1), chan_b.reshape(-1), out_w, out_b, up_w, up_b, down_w, down_b,
    )


def widen_kernel(here, *refs):
    out = refs[-1]
    cols = out.shape[2]
    for step, part in enumerate(refs[:-1]):

        @pl.when(pl.program_id(0) == step)
        def _():
            out[0] = part[:, :cols, :].astype(F32)


def widen(parts, here, cols):
    images = len(parts)
    height, width, chans = parts[0].shape
    return pl.pallas_call(
        widen_kernel,
        grid_spec=pltpu.PrefetchScalarGridSpec(
            num_scalar_prefetch=1,
            grid=(images,),
            in_specs=[pl.BlockSpec(x.shape, lambda i, at: (0, 0, 0), pipeline_mode=pl.Buffered(1)) for x in parts],
            out_specs=pl.BlockSpec(
                (1, height, cols, chans), lambda i, at: ((at[0] + images - i) % images, 0, 0, 0)
            ),
        ),
        out_shape=jax.ShapeDtypeStruct((images, height, cols, chans), F32),
        compiler_params=pltpu.CompilerParams(vmem_limit_bytes=VMEM_LIMIT),
    )(here.astype(jnp.int32).reshape(1), *parts)


def local(
    tokens, heights, conv_weight, conv_bias, norm_gain, norm_shift, mix_weight, window_bias, channel_bias,
    out_weight, out_bias, up_weight, up_bias, down_weight, down_bias, cotangent,
):
    images, height, cols, chans = tokens.shape
    count = lax.axis_size("rows")
    place = lax.axis_index("rows")
    width = -(-cols // 8) * 8
    groups = count // images
    members = [[g * images + j for j in range(images)] for g in range(groups)]
    rows_here = images * height
    level = lax.dynamic_index_in_dim(heights, place % images, 0, keepdims=False)
    open_rows = heights * 7 - place * height

    def gather_image(field):
        inside = jnp.arange(height, dtype=jnp.int32)[None, :] < open_rows[:, None]
        field = jnp.where(inside[:, :, None, None], field, jnp.zeros((), field.dtype))
        field = jnp.pad(field, ((0, 0), (0, 0), (0, width - cols), (0, 0)))
        field = lax.all_to_all(field, "rows", 0, 0, axis_index_groups=members, tiled=True)
        return field.reshape(rows_here, width, chans)

    def scatter_image(field):
        field = field.reshape(images, height, width, chans)
        field = lax.all_to_all(field, "rows", 0, 0, axis_index_groups=members, tiled=True)
        return field[:, :, :cols]

    def halo_of(field):
        flat = field.reshape(rows_here * width, chans)
        if groups == 1:
            return jnp.zeros((2 * width, chans), F32)
        down = [(i, i + images) for i in range(count - images)]
        up = [(i + images, i) for i in range(count - images)]
        above = lax.ppermute(flat[-width:].astype(BF16), "rows", down)
        below = lax.ppermute(flat[:width].astype(BF16), "rows", up)
        return jnp.concatenate([above, below], axis=0).astype(F32)

    def across(value):
        if groups == 1:
            return value
        other = [[j + g * images for g in range(groups)] for j in range(images)]
        return lax.psum(value, "rows", axis_index_groups=other)

    row = jnp.arange(rows_here * width, dtype=jnp.int32) // width + place // images * rows_here
    col = jnp.arange(rows_here * width, dtype=jnp.int32) % width
    mask = ((row < level * 7) & (col < cols)).astype(F32)
    mask = jnp.broadcast_to(mask[:, None], (rows_here * width, LANES))
    scale = lax.rsqrt((level * 7 * cols).astype(F32))
    scale = jnp.broadcast_to(scale, (8, LANES))
    x0 = gather_image(tokens)
    cot = gather_image(cotangent).reshape(rows_here * width, chans)

    def exchange(part, axis, step):
        size = lax.axis_size(axis)
        return lax.ppermute(part, axis, [(i, i ^ step) for i in range(size)])

    core = lax.axis_index("core").astype(jnp.int32).reshape(1)

    def share_cores(kept, sent):
        return (kept.astype(F32) + exchange(sent, "core", 1).astype(F32)).astype(BF16)

    def share(part, axis):
        size, me = lax.axis_size(axis), lax.axis_index(axis)
        rows = part.shape[0] // size

        def piece(step):
            return lax.dynamic_slice_in_dim(part, (me ^ step) * rows, rows, 0)

        total = piece(0).astype(F32)
        for step in range(1, size):
            total = total + exchange(piece(step), axis, step).astype(F32)
        return total.astype(BF16)

    def gather(part, axis):
        size, me = lax.axis_size(axis), lax.axis_index(axis)
        rows = part.shape[0]
        out = jnp.zeros((size * rows, part.shape[1]), part.dtype)
        for step in range(size):
            got = part if step == 0 else exchange(part, axis, step)
            out = lax.dynamic_update_slice_in_dim(out, got, (me ^ step) * rows, 0)
        return out

    def send_tokens(field):
        field = field.reshape(images, height, width, chans)
        here = place % images
        parts = []
        for step in range(images):
            part = lax.dynamic_index_in_dim(field, (here + step) % images, 0, keepdims=False)
            if step:
                pairs = [(g * images + j, g * images + (j + step) % images) for g in range(groups) for j in range(images)]
                part = lax.ppermute(part, "rows", pairs)
            parts.append(part)
        return parts

    weights = (
        conv_weight, conv_bias, norm_gain, norm_shift, mix_weight, window_bias, channel_bias,
        out_weight, out_bias, up_weight, up_bias, down_weight, down_bias,
    )
    result, tokens_grad, mid, kept, sent = image_block(
        x0, cot, halo_of(x0), mask, scale, halo_of, across, weights, cols, core,
        scatter_image, share_cores, lambda part: share(part, "plane"),
    )
    together = lax.optimization_barrier
    tokens_grad = send_tokens(tokens_grad)
    mid = share(mid, "rows")
    late = share_cores(kept, sent)
    late, mid = together((late, mid))
    late, mid = share(late, "plane"), gather(mid, "rows")
    late, mid = together((late, mid))
    late, mid = share(late, "rows"), gather(mid, "plane")
    late, mid, tokens_grad = together((late, mid, tokens_grad))
    late, mid = gather(late, "rows"), (mid, exchange(mid, "core", 1))
    tokens_grad = widen(tokens_grad, place % images, cols)
    late, mid, tokens_grad = together((late, mid, tokens_grad))
    late, feed = gather(late, "plane"), feed_grads(core, mid, chans, up_weight.shape[2])
    late, feed = together((late, feed))
    return assemble(result, tokens_grad, core, (late, exchange(late, "core", 1)), feed)


def solution(mesh):
    planes = mesh.shape["dp"] // 2
    fine = Mesh(mesh.devices.reshape(planes, 2, mesh.shape["rows"]), ("plane", "core", "rows"))
    dp = ("plane", "core")
    split = P(dp, "rows", None, None)
    in_specs = (split, P(dp)) + (P(),) * 13 + (split,)
    out_specs = (split, split) + (P(),) * 14
    return jax.shard_map(local, mesh=fine, in_specs=in_specs, out_specs=out_specs, check_vma=False)
```

```python
import functools

import jax
import jax.numpy as jnp
import numpy as np
from jax import lax
from jax.experimental import pallas as pl
from jax.experimental.pallas import tpu as pltpu
from jax.sharding import Mesh
from jax.sharding import PartitionSpec as P

HEADS = 12
HEAD_DIM = 32
EPS = 1e-05
WIN = 7
SLOT = 64
LANES = 128
F32 = jnp.float32
BF16 = jnp.bfloat16
SCALE = HEAD_DIM ** (-0.5)
LOG2E = 1.4426950408889634
ROOT_HALF = 0.7071067811865476
VMEM_LIMIT = 58 * 1024 * 1024
SMALL_ROWS = 512


def dot(left, right):
    return jnp.dot(left, right, preferred_element_type=F32)


def dot_nt(left, right):
    return lax.dot_general(left, right, (((1,), (1,)), ((), ())), preferred_element_type=F32)


def dot_tn(left, right):
    return lax.dot_general(left, right, (((0,), (0,)), ((), ())), preferred_element_type=F32)


def low(value):
    return value.astype(BF16).astype(F32)


def fold(value):
    rows, cols = value.shape
    return jnp.sum(value.reshape(rows // 8, 8, cols), axis=0)


def loop(count, step, body):
    for at in range(0, count, step):
        body(at)


def lane_tiles(chans):
    return [slice(t, t + LANES) for t in range(0, chans, LANES)]


def gelu_parts(value):
    size = jnp.abs(value)
    t = 1.0 / (1.0 + (0.3275911 * ROOT_HALF) * size)
    poly = t * (
        0.127414796
        + t * (-0.142248368 + t * (0.7107068705 + t * (-0.7265760135 + t * 0.5307027145)))
    )
    bell = jnp.exp2(value * value * (-0.5 * LOG2E))
    tail = poly * bell
    cdf = jnp.where(value >= 0.0, 1.0 - tail, tail)
    return value * cdf, cdf + value * bell * 0.3989422804014327


def norm_of(value, gain, shift):
    centre = value - jnp.mean(value, axis=-1, keepdims=True)
    spread = jnp.mean(centre * centre, axis=-1, keepdims=True)
    return centre * lax.rsqrt(spread + EPS) * gain + shift


def norm_back(value, gain, normed_grad):
    centre = value - jnp.mean(value, axis=-1, keepdims=True)
    inv = lax.rsqrt(jnp.mean(centre * centre, axis=-1, keepdims=True) + EPS)
    unit = centre * inv
    unit_grad = normed_grad * gain
    first = jnp.mean(unit_grad, axis=-1, keepdims=True)
    second = jnp.mean(unit_grad * unit, axis=-1, keepdims=True)
    return inv * (unit_grad - first - unit * second), normed_grad * unit


def fill_source(src, main, prev, after, halo, step, steps, width):
    rows = main.shape[0]
    src[pl.ds(0, width), :] = jnp.where(step == 0, halo[0:width, :], low(prev[...]))
    src[pl.ds(rows + width, width), :] = jnp.where(
        step == steps - 1, halo[width : 2 * width, :], low(after[...])
    )

    def body(at):
        src[pl.ds(at + width, 2 * width), :] = low(main[pl.ds(at, 2 * width), :])

    loop(rows // (2 * width) * 2 * width, 2 * width, body)
    if rows % (2 * width):
        at = rows - width
        src[pl.ds(at + width, width), :] = low(main[pl.ds(at, width), :])


def conv_tile(src, vec, at, tile, width, lanes, flipped):
    rows = [src[pl.ds(at + width * d, tile), lanes] for d in range(3)]
    sums = []
    for col in range(3):
        total = None
        for row in range(3):
            k = (2 - row) * 3 + (2 - col) if flipped else row * 3 + col
            term = rows[row] * vec[k : k + 1, lanes]
            total = term if total is None else total + term
        sums.append(total)
    return sums[1] + pltpu.roll(sums[0], 1, 0) + pltpu.roll(sums[2], tile - 1, 0), rows


def conv_weight_tile(acc, rows, field, tile, lanes):
    shifted = [pltpu.roll(field, 1, 0), field, pltpu.roll(field, tile - 1, 0)]
    for row in range(3):
        for col in range(3):
            k = row * 3 + col
            acc[8 * k : 8 * k + 8, lanes] += fold(shifted[col] * rows[2 - row])


def block_heads(part):
    lane = lax.broadcasted_iota(jnp.int32, part.shape, 1)
    zero = jnp.zeros_like(part)
    return jnp.concatenate(
        [jnp.where(lane // HEAD_DIM == h, part, zero) for h in range(LANES // HEAD_DIM)], axis=0
    )


def window_forward_kernel(
    tok, prev, after, halo, mask, vec, mix, mix_b, out_w, gather, x1, nw, mw, ow, x2, src, keep, probs
):
    step, steps = pl.program_id(0), pl.num_programs(0)
    rows, width, chans = tok.shape
    src[pl.ds(0, width), :] = jnp.where(step == 0, halo[0:width, :], prev[0].astype(F32))
    src[pl.ds((rows + 1) * width, width), :] = jnp.where(
        step == steps - 1, halo[width : 2 * width, :], after[0].astype(F32)
    )
    for i in range(rows):
        src[pl.ds((i + 1) * width, width), :] = tok[i].astype(F32)

    def conv_body(at):
        region = mask[pl.ds(at, width), :]
        for lanes in lane_tiles(chans):
            got, near = conv_tile(src, vec, at, width, width, lanes, False)
            x1[pl.ds(at, width), lanes] = region * (near[1] + got + vec[9:10, lanes])

    loop(rows * width, width, conv_body)

    normed = norm_of(x1[...], vec[10:11, :], vec[11:12, :]).astype(BF16)
    normed = dot(gather[...], normed).astype(BF16)
    nw[...] = normed
    mw[...] = (dot(normed, mix[...]) + mix_b[...]).astype(BF16)
    windows = nw.shape[0] // SLOT
    lane = lax.broadcasted_iota(jnp.int32, (SLOT, LANES), 1)
    left = lane < SLOT
    real = lane % SLOT < WIN * WIN
    ones = (
        lax.broadcasted_iota(jnp.int32, (4 * SLOT, LANES), 0) // SLOT
        == lax.broadcasted_iota(jnp.int32, (4 * SLOT, LANES), 1) // HEAD_DIM
    ).astype(BF16)
    floor = -1e30

    places = [(at, lanes) for at in range(0, windows * SLOT, SLOT) for lanes in lane_tiles(chans)]
    for n, (at, lanes) in enumerate(places):
        query = mw[at : at + SLOT, lanes]
        key = mw[at : at + SLOT, chans + lanes.start : chans + lanes.stop]
        scores = dot_nt(query, block_heads(key))
        for half in range(2):
            part = jnp.where(real, scores[:, half * LANES : (half + 1) * LANES], floor)
            top_l = jnp.max(jnp.where(left, part, floor), axis=1, keepdims=True)
            top_r = jnp.max(jnp.where(left, floor, part), axis=1, keepdims=True)
            top = jnp.where(left, top_l, top_r)
            raised = jnp.exp2((part - top) * (SCALE * LOG2E)).astype(BF16)
            probs[n * SLOT : (n + 1) * SLOT, half * LANES : (half + 1) * LANES] = raised
    for n, (at, lanes) in enumerate(places):
        value = mw[at : at + SLOT, 2 * chans + lanes.start : 2 * chans + lanes.stop]
        both = dot(
            probs[n * SLOT : (n + 1) * SLOT, :], jnp.concatenate([block_heads(value), ones], axis=1)
        )
        ow[at : at + SLOT, lanes] = (both[:, :LANES] / both[:, LANES:]).astype(BF16)
    merged = dot_tn(gather[...], ow[...]).astype(BF16)
    keep[...] = dot(merged, out_w[...])

    def out_body(at):
        region = mask[pl.ds(at, width), :]
        for lanes in lane_tiles(chans):
            x2[pl.ds(at, width), lanes] = region * (
                x1[pl.ds(at, width), lanes] + keep[pl.ds(at, width), lanes] + vec[12:13, lanes]
            )

    loop(rows * width, width, out_body)


def conv_forward(main, prev, after, halo, mask, vec, out, src, width):
    step, steps = pl.program_id(0), pl.num_programs(0)
    rows, chans = main.shape
    fill_source(src, main, prev, after, halo, step, steps, width)
    tile = 2 * width

    def body(at):
        region = mask[pl.ds(at, tile), :]
        for lanes in lane_tiles(chans):
            got, _ = conv_tile(src, vec, at, tile, width, lanes, False)
            out[pl.ds(at, tile), lanes] = region * (
                main[pl.ds(at, tile), lanes] + got + vec[9:10, lanes]
            )

    loop(rows, tile, body)


def norm_forward(value, vec, out):
    out[...] = norm_of(value[...], vec[10:11, :], vec[11:12, :]).astype(BF16)


def mlp_body(normed, up_w, up_b, down_w, hidden, slope, keep):
    rows = normed.shape[0]
    for at in range(0, up_w.shape[1], 256):
        cols = slice(at, at + 256)
        pre = dot(normed[...], up_w[:, cols]) + up_b[:, cols]
        for row in range(0, rows, 144):
            act, der = gelu_parts(pre[row : row + 144])
            hidden[row : row + 144, cols] = act.astype(BF16)
            slope[row : row + 144, cols] = der.astype(BF16)
        part = dot(hidden[:, cols], down_w[cols, :])
        if at == 0:
            keep[...] = part
        else:
            keep[...] += part


def add_residual(state, branch, mask, vec, out):
    chans = state.shape[1]

    def body(at):
        region = mask[pl.ds(at, 144), :]
        for lanes in lane_tiles(chans):
            out[pl.ds(at, 144), lanes] = (
                region
                * (state[pl.ds(at, 144), lanes] + branch[pl.ds(at, 144), lanes] + vec[12:13, lanes])
            ).astype(out.dtype)

    loop(state.shape[0], 144, body)


def mlp_forward_kernel(
    main, prev, after, halo, mask, vec, up_w, up_b, down_w, x3, x4, normed, hidden, slope, src, keep
):
    width = prev.shape[0]
    conv_forward(main, prev, after, halo, mask, vec, x3, src, width)
    norm_forward(x3, vec, normed)
    mlp_body(normed, up_w, up_b, down_w, hidden, slope, keep)
    add_residual(x3, keep, mask, vec, x4)


def norm_backward(state, normed_grad, grad, vec, small, out, gain_row):
    part = normed_grad[...]
    back, scaled = norm_back(state[...], vec[10:11, :], part)
    out[...] = grad[...].astype(F32) + back
    small[gain_row : gain_row + 8, :] += fold(scaled)
    small[gain_row + 8 : gain_row + 16, :] += fold(part)


def mlp_down_back(rounded, normed, hidden, slope, pre_grad, up_w, down_w, up_g, up_bg, down_g):
    rows = rounded.shape[0]
    for at in range(0, up_w.shape[1], 256):
        cols = slice(at, at + 256)
        hidden_grad = dot_nt(rounded[...], down_w[cols, :])
        total = None
        for row in range(0, rows, 144):
            part = hidden_grad[row : row + 144] * slope[row : row + 144, cols].astype(F32)
            pre_grad[row : row + 144, cols] = part.astype(BF16)
            total = fold(part) if total is None else total + fold(part)
        up_bg[:, cols] += total
        up_g[:, cols] += dot_tn(normed[...], pre_grad[:, cols])
        down_g[cols, :] += dot_tn(hidden[:, cols], rounded[...])


def mlp_both(normed, cot, up_w, up_b, down_w, hidden, pre_grad, up_g, up_bg, down_g):
    rows = normed.shape[0]
    for at in range(0, up_w.shape[1], 256):
        cols = slice(at, at + 256)
        pre = dot(normed[...], up_w[:, cols]) + up_b[:, cols]
        hidden_grad = dot_nt(cot[...], down_w[cols, :])
        total = None
        for row in range(0, rows, 144):
            act, der = gelu_parts(pre[row : row + 144])
            hidden[row : row + 144, cols] = act.astype(BF16)
            part = hidden_grad[row : row + 144] * der
            pre_grad[row : row + 144, cols] = part.astype(BF16)
            total = fold(part) if total is None else total + fold(part)
        up_bg[:, cols] += total
        up_g[:, cols] += dot_tn(normed[...], pre_grad[:, cols])
        down_g[cols, :] += dot_tn(hidden[:, cols], cot[...])


def column_blocks(source, chans):
    return [source.at[:, col : col + chans] for col in range(0, source.shape[1], chans)]


def spread(core, kept, sent, blocks):
    half = kept.shape[0]
    for flag in range(2):

        @pl.when(core[0] == flag)
        def _():
            at = 0
            for block in blocks:
                rows = block.shape[0]
                cuts = [0, rows] if not at < half < at + rows else [0, half - at, rows]
                for low_cut, high_cut in zip(cuts, cuts[1:]):
                    start = at + low_cut
                    target = kept if (start >= half) == (flag == 1) else sent
                    start = start % half
                    target[start : start + high_cut - low_cut, :] = block[
                        low_cut:high_cut, :
                    ].astype(BF16)
                at += rows


def last_step():
    return pl.program_id(0) == pl.num_programs(0) - 1


def zero_first(*refs):
    @pl.when(pl.program_id(0) == 0)
    def _():
        for ref in refs:
            ref[...] = jnp.zeros_like(ref)


def last_mlp_kernel(
    main, prev, after, halo, mask, vec, up_w, up_b, down_w, cot,
    result, grad, packed, up_bg, small,
    src, x7, keep, back, normed, hidden, pre_grad, up_g, down_g,
):
    width = prev.shape[0]
    zero_first(up_g, up_bg, down_g, small)
    conv_forward(main, prev, after, halo, mask, vec, x7, src, width)
    norm_forward(x7, vec, normed)
    mlp_both(normed, cot, up_w, up_b, down_w, hidden, pre_grad, up_g, up_bg, down_g)
    keep[...] = dot(hidden[...], down_w[...])
    back[...] = dot_nt(pre_grad[...], up_w[...])
    add_residual(x7, keep, mask, vec, result)
    small[0:8, :] += fold(cot[...].astype(F32))
    norm_backward(x7, back, cot, vec, small, grad, 8)

    @pl.when(last_step())
    def _():
        at = 0
        for block in column_blocks(up_g, packed.shape[1]) + [down_g]:
            packed[at : at + block.shape[0], :] = block[...].astype(BF16)
            at += block.shape[0]


def conv_backward(main, prev, after, halo, mask, vec, field, out, conv_g, small, src, width):
    step, steps = pl.program_id(0), pl.num_programs(0)
    rows, chans = main.shape
    fill_source(src, main, prev, after, halo, step, steps, width)
    tile = 72

    def body(at):
        region = mask[pl.ds(at, tile), :]
        for lanes in lane_tiles(chans):
            got, near = conv_tile(src, vec, at, tile, width, lanes, True)
            grad = main[pl.ds(at, tile), lanes]
            out[pl.ds(at, tile), lanes] = (region * (grad + got)).astype(out.dtype)
            conv_weight_tile(conv_g, near, low(field[pl.ds(at, tile), lanes]), tile, lanes)
            small[0:8, lanes] += fold(grad)

    loop(rows, tile, body)


def fold_rows(source, small, row):
    def body(at):
        small[row : row + 8, :] += fold(source[pl.ds(at, 72), :])

    loop(source.shape[0], 72, body)


def channel_mix_kernel(
    main, prev, after, halo, mask, vec, mix, mix_b, x5, normed, mixed, gram, src
):
    width = prev.shape[0]
    chans = main.shape[1]
    zero_first(gram)
    conv_forward(main, prev, after, halo, mask, vec, x5, src, width)
    norm_forward(x5, vec, normed)
    rows = main.shape[0]
    for part in range(3):
        cols = slice(part * chans, (part + 1) * chans)
        got = dot(normed[...], mix[:, cols]) + mix_b[:, cols]
        if part == 1:
            got = got * jnp.concatenate([mask[...]] * (chans // LANES), axis=1)
        mixed[:, cols] = got.astype(BF16)
    for t, lanes in enumerate(lane_tiles(chans)):
        gram[t] += dot_tn(
            mixed[:, chans + lanes.start : chans + lanes.stop],
            mixed[:, 2 * chans + lanes.start : 2 * chans + lanes.stop],
        )


def same_head():
    row = lax.broadcasted_iota(jnp.int32, (LANES, LANES), 0)
    col = lax.broadcasted_iota(jnp.int32, (LANES, LANES), 1)
    return row // HEAD_DIM == col // HEAD_DIM


def channel_weights(gram, scale):
    own = same_head()
    logits = jnp.where(own, gram * scale, -1e30)
    top = jnp.max(logits, axis=1, keepdims=True)
    raised = jnp.where(own, jnp.exp(logits - top), 0.0)
    return raised / jnp.sum(raised, axis=1, keepdims=True)


def channel_out_kernel(mixed, gram, scale, x5, mask, vec, out_w, o2, x6, keep):
    chans = x5.shape[1]
    for t, lanes in enumerate(lane_tiles(chans)):
        weights = channel_weights(gram[t], scale[0:1, :]).astype(BF16)
        o2[:, lanes] = dot_nt(mixed[:, lanes], weights).astype(BF16)
    keep[...] = dot(o2[...], out_w[...])
    add_residual(x5, keep, mask, vec, x6)


def channel_grad_kernel(
    main, prev, after, halo, mask, vec, x6, mixed, o2, out_w,
    grad, attended_grad, weights_g, packed, conv_g, small, src, rounded, out_g,
):
    width = prev.shape[0]
    chans = main.shape[1]
    zero_first(weights_g, out_g, conv_g, small)
    conv_backward(main, prev, after, halo, mask, vec, x6, grad, conv_g, small, src, width)
    rounded[...] = grad[...].astype(BF16)
    fold_rows(grad, small, 8)
    out_g[...] += dot_tn(o2[...], rounded[...])
    attended_grad[...] = dot_nt(rounded[...], out_w[...]).astype(BF16)
    for t, lanes in enumerate(lane_tiles(chans)):
        weights_g[t] += dot_tn(attended_grad[:, lanes], mixed[:, lanes])

    @pl.when(last_step())
    def _():
        packed[...] = out_g[...].astype(BF16)


def channel_back_kernel(
    attended_grad, mixed, gram, weights_g, scale, normed, x5, g6, mask, vec, mix,
    grad, packed, mix_bg, small, mixed_grad, keep, mix_g,
):
    chans = x5.shape[1]
    zero_first(mix_g, mix_bg, small)
    own = same_head()
    wide = mask[...]
    for t, lanes in enumerate(lane_tiles(chans)):
        weights = channel_weights(gram[t], scale[0:1, :])
        back = jnp.where(own, weights_g[t], 0.0)
        logit = weights * (back - jnp.sum(back * weights, axis=1, keepdims=True))
        logit = logit.astype(BF16)
        key = slice(chans + lanes.start, chans + lanes.stop)
        val = slice(2 * chans + lanes.start, 2 * chans + lanes.stop)
        query_grad = dot(attended_grad[:, lanes], weights.astype(BF16))
        key_grad = dot_nt(mixed[:, val], logit) * scale[0:1, :] * wide
        value_grad = dot(mixed[:, key], logit) * scale[0:1, :]
        for cols, part in ((lanes, query_grad), (key, key_grad), (val, value_grad)):
            mix_bg[:, cols] += fold(part)
            mixed_grad[:, cols] = part.astype(BF16)
    for part in range(3):
        cols = slice(part * chans, (part + 1) * chans)
        mix_g[part * chans : (part + 1) * chans, :] += dot_tn(normed[...], mixed_grad[:, cols])
    keep[...] = dot_nt(mixed_grad[...], mix[...])
    norm_backward(x5, keep, g6, vec, small, grad, 0)

    @pl.when(last_step())
    def _():
        packed[...] = mix_g[...].astype(BF16)


def mlp_back_kernel(
    main, prev, after, halo, mask, vec_conv, vec, x4, x3, normed, hidden, slope, up_w, down_w, mlp1, mix1, out1, core,
    grad, kept, sent, up_bg, conv_g, small,
    src, g4, rounded, keep, pre_grad, up_g, down_g,
):
    width = prev.shape[0]
    zero_first(up_g, up_bg, down_g, conv_g, small)
    conv_backward(main, prev, after, halo, mask, vec_conv, x4, g4, conv_g, small, src, width)
    rounded[...] = g4[...].astype(BF16)
    fold_rows(g4, small, 8)
    mlp_down_back(rounded, normed, hidden, slope, pre_grad, up_w, down_w, up_g, up_bg, down_g)
    keep[...] = dot_nt(pre_grad[...], up_w[...])
    norm_backward(x3, keep, g4, vec, small, grad, 16)

    @pl.when(last_step())
    def _():
        spread(core, kept, sent, [mlp1, mix1, out1] + column_blocks(up_g, kept.shape[1]) + [down_g])


def window_back_kernel(
    main, prev, after, halo, mask, vec_conv, vec, x2, x1, nw, mw, ow, mix, out_w, gather,
    grad, packed, mix_bg, conv_g, small,
    src, mix_g, out_g, g2, gw, dow, dmw, keep, probs, slopes,
):
    width = prev.shape[0]
    chans = main.shape[1]
    zero_first(mix_g, mix_bg, out_g, conv_g, small)
    conv_backward(main, prev, after, halo, mask, vec_conv, x2, g2, conv_g, small, src, width)
    fold_rows(g2, small, 8)
    gw[...] = dot(gather[...], g2[...].astype(BF16)).astype(BF16)
    out_g[...] += dot_tn(ow[...], gw[...])
    dow[...] = dot_nt(gw[...], out_w[...]).astype(BF16)
    windows = nw.shape[0] // SLOT
    real = lax.broadcasted_iota(jnp.int32, (SLOT, 4 * SLOT), 0) < WIN * WIN
    head = lax.broadcasted_iota(jnp.int32, (SLOT, LANES), 1) // HEAD_DIM

    places = [(at, lanes) for at in range(0, windows * SLOT, SLOT) for lanes in lane_tiles(chans)]
    for n, (at, lanes) in enumerate(places):
        rows = slice(at, at + SLOT)
        query = mw[rows, lanes]
        key = mw[rows, chans + lanes.start : chans + lanes.stop]
        value = mw[rows, 2 * chans + lanes.start : 2 * chans + lanes.stop]
        scores = jnp.where(real, dot_nt(key, block_heads(query)), -1e30)
        top = jnp.max(scores, axis=0, keepdims=True)
        raised = jnp.exp2((scores - top) * (SCALE * LOG2E))
        share = raised * (1.0 / jnp.sum(raised, axis=0, keepdims=True))
        share_grad = dot_nt(value, block_heads(dow[rows, lanes]))
        inner = jnp.sum(share_grad * share, axis=0, keepdims=True)
        probs[n * SLOT : (n + 1) * SLOT, :] = share.astype(BF16)
        slopes[n * SLOT : (n + 1) * SLOT, :] = (share * (share_grad - inner)).astype(BF16)
    for n, (at, lanes) in enumerate(places):
        rows = slice(at, at + SLOT)
        key_cols = slice(chans + lanes.start, chans + lanes.stop)
        value_cols = slice(2 * chans + lanes.start, 2 * chans + lanes.stop)
        share, slope = probs[n * SLOT : (n + 1) * SLOT, :], slopes[n * SLOT : (n + 1) * SLOT, :]
        value_grad = dot(share, block_heads(dow[rows, lanes]))
        key_grad = dot(slope, block_heads(mw[rows, lanes])) * SCALE
        full = dot_tn(slope, mw[rows, key_cols])
        query_grad = jnp.zeros((SLOT, LANES), F32)
        for h in range(LANES // HEAD_DIM):
            query_grad = jnp.where(head == h, full[h * SLOT : (h + 1) * SLOT], query_grad)
        query_grad = query_grad * SCALE
        for cols, part in ((lanes, query_grad), (key_cols, key_grad), (value_cols, value_grad)):
            dmw[rows, cols] = part.astype(BF16)
            mix_bg[:, cols] += fold(part)
    for part in range(3):
        cols = slice(part * chans, (part + 1) * chans)
        mix_g[part * chans : (part + 1) * chans, :] += dot_tn(nw[...], dmw[:, cols])
    normed_grad = dot_nt(dmw[...], mix[...]).astype(BF16)
    keep[...] = dot_tn(gather[...], normed_grad)
    norm_backward(x1, keep, g2, vec, small, grad, 16)

    @pl.when(last_step())
    def _():
        packed[: 3 * chans, :] = mix_g[...].astype(BF16)
        packed[3 * chans :, :] = out_g[...].astype(BF16)


def token_grad_kernel(main, prev, after, halo, mask, vec, field, out, conv_g, small, src):
    width = prev.shape[0]
    zero_first(conv_g, small)
    conv_backward(main, prev, after, halo, mask, vec, field, out, conv_g, small, src, width)


def call(kernel, steps, ins, outs, scratch, cost, after=()):
    count = len(ins)

    def body(*refs):
        kernel(*refs[:count], *refs[count + len(after) :])

    def spec(block, index):
        if block is None:
            return pl.BlockSpec(memory_space=pltpu.SMEM)
        if isinstance(index, int):
            fixed = (index,) + tuple(0 for _ in block[1:])
            return pl.BlockSpec((None,) + block[1:], lambda i: fixed, pipeline_mode=pl.Buffered(1))
        fixed = tuple(0 for _ in block)
        if index is None:
            return pl.BlockSpec(block, lambda i: fixed, pipeline_mode=pl.Buffered(1))
        return pl.BlockSpec(block, index)

    def out_spec(block, index):
        fixed = tuple(0 for _ in block)
        return pl.BlockSpec(block, (lambda i: fixed) if index is None else index)

    return pl.pallas_call(
        body,
        grid=(steps,),
        in_specs=[spec(block, index) for _, block, index in ins]
        + [pl.BlockSpec(memory_space=pl.ANY) for _ in after],
        out_specs=[out_spec(block, index) for _, _, block, index in outs],
        out_shape=[jax.ShapeDtypeStruct(shape, dtype) for shape, dtype, _, _ in outs],
        scratch_shapes=[pltpu.VMEM(shape, dtype) for shape, dtype in scratch],
        compiler_params=pltpu.CompilerParams(vmem_limit_bytes=VMEM_LIMIT),
        cost_estimate=pl.CostEstimate(flops=1, bytes_accessed=1, transcendentals=0),
    )(*[array for array, _, _ in ins], *after)


def gather_matrix(cols, width):
    windows = cols // WIN
    slot = np.arange(windows * SLOT)[:, None]
    window, inside = slot // SLOT, slot % SLOT
    source = inside // WIN * width + window * WIN + inside % WIN
    patch = np.arange(WIN * width)[None, :]
    return jnp.asarray(((source == patch) & (inside < WIN * WIN)).astype(BF16))


def prepare_kernel(conv_w, conv_b, gain, shift, out_b, down_b, up_b, vecs, up_bias):
    for k in range(4):
        for i in range(3):
            vecs[k, 3 * i : 3 * i + 3, :] = conv_w[k, i].astype(F32)
        last = out_b if k % 2 == 0 else down_b
        for at, ref, row in ((9, conv_b, k), (10, gain, k), (11, shift, k), (12, last, k // 2)):
            vecs[k, at : at + 1, :] = ref[row : row + 1, :].astype(F32)
    for k in range(2):
        up_bias[k] = up_b[k : k + 1, :].astype(F32)


def prepare(*parts):
    chans, ff = parts[0].shape[-1], parts[-1].shape[-1]
    return pl.pallas_call(
        prepare_kernel,
        out_shape=tuple(jax.ShapeDtypeStruct(x, F32) for x in ((4, 16, chans), (2, 1, ff))),
    )(*parts)


def image_block(x0, cot, tok_halo, mask, scale, halo_of, across, weights, small, cols, core, send_result, share_cores, share_planes):
    mix_w, out_w, up_w, down_w = weights
    height, width, chans = x0.shape
    tokens = height * width
    ff = up_w.shape[2]
    vecs, up_bias, bias0, bias1 = small
    gather = gather_matrix(cols, width)
    wrows = cols // WIN * SLOT
    unit = WIN * width
    units = height // WIN
    chunk = 2 * unit if units % 2 == 0 else unit
    chunks = tokens // chunk

    def near(array, rows):
        per = rows // width
        return [
            (array, (rows, chans), lambda i: (i, 0)),
            (array, (width, chans), lambda i: (jnp.maximum(i * per - 1, 0), 0)),
            (array, (width, chans), lambda i: (jnp.minimum(i * per + per, height - 1), 0)),
            (halo_of(array), (2 * width, chans), None),
        ]

    def rows_in(array, rows):
        return (array, (rows, array.shape[1]), lambda i: (i, 0))

    def whole(array):
        return (array, array.shape, None)

    def layer(array, k):
        return (array, array.shape, k)

    def rows_out(cols_, dtype, rows=chunk, total=tokens):
        return ((total, cols_), dtype, (rows, cols_), lambda i: (i, 0))

    def sums(*shape, dtype=F32):
        return (shape, dtype, shape, None)

    def vec(k):
        return layer(vecs, k)

    scalar = (core, None, None)

    dense = 2 * tokens * chans
    x1, nw, mw, ow, x2 = call(
        window_forward_kernel,
        units,
        [
            (x0, (WIN, width, chans), lambda i: (i, 0, 0)),
            (x0, (1, width, chans), lambda i: (jnp.maximum(i * WIN - 1, 0), 0, 0)),
            (x0, (1, width, chans), lambda i: (jnp.minimum(i * WIN + WIN, height - 1), 0, 0)),
            whole(tok_halo),
            rows_in(mask, unit),
            vec(0),
            layer(mix_w, 0),
            whole(bias0),
            layer(out_w, 0),
            whole(gather),
        ],
        [
            rows_out(chans, F32, unit),
            rows_out(chans, BF16, wrows, units * wrows),
            rows_out(3 * chans, BF16, wrows, units * wrows),
            rows_out(chans, BF16, wrows, units * wrows),
            rows_out(chans, F32, unit),
        ],
        [
            ((unit + 2 * width, chans), F32),
            ((unit, chans), F32),
            ((wrows * chans // LANES, 4 * SLOT), BF16),
        ],
        dense * 4 * chans,
    )
    x3, x4, n1, h1, s1 = call(
        mlp_forward_kernel,
        chunks,
        near(x2, chunk) + [rows_in(mask, chunk), vec(1), layer(up_w, 0), layer(up_bias, 0), layer(down_w, 0)],
        [
            rows_out(chans, F32),
            rows_out(chans, F32),
            rows_out(chans, BF16),
            rows_out(ff, BF16),
            rows_out(ff, BF16),
        ],
        [((chunk + 2 * width, chans), F32), ((chunk, chans), F32)],
        dense * 2 * ff,
    )
    x5, n2, m2, gram = call(
        channel_mix_kernel,
        chunks,
        near(x4, chunk) + [rows_in(mask, chunk), vec(2), layer(mix_w, 1), whole(bias1)],
        [
            rows_out(chans, F32),
            rows_out(chans, BF16),
            rows_out(3 * chans, BF16),
            sums(chans // LANES, LANES, LANES),
        ],
        [((chunk + 2 * width, chans), F32)],
        dense * 3 * chans,
    )
    gram = across(gram)
    o2, x6 = call(
        channel_out_kernel,
        chunks,
        [
            rows_in(m2, chunk),
            whole(gram),
            whole(scale),
            rows_in(x5, chunk),
            rows_in(mask, chunk),
            vec(2),
            layer(out_w, 1),
        ],
        [rows_out(chans, BF16), rows_out(chans, F32)],
        [((chunk, chans), F32)],
        dense * 2 * chans,
    )
    result, g7, mlp1, up_bg1, small7 = call(
        last_mlp_kernel,
        chunks,
        near(x6, chunk)
        + [
            rows_in(mask, chunk),
            vec(3),
            layer(up_w, 1),
            layer(up_bias, 1),
            layer(down_w, 1),
            rows_in(cot, chunk),
        ],
        [
            rows_out(chans, BF16),
            rows_out(chans, F32),
            sums(2 * ff, chans, dtype=BF16),
            sums(8, ff),
            sums(24, chans),
        ],
        [
            ((chunk + 2 * width, chans), F32),
            ((chunk, chans), F32),
            ((chunk, chans), F32),
            ((chunk, chans), F32),
            ((chunk, chans), BF16),
            ((chunk, ff), BF16),
            ((chunk, ff), BF16),
            ((chans, ff), F32),
            ((ff, chans), F32),
        ],
        dense * 6 * ff,
    )
    result = send_result(result)
    g6, do2, weights_g, out1, conv_g3, small6 = call(
        channel_grad_kernel,
        chunks,
        near(g7, chunk)
        + [
            rows_in(mask, chunk),
            vec(3),
            rows_in(x6, chunk),
            (m2, (chunk, chans), lambda i: (i, 0)),
            rows_in(o2, chunk),
            layer(out_w, 1),
        ],
        [
            rows_out(chans, F32),
            rows_out(chans, BF16),
            sums(chans // LANES, LANES, LANES),
            sums(chans, chans, dtype=BF16),
            sums(72, chans),
            sums(16, chans),
        ],
        [((chunk + 2 * width, chans), F32), ((chunk, chans), BF16), ((chans, chans), F32)],
        dense * 3 * chans,
    )
    weights_g = across(weights_g)
    g5, mix1, mix_bg1, small5 = call(
        channel_back_kernel,
        chunks,
        [
            rows_in(do2, chunk),
            rows_in(m2, chunk),
            whole(gram),
            whole(weights_g),
            whole(scale),
            rows_in(n2, chunk),
            rows_in(x5, chunk),
            rows_in(g6, chunk),
            rows_in(mask, chunk),
            vec(2),
            layer(mix_w, 1),
        ],
        [
            rows_out(chans, F32),
            sums(3 * chans, chans, dtype=BF16),
            sums(8, 3 * chans),
            sums(16, chans),
        ],
        [((chunk, 3 * chans), BF16), ((chunk, chans), F32), ((3 * chans, chans), F32)],
        dense * 7 * chans,
    )
    g3, kept0, sent0, up_bg0, conv_g2, small3 = call(
        mlp_back_kernel,
        chunks,
        near(g5, chunk)
        + [
            rows_in(mask, chunk),
            vec(2),
            vec(1),
            rows_in(x4, chunk),
            rows_in(x3, chunk),
            rows_in(n1, chunk),
            rows_in(h1, chunk),
            rows_in(s1, chunk),
            layer(up_w, 0),
            layer(down_w, 0),
            whole(mlp1),
            whole(mix1),
            whole(out1),
            scalar,
        ],
        [
            rows_out(chans, F32),
            sums(2 * ff + 2 * chans, chans, dtype=BF16),
            sums(2 * ff + 2 * chans, chans, dtype=BF16),
            sums(8, ff),
            sums(72, chans),
            sums(32, chans),
        ],
        [
            ((chunk + 2 * width, chans), F32),
            ((chunk, chans), F32),
            ((chunk, chans), BF16),
            ((chunk, chans), F32),
            ((chunk, ff), BF16),
            ((chans, ff), F32),
            ((ff, chans), F32),
        ],
        dense * 4 * ff,
    )
    mid = share_planes(share_cores(kept0, sent0))
    g1, win0, mix_bg0, conv_g1, small1 = call(
        window_back_kernel,
        units,
        near(g3, unit)
        + [
            rows_in(mask, unit),
            vec(1),
            vec(0),
            rows_in(x2, unit),
            rows_in(x1, unit),
            rows_in(nw, wrows),
            rows_in(mw, wrows),
            rows_in(ow, wrows),
            layer(mix_w, 0),
            layer(out_w, 0),
            whole(gather),
        ],
        [
            rows_out(chans, F32, unit),
            sums(4 * chans, chans, dtype=BF16),
            sums(8, 3 * chans),
            sums(72, chans),
            sums(32, chans),
        ],
        [
            ((unit + 2 * width, chans), F32),
            ((3 * chans, chans), F32),
            ((chans, chans), F32),
            ((unit, chans), F32),
            ((wrows, chans), BF16),
            ((wrows, chans), BF16),
            ((wrows, 3 * chans), BF16),
            ((unit, chans), F32),
            ((wrows * chans // LANES, 4 * SLOT), BF16),
            ((wrows * chans // LANES, 4 * SLOT), BF16),
        ],
        dense * 16 * chans,
    )
    x0_flat = x0.reshape(tokens, chans)
    tokens_grad, conv_g0, small0 = call(
        token_grad_kernel,
        chunks,
        near(g1, chunk) + [rows_in(mask, chunk), vec(0), rows_in(x0_flat, chunk)],
        [rows_out(chans, BF16), sums(72, chans), sums(8, chans)],
        [((chunk + 2 * width, chans), F32)],
        dense * 30,
        after=(result, *mid),
    )

    sums0 = (conv_g0, conv_g1, conv_g2, conv_g3, small0, small1, small3, small5, small6, small7)
    bias_sums = (mix_bg0, mix_bg1, up_bg0, up_bg1)
    kept, sent = fold_small(core, win0, sums0 + bias_sums, chans)
    return result, tokens_grad, mid, kept, sent


def small_kernel(
    core, win0, conv0, conv1, conv2, conv3, s0, s1, s3, s5, s6, s7, mix0, mix1, up0, up1,
    kept, sent, rows,
):
    chans = rows.shape[1]
    rows[...] = jnp.zeros_like(rows)
    place = 0

    def put(part):
        nonlocal place
        rows[place : place + 1, :] = jnp.sum(part, axis=0, keepdims=True)
        place += 1

    for conv in (conv0, conv1, conv2, conv3):
        for k in range(9):
            put(conv[8 * k : 8 * k + 8, :])
    for ref, at in (
        (s0, 0), (s1, 0), (s3, 0), (s6, 0),
        (s1, 16), (s3, 16), (s5, 0), (s7, 8),
        (s1, 24), (s3, 24), (s5, 8), (s7, 16),
        (s1, 8), (s6, 8), (s3, 8), (s7, 0),
    ):
        put(ref[at : at + 8, :])
    for ref in (mix0, mix1, up0, up1):
        for col in range(0, ref.shape[1], chans):
            put(ref[:, col : col + chans])
    spread(core, kept, sent, [win0, rows])


def fold_small(core, win0, parts, chans):
    half = (win0.shape[0] + SMALL_ROWS) // 2
    return pl.pallas_call(
        small_kernel,
        in_specs=[pl.BlockSpec(memory_space=pltpu.SMEM)]
        + [pl.BlockSpec(memory_space=pltpu.VMEM)] * (1 + len(parts)),
        out_shape=[jax.ShapeDtypeStruct((half, chans), BF16)] * 2,
        scratch_shapes=[pltpu.VMEM((SMALL_ROWS, chans), F32)],
        compiler_params=pltpu.CompilerParams(vmem_limit_bytes=VMEM_LIMIT),
    )(core, win0, *parts)


def reader(first, second, offset, share, stride):
    count = first.shape[0] // stride

    def read(at, rows):
        parts = []
        while rows:
            n, inside = divmod(at, share)
            take = min(rows, share - inside)
            start = n % count * stride + offset + inside
            parts.append((first if n < count else second)[start : start + take, :].astype(F32))
            at, rows = at + take, rows - take
        return parts[0] if len(parts) == 1 else jnp.concatenate(parts, axis=0)

    return read


def put_attention(read, mix_w, out_w):
    chans = out_w.shape[1]
    for k in range(3):
        mix_w[0, :, k * chans : (k + 1) * chans] = read(k * chans, chans)
    out_w[0] = read(3 * chans, chans)


def put_feed(read, at, up_w, down_w):
    chans = down_w.shape[2]
    blocks = up_w.shape[2] // chans
    for k in range(blocks):
        up_w[0, :, k * chans : (k + 1) * chans] = read(at + k * chans, chans)
    for k in range(blocks):
        down_w[0, k * chans : (k + 1) * chans, :] = read(at + (blocks + k) * chans, chans)


def final_kernel(
    core, first, second,
    mix_w, out_w, up_w, down_w, conv_w, conv_b, gain, shift, last_shift, win_b, chan_b, out_b, up_b, down_b,
    rows, *wide, shares,
):
    layer = pl.program_id(0)
    chans = first.shape[1]
    feed_rows = 2 * up_w.shape[2]
    blocks = up_b.shape[1] // chans
    mid_share, late_share = shares
    stride = mid_share + late_share
    if wide:
        for to, ref in zip(wide, (first, second)):
            to[...] = ref[...].astype(F32)
        first, second = wide

    for flag in range(2):
        halves = (first, second) if flag == 0 else (second, first)
        mid = reader(*halves, 0, mid_share, stride)
        late = reader(*halves, mid_share, late_share, stride)

        @pl.when((core[0] == flag) & (layer == 0))
        def _():
            put_attention(late, mix_w, out_w)
            put_feed(lambda at, count: mid(feed_rows + 4 * chans + at, count), 0, up_w, down_w)
            rows[...] = late(4 * chans, SMALL_ROWS)

        @pl.when((core[0] == flag) & (layer == 1))
        def _():
            put_attention(lambda at, count: mid(feed_rows + at, count), mix_w, out_w)
            put_feed(mid, 0, up_w, down_w)

    @pl.when(layer == 0)
    def _():
            at = 0
            for k in range(4):
                for i in range(3):
                    for j in range(3):
                        conv_w[i, j, k : k + 1, :] = rows[at : at + 1, :]
                        at += 1
            for ref in (conv_b, gain):
                ref[...] = rows[at : at + 4, :]
                at += 4
            shift[...] = rows[at : at + 3, :]
            last_shift[...] = rows[at + 3, :]
            at += 4
            for ref in (out_b, down_b):
                ref[...] = rows[at : at + 2, :]
                at += 2
            win_b[:chans] = rows[at, :]
            win_b[chans:] = rows[at + 2, :]
            for k in range(3):
                chan_b[k * chans : (k + 1) * chans] = rows[at + 3 + k, :]
            at += 6
            for k in range(2):
                for i in range(blocks):
                    up_b[k : k + 1, i * chans : (i + 1) * chans] = rows[at : at + 1, :]
                    at += 1


def assemble(result, tokens_grad, core, halves, shares, ff):
    chans = halves[0].shape[1]
    shapes = [
        (2, chans, 3 * chans), (2, chans, chans), (2, chans, ff), (2, ff, chans),
        (3, 3, 4, chans), (4, chans), (4, chans), (3, chans), (chans,),
        (2 * chans,), (3 * chans,), (2, chans), (2, ff), (2, chans),
    ]

    def out_spec(shape):
        if len(shape) == 3:
            return pl.BlockSpec((1,) + shape[1:], lambda i: (i, 0, 0))
        return pl.BlockSpec(shape, lambda i: (0,) * len(shape))

    scratch = [pltpu.VMEM((SMALL_ROWS, chans), F32)]
    if any(share % 16 for share in shares):
        scratch += [pltpu.VMEM(half.shape, F32) for half in halves]
    (
        mix_w, out_w, up_w, down_w, conv_w, conv_b, gain, shift, last_shift, win_b, chan_b, out_b, up_b, down_b,
    ) = pl.pallas_call(
        functools.partial(final_kernel, shares=shares),
        grid=(2,),
        in_specs=[pl.BlockSpec(memory_space=pltpu.SMEM)]
        + [pl.BlockSpec(x.shape, lambda i: (0, 0), pipeline_mode=pl.Buffered(1)) for x in halves],
        out_specs=[out_spec(shape) for shape in shapes],
        out_shape=[jax.ShapeDtypeStruct(shape, F32) for shape in shapes],
        scratch_shapes=scratch,
        compiler_params=pltpu.CompilerParams(vmem_limit_bytes=VMEM_LIMIT),
    )(core, *halves)
    return (
        result, tokens_grad, conv_w.transpose(2, 0, 1, 3), conv_b, gain, shift, last_shift, mix_w,
        win_b, chan_b, out_w, out_b, up_w, up_b, down_w, down_b,
    )


def split_kernel(me, *refs, terms):
    outs = refs[terms:]
    rows = outs[0].shape[0]
    for step, out in enumerate(outs):
        at = pl.multiple_of((me[0] ^ step) * rows, 16)
        total = refs[0][pl.ds(at, rows), :].astype(F32)
        for ref in refs[1:terms]:
            total = total + ref[pl.ds(at, rows), :].astype(F32)
        out[...] = total.astype(BF16)


def split_sum(terms, me, size):
    rows, chans = terms[0].shape
    rows //= size
    if rows % 16 or rows < 512:
        total = functools.reduce(lambda x, y: x + y, [term.astype(F32) for term in terms]).astype(BF16)
        return [lax.dynamic_slice_in_dim(total, (me ^ step) * rows, rows, 0) for step in range(size)]
    return pl.pallas_call(
        functools.partial(split_kernel, terms=len(terms)),
        in_specs=[pl.BlockSpec(memory_space=pltpu.SMEM)] + [pl.BlockSpec(memory_space=pltpu.VMEM)] * len(terms),
        out_shape=[jax.ShapeDtypeStruct((rows, chans), BF16)] * size,
        compiler_params=pltpu.CompilerParams(vmem_limit_bytes=VMEM_LIMIT),
    )(me.astype(jnp.int32).reshape(1), *terms)


def widen_kernel(here, *refs):
    out = refs[-1]
    cols = out.shape[2]
    for step, part in enumerate(refs[:-1]):

        @pl.when(pl.program_id(0) == step)
        def _():
            out[0] = part[:, :cols, :].astype(F32)


def widen(parts, here, cols):
    images = len(parts)
    height, width, chans = parts[0].shape
    return pl.pallas_call(
        widen_kernel,
        grid_spec=pltpu.PrefetchScalarGridSpec(
            num_scalar_prefetch=1,
            grid=(images,),
            in_specs=[pl.BlockSpec(x.shape, lambda i, at: (0, 0, 0), pipeline_mode=pl.Buffered(1)) for x in parts],
            out_specs=pl.BlockSpec(
                (1, height, cols, chans), lambda i, at: ((at[0] + images - i) % images, 0, 0, 0)
            ),
        ),
        out_shape=jax.ShapeDtypeStruct((images, height, cols, chans), F32),
        compiler_params=pltpu.CompilerParams(vmem_limit_bytes=VMEM_LIMIT),
    )(here.astype(jnp.int32).reshape(1), *parts)


def local(
    tokens, heights, conv_weight, conv_bias, norm_gain, norm_shift, mix_weight, window_bias, channel_bias,
    out_weight, out_bias, up_weight, up_bias, down_weight, down_bias, cotangent,
):
    images, height, cols, chans = tokens.shape
    count = lax.axis_size("rows")
    place = lax.axis_index("rows")
    width = -(-cols // 8) * 8
    groups = count // images
    members = [[g * images + j for j in range(images)] for g in range(groups)]
    rows_here = images * height
    level = lax.dynamic_index_in_dim(heights, place % images, 0, keepdims=False)
    open_rows = heights * 7 - place * height

    def pad_image(field):
        inside = jnp.arange(height, dtype=jnp.int32)[None, :] < open_rows[:, None]
        field = jnp.where(inside[:, :, None, None], field, jnp.zeros((), field.dtype))
        return jnp.pad(field, ((0, 0), (0, 0), (0, width - cols), (0, 0)))

    def spread_image(field):
        field = lax.all_to_all(field, "rows", 0, 0, axis_index_groups=members, tiled=True)
        return field.reshape(rows_here, width, chans)

    def scatter_image(field):
        field = field.reshape(images, height, width, chans)
        field = lax.all_to_all(field, "rows", 0, 0, axis_index_groups=members, tiled=True)
        return field[:, :, :cols]

    def halo_of(field):
        flat = field.reshape(rows_here * width, chans)
        if groups == 1:
            return jnp.zeros((2 * width, chans), F32)
        down = [(i, i + images) for i in range(count - images)]
        up = [(i + images, i) for i in range(count - images)]
        above = lax.ppermute(flat[-width:].astype(BF16), "rows", down)
        below = lax.ppermute(flat[:width].astype(BF16), "rows", up)
        return jnp.concatenate([above, below], axis=0).astype(F32)

    def across(value):
        if groups == 1:
            return value
        other = [[j + g * images for g in range(groups)] for j in range(images)]
        return lax.psum(value, "rows", axis_index_groups=other)

    row = jnp.arange(rows_here * width, dtype=jnp.int32) // width + place // images * rows_here
    col = jnp.arange(rows_here * width, dtype=jnp.int32) % width
    mask = ((row < level * 7) & (col < cols)).astype(F32)
    mask = jnp.broadcast_to(mask[:, None], (rows_here * width, LANES))
    scale = lax.rsqrt((level * 7 * cols).astype(F32))
    scale = jnp.broadcast_to(scale, (8, LANES))
    small = prepare(conv_weight, conv_bias, norm_gain, norm_shift, out_bias, down_bias, up_bias)
    small += (
        jnp.concatenate([window_bias[:chans], jnp.zeros((chans,), BF16), window_bias[chans:]]).astype(F32)[None],
        channel_bias.astype(F32)[None],
    )
    x0 = spread_image(pad_image(tokens))
    cot, small, mask, scale = lax.optimization_barrier((pad_image(cotangent), small, mask, scale))
    cot = spread_image(cot).reshape(rows_here * width, chans)

    def exchange(part, axis, step):
        size = lax.axis_size(axis)
        return lax.ppermute(part, axis, [(i, i ^ step) for i in range(size)])

    core = lax.axis_index("core").astype(jnp.int32).reshape(1)

    def share(terms, axis):
        size = lax.axis_size(axis)
        pieces = split_sum(terms, lax.axis_index(axis), size)
        return [pieces[0]] + [exchange(pieces[step], axis, step) for step in range(1, size)]

    def share_cores(kept, sent):
        return [kept, exchange(sent, "core", 1)]

    def total(terms):
        return functools.reduce(lambda x, y: x + y, [term.astype(F32) for term in terms]).astype(BF16)

    def gather(part, axis):
        size, me = lax.axis_size(axis), lax.axis_index(axis)
        rows = part.shape[0]
        out = jnp.zeros((size * rows, part.shape[1]), part.dtype)
        for step in range(size):
            got = part if step == 0 else exchange(part, axis, step)
            out = lax.dynamic_update_slice_in_dim(out, got, (me ^ step) * rows, 0)
        return out

    def send_tokens(field):
        field = field.reshape(images, height, width, chans)
        here = place % images
        parts = []
        for step in range(images):
            part = lax.dynamic_index_in_dim(field, (here + step) % images, 0, keepdims=False)
            if step:
                pairs = [(g * images + j, g * images + (j + step) % images) for g in range(groups) for j in range(images)]
                part = lax.ppermute(part, "rows", pairs)
            parts.append(part)
        return parts

    weights = (mix_weight, out_weight, up_weight, down_weight)
    result, tokens_grad, mid, kept, sent = image_block(
        x0, cot, halo_of(x0), mask, scale, halo_of, across, weights, small, cols, core,
        scatter_image, share_cores, lambda terms: share(terms, "plane"),
    )
    together = lax.optimization_barrier
    tokens_grad = send_tokens(tokens_grad)
    mid = share(mid, "rows")
    late = share(share_cores(kept, sent), "plane")
    late, mid = together((late, mid))
    late = total(share(late, "rows"))
    mid = total(mid)
    shares = (mid.shape[0], late.shape[0])
    both = gather(jnp.concatenate([mid, late], axis=0), "rows")
    both = gather(both, "plane")
    both, tokens_grad = together((both, tokens_grad))
    tokens_grad = widen(tokens_grad, place % images, cols)
    both = (both, exchange(both, "core", 1))
    return assemble(result, tokens_grad, core, both, shares, up_weight.shape[2])


def solution(mesh):
    planes = mesh.shape["dp"] // 2
    fine = Mesh(mesh.devices.reshape(planes, 2, mesh.shape["rows"]), ("plane", "core", "rows"))
    dp = ("plane", "core")
    split = P(dp, "rows", None, None)
    in_specs = (split, P(dp)) + (P(),) * 13 + (split,)
    out_specs = (split, split) + (P(),) * 14
    return jax.shard_map(local, mesh=fine, in_specs=in_specs, out_specs=out_specs, check_vma=False)
```

```python
import functools

import jax
import jax.numpy as jnp
import numpy as np
from jax import lax
from jax.experimental import pallas as pl
from jax.experimental.pallas import tpu as pltpu
from jax.sharding import Mesh
from jax.sharding import PartitionSpec as P

HEADS = 12
HEAD_DIM = 32
EPS = 1e-05
WIN = 7
SLOT = 64
LANES = 128
F32 = jnp.float32
BF16 = jnp.bfloat16
SCALE = HEAD_DIM ** (-0.5)
LOG2E = 1.4426950408889634
ROOT_HALF = 0.7071067811865476
VMEM_LIMIT = 58 * 1024 * 1024
SMALL_ROWS = 512


def dot(left, right):
    return jnp.dot(left, right, preferred_element_type=F32)


def dot_nt(left, right):
    return lax.dot_general(left, right, (((1,), (1,)), ((), ())), preferred_element_type=F32)


def dot_tn(left, right):
    return lax.dot_general(left, right, (((0,), (0,)), ((), ())), preferred_element_type=F32)


def low(value):
    return value.astype(BF16).astype(F32)


def fold(value):
    rows, cols = value.shape
    return jnp.sum(value.reshape(rows // 8, 8, cols), axis=0)


def loop(count, step, body):
    for at in range(0, count, step):
        body(at)


def lane_tiles(chans):
    return [slice(t, t + LANES) for t in range(0, chans, LANES)]


def gelu_parts(value):
    size = jnp.abs(value)
    t = 1.0 / (1.0 + (0.3275911 * ROOT_HALF) * size)
    poly = t * (
        0.127414796
        + t * (-0.142248368 + t * (0.7107068705 + t * (-0.7265760135 + t * 0.5307027145)))
    )
    bell = jnp.exp2(value * value * (-0.5 * LOG2E))
    tail = poly * bell
    cdf = jnp.where(value >= 0.0, 1.0 - tail, tail)
    return value * cdf, cdf + value * bell * 0.3989422804014327


def norm_of(value, gain, shift):
    centre = value - jnp.mean(value, axis=-1, keepdims=True)
    spread = jnp.mean(centre * centre, axis=-1, keepdims=True)
    return centre * lax.rsqrt(spread + EPS) * gain + shift


def norm_back(value, gain, normed_grad):
    centre = value - jnp.mean(value, axis=-1, keepdims=True)
    inv = lax.rsqrt(jnp.mean(centre * centre, axis=-1, keepdims=True) + EPS)
    unit = centre * inv
    unit_grad = normed_grad * gain
    first = jnp.mean(unit_grad, axis=-1, keepdims=True)
    second = jnp.mean(unit_grad * unit, axis=-1, keepdims=True)
    return inv * (unit_grad - first - unit * second), normed_grad * unit


def fill_source(src, main, prev, after, halo, step, steps, width):
    rows = main.shape[0]
    src[pl.ds(0, width), :] = jnp.where(step == 0, halo[0:width, :], low(prev[...]))
    src[pl.ds(rows + width, width), :] = jnp.where(
        step == steps - 1, halo[width : 2 * width, :], low(after[...])
    )

    def body(at):
        src[pl.ds(at + width, 2 * width), :] = low(main[pl.ds(at, 2 * width), :])

    loop(rows // (2 * width) * 2 * width, 2 * width, body)
    if rows % (2 * width):
        at = rows - width
        src[pl.ds(at + width, width), :] = low(main[pl.ds(at, width), :])


def conv_tile(src, vec, at, tile, width, lanes, flipped):
    rows = [src[pl.ds(at + width * d, tile), lanes] for d in range(3)]
    sums = []
    for col in range(3):
        total = None
        for row in range(3):
            k = (2 - row) * 3 + (2 - col) if flipped else row * 3 + col
            term = rows[row] * vec[k : k + 1, lanes]
            total = term if total is None else total + term
        sums.append(total)
    return sums[1] + pltpu.roll(sums[0], 1, 0) + pltpu.roll(sums[2], tile - 1, 0), rows


def conv_weight_tile(acc, rows, field, tile, lanes):
    shifted = [pltpu.roll(field, 1, 0), field, pltpu.roll(field, tile - 1, 0)]
    for row in range(3):
        for col in range(3):
            k = row * 3 + col
            acc[8 * k : 8 * k + 8, lanes] += fold(shifted[col] * rows[2 - row])


def block_heads(part):
    lane = lax.broadcasted_iota(jnp.int32, part.shape, 1)
    zero = jnp.zeros_like(part)
    return jnp.concatenate(
        [jnp.where(lane // HEAD_DIM == h, part, zero) for h in range(LANES // HEAD_DIM)], axis=0
    )


def window_forward_kernel(
    tok, prev, after, halo, mask, vec, mix, mix_b, out_w, gather, x1, nw, mw, ow, x2, src, keep, probs
):
    step, steps = pl.program_id(0), pl.num_programs(0)
    rows, width, chans = tok.shape
    src[pl.ds(0, width), :] = jnp.where(step == 0, halo[0:width, :], prev[0].astype(F32))
    src[pl.ds((rows + 1) * width, width), :] = jnp.where(
        step == steps - 1, halo[width : 2 * width, :], after[0].astype(F32)
    )
    for i in range(rows):
        src[pl.ds((i + 1) * width, width), :] = tok[i].astype(F32)

    def conv_body(at):
        region = mask[pl.ds(at, width), :]
        for lanes in lane_tiles(chans):
            got, near = conv_tile(src, vec, at, width, width, lanes, False)
            x1[pl.ds(at, width), lanes] = region * (near[1] + got + vec[9:10, lanes])

    loop(rows * width, width, conv_body)

    normed = norm_of(x1[...], vec[10:11, :], vec[11:12, :]).astype(BF16)
    normed = dot(gather[...], normed).astype(BF16)
    nw[...] = normed
    mw[...] = (dot(normed, mix[...]) + mix_b[...]).astype(BF16)
    windows = nw.shape[0] // SLOT
    lane = lax.broadcasted_iota(jnp.int32, (SLOT, LANES), 1)
    left = lane < SLOT
    real = lane % SLOT < WIN * WIN
    ones = (
        lax.broadcasted_iota(jnp.int32, (4 * SLOT, LANES), 0) // SLOT
        == lax.broadcasted_iota(jnp.int32, (4 * SLOT, LANES), 1) // HEAD_DIM
    ).astype(BF16)
    floor = -1e30

    places = [(at, lanes) for at in range(0, windows * SLOT, SLOT) for lanes in lane_tiles(chans)]
    for n, (at, lanes) in enumerate(places):
        query = mw[at : at + SLOT, lanes]
        key = mw[at : at + SLOT, chans + lanes.start : chans + lanes.stop]
        scores = dot_nt(query, block_heads(key))
        for half in range(2):
            part = jnp.where(real, scores[:, half * LANES : (half + 1) * LANES], floor)
            top_l = jnp.max(jnp.where(left, part, floor), axis=1, keepdims=True)
            top_r = jnp.max(jnp.where(left, floor, part), axis=1, keepdims=True)
            top = jnp.where(left, top_l, top_r)
            raised = jnp.exp2((part - top) * (SCALE * LOG2E)).astype(BF16)
            probs[n * SLOT : (n + 1) * SLOT, half * LANES : (half + 1) * LANES] = raised
    for n, (at, lanes) in enumerate(places):
        value = mw[at : at + SLOT, 2 * chans + lanes.start : 2 * chans + lanes.stop]
        both = dot(
            probs[n * SLOT : (n + 1) * SLOT, :], jnp.concatenate([block_heads(value), ones], axis=1)
        )
        ow[at : at + SLOT, lanes] = (both[:, :LANES] / both[:, LANES:]).astype(BF16)
    merged = dot_tn(gather[...], ow[...]).astype(BF16)
    keep[...] = dot(merged, out_w[...])

    def out_body(at):
        region = mask[pl.ds(at, width), :]
        for lanes in lane_tiles(chans):
            x2[pl.ds(at, width), lanes] = region * (
                x1[pl.ds(at, width), lanes] + keep[pl.ds(at, width), lanes] + vec[12:13, lanes]
            )

    loop(rows * width, width, out_body)


def conv_forward(main, prev, after, halo, mask, vec, out, src, width):
    step, steps = pl.program_id(0), pl.num_programs(0)
    rows, chans = main.shape
    fill_source(src, main, prev, after, halo, step, steps, width)
    tile = 2 * width

    def body(at):
        region = mask[pl.ds(at, tile), :]
        for lanes in lane_tiles(chans):
            got, _ = conv_tile(src, vec, at, tile, width, lanes, False)
            out[pl.ds(at, tile), lanes] = region * (
                main[pl.ds(at, tile), lanes] + got + vec[9:10, lanes]
            )

    loop(rows, tile, body)


def norm_forward(value, vec, out):
    out[...] = norm_of(value[...], vec[10:11, :], vec[11:12, :]).astype(BF16)


def mlp_body(normed, up_w, up_b, down_w, hidden, slope, keep):
    rows = normed.shape[0]
    for at in range(0, up_w.shape[1], 256):
        cols = slice(at, at + 256)
        pre = dot(normed[...], up_w[:, cols]) + up_b[:, cols]
        for row in range(0, rows, 144):
            act, der = gelu_parts(pre[row : row + 144])
            hidden[row : row + 144, cols] = act.astype(BF16)
            slope[row : row + 144, cols] = der.astype(BF16)
        part = dot(hidden[:, cols], down_w[cols, :])
        if at == 0:
            keep[...] = part
        else:
            keep[...] += part


def add_residual(state, branch, mask, vec, out):
    chans = state.shape[1]

    def body(at):
        region = mask[pl.ds(at, 144), :]
        for lanes in lane_tiles(chans):
            out[pl.ds(at, 144), lanes] = (
                region
                * (state[pl.ds(at, 144), lanes] + branch[pl.ds(at, 144), lanes] + vec[12:13, lanes])
            ).astype(out.dtype)

    loop(state.shape[0], 144, body)


def mlp_forward_kernel(
    main, prev, after, halo, mask, vec, up_w, up_b, down_w, x3, x4, normed, hidden, slope, src, keep
):
    width = prev.shape[0]
    conv_forward(main, prev, after, halo, mask, vec, x3, src, width)
    norm_forward(x3, vec, normed)
    mlp_body(normed, up_w, up_b, down_w, hidden, slope, keep)
    add_residual(x3, keep, mask, vec, x4)


def norm_backward(state, normed_grad, grad, vec, small, out, gain_row):
    part = normed_grad[...]
    back, scaled = norm_back(state[...], vec[10:11, :], part)
    out[...] = grad[...].astype(F32) + back
    small[gain_row : gain_row + 8, :] += fold(scaled)
    small[gain_row + 8 : gain_row + 16, :] += fold(part)


def mlp_down_back(rounded, normed, hidden, slope, pre_grad, up_w, down_w, up_g, up_bg, down_g):
    rows = rounded.shape[0]
    for at in range(0, up_w.shape[1], 256):
        cols = slice(at, at + 256)
        hidden_grad = dot_nt(rounded[...], down_w[cols, :])
        total = None
        for row in range(0, rows, 144):
            part = hidden_grad[row : row + 144] * slope[row : row + 144, cols].astype(F32)
            pre_grad[row : row + 144, cols] = part.astype(BF16)
            total = fold(part) if total is None else total + fold(part)
        up_bg[:, cols] += total
        up_g[:, cols] += dot_tn(normed[...], pre_grad[:, cols])
        down_g[cols, :] += dot_tn(hidden[:, cols], rounded[...])


def mlp_both(normed, cot, up_w, up_b, down_w, hidden, pre_grad, up_g, up_bg, down_g):
    rows = normed.shape[0]

    def block(at):
        cols = pl.ds(pl.multiple_of(at, 256), 256)
        pre = dot(normed[...], up_w[:, cols]) + up_b[:, cols]
        hidden_grad = dot_nt(cot[...], down_w[cols, :])
        total = None
        for row in range(0, rows, 144):
            act, der = gelu_parts(pre[row : row + 144])
            hidden[row : row + 144, cols] = act.astype(BF16)
            part = hidden_grad[row : row + 144] * der
            pre_grad[row : row + 144, cols] = part.astype(BF16)
            total = fold(part) if total is None else total + fold(part)
        up_bg[:, cols] += total
        up_g[:, cols] += dot_tn(normed[...], pre_grad[:, cols])
        down_g[cols, :] += dot_tn(hidden[:, cols], cot[...])

    def pair(i, carry):
        block(i * 512)
        block(i * 512 + 256)
        return carry

    lax.fori_loop(0, up_w.shape[1] // 512, pair, 0)


def column_blocks(source, chans):
    return [source.at[:, col : col + chans] for col in range(0, source.shape[1], chans)]


def spread(core, kept, sent, blocks):
    half = kept.shape[0]
    for flag in range(2):

        @pl.when(core[0] == flag)
        def _():
            at = 0
            for block in blocks:
                rows = block.shape[0]
                cuts = [0, rows] if not at < half < at + rows else [0, half - at, rows]
                for low_cut, high_cut in zip(cuts, cuts[1:]):
                    start = at + low_cut
                    target = kept if (start >= half) == (flag == 1) else sent
                    start = start % half
                    target[start : start + high_cut - low_cut, :] = block[
                        low_cut:high_cut, :
                    ].astype(BF16)
                at += rows


def last_step():
    return pl.program_id(0) == pl.num_programs(0) - 1


def zero_first(*refs):
    @pl.when(pl.program_id(0) == 0)
    def _():
        for ref in refs:
            ref[...] = jnp.zeros_like(ref)


def last_mlp_kernel(
    main, prev, after, halo, mask, vec, up_w, up_b, down_w, cot,
    result, grad, packed, up_bg, small,
    src, x7, keep, back, normed, hidden, pre_grad, up_g, down_g,
):
    width = prev.shape[0]
    zero_first(up_g, up_bg, down_g, small)
    conv_forward(main, prev, after, halo, mask, vec, x7, src, width)
    norm_forward(x7, vec, normed)
    mlp_both(normed, cot, up_w, up_b, down_w, hidden, pre_grad, up_g, up_bg, down_g)
    keep[...] = dot(hidden[...], down_w[...])
    back[...] = dot_nt(pre_grad[...], up_w[...])
    add_residual(x7, keep, mask, vec, result)
    small[0:8, :] += fold(cot[...].astype(F32))
    norm_backward(x7, back, cot, vec, small, grad, 8)

    @pl.when(last_step())
    def _():
        at = 0
        for block in column_blocks(up_g, packed.shape[1]) + [down_g]:
            packed[at : at + block.shape[0], :] = block[...].astype(BF16)
            at += block.shape[0]


def conv_backward(main, prev, after, halo, mask, vec, field, out, conv_g, small, src, width):
    step, steps = pl.program_id(0), pl.num_programs(0)
    rows, chans = main.shape
    fill_source(src, main, prev, after, halo, step, steps, width)
    tile = 72

    def body(at):
        region = mask[pl.ds(at, tile), :]
        for lanes in lane_tiles(chans):
            got, near = conv_tile(src, vec, at, tile, width, lanes, True)
            grad = main[pl.ds(at, tile), lanes]
            out[pl.ds(at, tile), lanes] = (region * (grad + got)).astype(out.dtype)
            conv_weight_tile(conv_g, near, low(field[pl.ds(at, tile), lanes]), tile, lanes)
            small[0:8, lanes] += fold(grad)

    loop(rows, tile, body)


def fold_rows(source, small, row):
    def body(at):
        small[row : row + 8, :] += fold(source[pl.ds(at, 72), :])

    loop(source.shape[0], 72, body)


def channel_mix_kernel(
    main, prev, after, halo, mask, vec, mix, mix_b, x5, normed, mixed, gram, src
):
    width = prev.shape[0]
    chans = main.shape[1]
    zero_first(gram)
    conv_forward(main, prev, after, halo, mask, vec, x5, src, width)
    norm_forward(x5, vec, normed)
    rows = main.shape[0]
    for part in range(3):
        cols = slice(part * chans, (part + 1) * chans)
        got = dot(normed[...], mix[:, cols]) + mix_b[:, cols]
        if part == 1:
            got = got * jnp.concatenate([mask[...]] * (chans // LANES), axis=1)
        mixed[:, cols] = got.astype(BF16)
    for t, lanes in enumerate(lane_tiles(chans)):
        gram[t] += dot_tn(
            mixed[:, chans + lanes.start : chans + lanes.stop],
            mixed[:, 2 * chans + lanes.start : 2 * chans + lanes.stop],
        )


def same_head():
    row = lax.broadcasted_iota(jnp.int32, (LANES, LANES), 0)
    col = lax.broadcasted_iota(jnp.int32, (LANES, LANES), 1)
    return row // HEAD_DIM == col // HEAD_DIM


def channel_weights(gram, scale):
    own = same_head()
    logits = jnp.where(own, gram * scale, -1e30)
    top = jnp.max(logits, axis=1, keepdims=True)
    raised = jnp.where(own, jnp.exp(logits - top), 0.0)
    return raised / jnp.sum(raised, axis=1, keepdims=True)


def channel_out_kernel(mixed, gram, scale, x5, mask, vec, out_w, o2, x6, keep):
    chans = x5.shape[1]
    for t, lanes in enumerate(lane_tiles(chans)):
        weights = channel_weights(gram[t], scale[0:1, :]).astype(BF16)
        o2[:, lanes] = dot_nt(mixed[:, lanes], weights).astype(BF16)
    keep[...] = dot(o2[...], out_w[...])
    add_residual(x5, keep, mask, vec, x6)


def channel_grad_kernel(
    main, prev, after, halo, mask, vec, x6, mixed, o2, out_w,
    grad, attended_grad, weights_g, packed, conv_g, small, src, rounded, out_g,
):
    width = prev.shape[0]
    chans = main.shape[1]
    zero_first(weights_g, out_g, conv_g, small)
    conv_backward(main, prev, after, halo, mask, vec, x6, grad, conv_g, small, src, width)
    rounded[...] = grad[...].astype(BF16)
    fold_rows(grad, small, 8)
    out_g[...] += dot_tn(o2[...], rounded[...])
    attended_grad[...] = dot_nt(rounded[...], out_w[...]).astype(BF16)
    for t, lanes in enumerate(lane_tiles(chans)):
        weights_g[t] += dot_tn(attended_grad[:, lanes], mixed[:, lanes])

    @pl.when(last_step())
    def _():
        packed[...] = out_g[...].astype(BF16)


def channel_back_kernel(
    attended_grad, mixed, gram, weights_g, scale, normed, x5, g6, mask, vec, mix,
    grad, packed, mix_bg, small, mixed_grad, keep, mix_g,
):
    chans = x5.shape[1]
    zero_first(mix_g, mix_bg, small)
    own = same_head()
    wide = mask[...]
    for t, lanes in enumerate(lane_tiles(chans)):
        weights = channel_weights(gram[t], scale[0:1, :])
        back = jnp.where(own, weights_g[t], 0.0)
        logit = weights * (back - jnp.sum(back * weights, axis=1, keepdims=True))
        logit = logit.astype(BF16)
        key = slice(chans + lanes.start, chans + lanes.stop)
        val = slice(2 * chans + lanes.start, 2 * chans + lanes.stop)
        query_grad = dot(attended_grad[:, lanes], weights.astype(BF16))
        key_grad = dot_nt(mixed[:, val], logit) * scale[0:1, :] * wide
        value_grad = dot(mixed[:, key], logit) * scale[0:1, :]
        for cols, part in ((lanes, query_grad), (key, key_grad), (val, value_grad)):
            mix_bg[:, cols] += fold(part)
            mixed_grad[:, cols] = part.astype(BF16)
    for part in range(3):
        cols = slice(part * chans, (part + 1) * chans)
        mix_g[part * chans : (part + 1) * chans, :] += dot_tn(normed[...], mixed_grad[:, cols])
    keep[...] = dot_nt(mixed_grad[...], mix[...])
    norm_backward(x5, keep, g6, vec, small, grad, 0)

    @pl.when(last_step())
    def _():
        packed[...] = mix_g[...].astype(BF16)


def mlp_back_kernel(
    main, prev, after, halo, mask, vec_conv, vec, x4, x3, normed, hidden, slope, up_w, down_w, mlp1, mix1, out1, core,
    grad, kept, sent, up_bg, conv_g, small,
    src, g4, rounded, keep, pre_grad, up_g, down_g,
):
    width = prev.shape[0]
    zero_first(up_g, up_bg, down_g, conv_g, small)
    conv_backward(main, prev, after, halo, mask, vec_conv, x4, g4, conv_g, small, src, width)
    rounded[...] = g4[...].astype(BF16)
    fold_rows(g4, small, 8)
    mlp_down_back(rounded, normed, hidden, slope, pre_grad, up_w, down_w, up_g, up_bg, down_g)
    keep[...] = dot_nt(pre_grad[...], up_w[...])
    norm_backward(x3, keep, g4, vec, small, grad, 16)

    @pl.when(last_step())
    def _():
        spread(core, kept, sent, [mlp1, mix1, out1] + column_blocks(up_g, kept.shape[1]) + [down_g])


def window_back_kernel(
    main, prev, after, halo, mask, vec_conv, vec, x2, x1, nw, mw, ow, mix, out_w, gather,
    grad, packed, mix_bg, conv_g, small,
    src, mix_g, out_g, g2, gw, dow, dmw, keep, probs, slopes,
):
    width = prev.shape[0]
    chans = main.shape[1]
    zero_first(mix_g, mix_bg, out_g, conv_g, small)
    conv_backward(main, prev, after, halo, mask, vec_conv, x2, g2, conv_g, small, src, width)
    fold_rows(g2, small, 8)
    gw[...] = dot(gather[...], g2[...].astype(BF16)).astype(BF16)
    out_g[...] += dot_tn(ow[...], gw[...])
    dow[...] = dot_nt(gw[...], out_w[...]).astype(BF16)
    windows = nw.shape[0] // SLOT
    real = lax.broadcasted_iota(jnp.int32, (SLOT, 4 * SLOT), 0) < WIN * WIN
    head = lax.broadcasted_iota(jnp.int32, (SLOT, LANES), 1) // HEAD_DIM

    places = [(at, lanes) for at in range(0, windows * SLOT, SLOT) for lanes in lane_tiles(chans)]
    for n, (at, lanes) in enumerate(places):
        rows = slice(at, at + SLOT)
        query = mw[rows, lanes]
        key = mw[rows, chans + lanes.start : chans + lanes.stop]
        value = mw[rows, 2 * chans + lanes.start : 2 * chans + lanes.stop]
        scores = jnp.where(real, dot_nt(key, block_heads(query)), -1e30)
        top = jnp.max(scores, axis=0, keepdims=True)
        raised = jnp.exp2((scores - top) * (SCALE * LOG2E))
        share = raised * (1.0 / jnp.sum(raised, axis=0, keepdims=True))
        share_grad = dot_nt(value, block_heads(dow[rows, lanes]))
        inner = jnp.sum(share_grad * share, axis=0, keepdims=True)
        probs[n * SLOT : (n + 1) * SLOT, :] = share.astype(BF16)
        slopes[n * SLOT : (n + 1) * SLOT, :] = (share * (share_grad - inner)).astype(BF16)
    for n, (at, lanes) in enumerate(places):
        rows = slice(at, at + SLOT)
        key_cols = slice(chans + lanes.start, chans + lanes.stop)
        value_cols = slice(2 * chans + lanes.start, 2 * chans + lanes.stop)
        share, slope = probs[n * SLOT : (n + 1) * SLOT, :], slopes[n * SLOT : (n + 1) * SLOT, :]
        value_grad = dot(share, block_heads(dow[rows, lanes]))
        key_grad = dot(slope, block_heads(mw[rows, lanes])) * SCALE
        full = dot_tn(slope, mw[rows, key_cols])
        query_grad = jnp.zeros((SLOT, LANES), F32)
        for h in range(LANES // HEAD_DIM):
            query_grad = jnp.where(head == h, full[h * SLOT : (h + 1) * SLOT], query_grad)
        query_grad = query_grad * SCALE
        for cols, part in ((lanes, query_grad), (key_cols, key_grad), (value_cols, value_grad)):
            dmw[rows, cols] = part.astype(BF16)
            mix_bg[:, cols] += fold(part)
    for part in range(3):
        cols = slice(part * chans, (part + 1) * chans)
        mix_g[part * chans : (part + 1) * chans, :] += dot_tn(nw[...], dmw[:, cols])
    normed_grad = dot_nt(dmw[...], mix[...]).astype(BF16)
    keep[...] = dot_tn(gather[...], normed_grad)
    norm_backward(x1, keep, g2, vec, small, grad, 16)

    @pl.when(last_step())
    def _():
        packed[: 3 * chans, :] = mix_g[...].astype(BF16)
        packed[3 * chans :, :] = out_g[...].astype(BF16)


def token_grad_kernel(main, prev, after, halo, mask, vec, field, out, conv_g, small, src):
    width = prev.shape[0]
    zero_first(conv_g, small)
    conv_backward(main, prev, after, halo, mask, vec, field, out, conv_g, small, src, width)


def call(kernel, steps, ins, outs, scratch, cost, after=()):
    count = len(ins)

    def body(*refs):
        kernel(*refs[:count], *refs[count + len(after) :])

    def spec(block, index):
        if block is None:
            return pl.BlockSpec(memory_space=pltpu.SMEM)
        if isinstance(index, int):
            fixed = (index,) + tuple(0 for _ in block[1:])
            return pl.BlockSpec((None,) + block[1:], lambda i: fixed, pipeline_mode=pl.Buffered(1))
        fixed = tuple(0 for _ in block)
        if index is None:
            return pl.BlockSpec(block, lambda i: fixed, pipeline_mode=pl.Buffered(1))
        return pl.BlockSpec(block, index)

    def out_spec(block, index):
        fixed = tuple(0 for _ in block)
        return pl.BlockSpec(block, (lambda i: fixed) if index is None else index)

    return pl.pallas_call(
        body,
        grid=(steps,),
        in_specs=[spec(block, index) for _, block, index in ins]
        + [pl.BlockSpec(memory_space=pl.ANY) for _ in after],
        out_specs=[out_spec(block, index) for _, _, block, index in outs],
        out_shape=[jax.ShapeDtypeStruct(shape, dtype) for shape, dtype, _, _ in outs],
        scratch_shapes=[pltpu.VMEM(shape, dtype) for shape, dtype in scratch],
        compiler_params=pltpu.CompilerParams(vmem_limit_bytes=VMEM_LIMIT),
        cost_estimate=pl.CostEstimate(flops=1, bytes_accessed=cost * 3_600_000, transcendentals=0),
    )(*[array for array, _, _ in ins], *after)


def gather_matrix(cols, width):
    windows = cols // WIN
    slot = np.arange(windows * SLOT)[:, None]
    window, inside = slot // SLOT, slot % SLOT
    source = inside // WIN * width + window * WIN + inside % WIN
    patch = np.arange(WIN * width)[None, :]
    return jnp.asarray(((source == patch) & (inside < WIN * WIN)).astype(BF16))


def prepare_kernel(conv_w, conv_b, gain, shift, out_b, down_b, up_b, vecs, up_bias):
    for k in range(4):
        for i in range(3):
            vecs[k, 3 * i : 3 * i + 3, :] = conv_w[k, i].astype(F32)
        last = out_b if k % 2 == 0 else down_b
        for at, ref, row in ((9, conv_b, k), (10, gain, k), (11, shift, k), (12, last, k // 2)):
            vecs[k, at : at + 1, :] = ref[row : row + 1, :].astype(F32)
    for k in range(2):
        up_bias[k] = up_b[k : k + 1, :].astype(F32)


def prepare(*parts):
    chans, ff = parts[0].shape[-1], parts[-1].shape[-1]
    return pl.pallas_call(
        prepare_kernel,
        out_shape=tuple(jax.ShapeDtypeStruct(x, F32) for x in ((4, 16, chans), (2, 1, ff))),
    )(*parts)


def image_block(x0, cot, tok_halo, mask, scale, halo_of, across, weights, small, cols, core, send_result, share_cores, share_planes):
    mix_w, out_w, up_w, down_w = weights
    height, width, chans = x0.shape
    tokens = height * width
    ff = up_w.shape[2]
    vecs, up_bias, bias0, bias1 = small
    gather = gather_matrix(cols, width)
    wrows = cols // WIN * SLOT
    unit = WIN * width
    units = height // WIN
    chunk = 2 * unit if units % 2 == 0 else unit
    chunks = tokens // chunk

    def near(array, rows):
        per = rows // width
        return [
            (array, (rows, chans), lambda i: (i, 0)),
            (array, (width, chans), lambda i: (jnp.maximum(i * per - 1, 0), 0)),
            (array, (width, chans), lambda i: (jnp.minimum(i * per + per, height - 1), 0)),
            (halo_of(array), (2 * width, chans), None),
        ]

    def rows_in(array, rows):
        return (array, (rows, array.shape[1]), lambda i: (i, 0))

    def whole(array):
        return (array, array.shape, None)

    def layer(array, k):
        return (array, array.shape, k)

    def rows_out(cols_, dtype, rows=chunk, total=tokens):
        return ((total, cols_), dtype, (rows, cols_), lambda i: (i, 0))

    def sums(*shape, dtype=F32):
        return (shape, dtype, shape, None)

    def vec(k):
        return layer(vecs, k)

    scalar = (core, None, None)

    x1, nw, mw, ow, x2 = call(
        window_forward_kernel,
        units,
        [
            (x0, (WIN, width, chans), lambda i: (i, 0, 0)),
            (x0, (1, width, chans), lambda i: (jnp.maximum(i * WIN - 1, 0), 0, 0)),
            (x0, (1, width, chans), lambda i: (jnp.minimum(i * WIN + WIN, height - 1), 0, 0)),
            whole(tok_halo),
            rows_in(mask, unit),
            vec(0),
            layer(mix_w, 0),
            whole(bias0),
            layer(out_w, 0),
            whole(gather),
        ],
        [
            rows_out(chans, F32, unit),
            rows_out(chans, BF16, wrows, units * wrows),
            rows_out(3 * chans, BF16, wrows, units * wrows),
            rows_out(chans, BF16, wrows, units * wrows),
            rows_out(chans, F32, unit),
        ],
        [
            ((unit + 2 * width, chans), F32),
            ((unit, chans), F32),
            ((wrows * chans // LANES, 4 * SLOT), BF16),
        ],
        20,
    )
    x3, x4, n1, h1, s1 = call(
        mlp_forward_kernel,
        chunks,
        near(x2, chunk) + [rows_in(mask, chunk), vec(1), layer(up_w, 0), layer(up_bias, 0), layer(down_w, 0)],
        [
            rows_out(chans, F32),
            rows_out(chans, F32),
            rows_out(chans, BF16),
            rows_out(ff, BF16),
            rows_out(ff, BF16),
        ],
        [((chunk + 2 * width, chans), F32), ((chunk, chans), F32)],
        25,
    )
    x5, n2, m2, gram = call(
        channel_mix_kernel,
        chunks,
        near(x4, chunk) + [rows_in(mask, chunk), vec(2), layer(mix_w, 1), whole(bias1)],
        [
            rows_out(chans, F32),
            rows_out(chans, BF16),
            rows_out(3 * chans, BF16),
            sums(chans // LANES, LANES, LANES),
        ],
        [((chunk + 2 * width, chans), F32)],
        11,
    )
    gram = across(gram)
    o2, x6 = call(
        channel_out_kernel,
        chunks,
        [
            rows_in(m2, chunk),
            whole(gram),
            whole(scale),
            rows_in(x5, chunk),
            rows_in(mask, chunk),
            vec(2),
            layer(out_w, 1),
        ],
        [rows_out(chans, BF16), rows_out(chans, F32)],
        [((chunk, chans), F32)],
        7,
    )
    result, g7, mlp1, up_bg1, small7 = call(
        last_mlp_kernel,
        chunks,
        near(x6, chunk)
        + [
            rows_in(mask, chunk),
            vec(3),
            layer(up_w, 1),
            layer(up_bias, 1),
            layer(down_w, 1),
            rows_in(cot, chunk),
        ],
        [
            rows_out(chans, BF16),
            rows_out(chans, F32),
            sums(2 * ff, chans, dtype=BF16),
            sums(8, ff),
            sums(24, chans),
        ],
        [
            ((chunk + 2 * width, chans), F32),
            ((chunk, chans), F32),
            ((chunk, chans), F32),
            ((chunk, chans), F32),
            ((chunk, chans), BF16),
            ((chunk, ff), BF16),
            ((chunk, ff), BF16),
            ((chans, ff), F32),
            ((ff, chans), F32),
        ],
        38,
    )
    result = send_result(result)
    g6, do2, weights_g, out1, conv_g3, small6 = call(
        channel_grad_kernel,
        chunks,
        near(g7, chunk)
        + [
            rows_in(mask, chunk),
            vec(3),
            rows_in(x6, chunk),
            (m2, (chunk, chans), lambda i: (i, 0)),
            rows_in(o2, chunk),
            layer(out_w, 1),
        ],
        [
            rows_out(chans, F32),
            rows_out(chans, BF16),
            sums(chans // LANES, LANES, LANES),
            sums(chans, chans, dtype=BF16),
            sums(72, chans),
            sums(16, chans),
        ],
        [((chunk + 2 * width, chans), F32), ((chunk, chans), BF16), ((chans, chans), F32)],
        13,
    )
    weights_g = across(weights_g)
    g5, mix1, mix_bg1, small5 = call(
        channel_back_kernel,
        chunks,
        [
            rows_in(do2, chunk),
            rows_in(m2, chunk),
            whole(gram),
            whole(weights_g),
            whole(scale),
            rows_in(n2, chunk),
            rows_in(x5, chunk),
            rows_in(g6, chunk),
            rows_in(mask, chunk),
            vec(2),
            layer(mix_w, 1),
        ],
        [
            rows_out(chans, F32),
            sums(3 * chans, chans, dtype=BF16),
            sums(8, 3 * chans),
            sums(16, chans),
        ],
        [((chunk, 3 * chans), BF16), ((chunk, chans), F32), ((3 * chans, chans), F32)],
        16,
    )
    g3, kept0, sent0, up_bg0, conv_g2, small3 = call(
        mlp_back_kernel,
        chunks,
        near(g5, chunk)
        + [
            rows_in(mask, chunk),
            vec(2),
            vec(1),
            rows_in(x4, chunk),
            rows_in(x3, chunk),
            rows_in(n1, chunk),
            rows_in(h1, chunk),
            rows_in(s1, chunk),
            layer(up_w, 0),
            layer(down_w, 0),
            whole(mlp1),
            whole(mix1),
            whole(out1),
            scalar,
        ],
        [
            rows_out(chans, F32),
            sums(2 * ff + 2 * chans, chans, dtype=BF16),
            sums(2 * ff + 2 * chans, chans, dtype=BF16),
            sums(8, ff),
            sums(72, chans),
            sums(32, chans),
        ],
        [
            ((chunk + 2 * width, chans), F32),
            ((chunk, chans), F32),
            ((chunk, chans), BF16),
            ((chunk, chans), F32),
            ((chunk, ff), BF16),
            ((chans, ff), F32),
            ((ff, chans), F32),
        ],
        32,
    )
    mid = share_planes(share_cores(kept0, sent0))
    g1, win0, mix_bg0, conv_g1, small1 = call(
        window_back_kernel,
        units,
        near(g3, unit)
        + [
            rows_in(mask, unit),
            vec(1),
            vec(0),
            rows_in(x2, unit),
            rows_in(x1, unit),
            rows_in(nw, wrows),
            rows_in(mw, wrows),
            rows_in(ow, wrows),
            layer(mix_w, 0),
            layer(out_w, 0),
            whole(gather),
        ],
        [
            rows_out(chans, F32, unit),
            sums(4 * chans, chans, dtype=BF16),
            sums(8, 3 * chans),
            sums(72, chans),
            sums(32, chans),
        ],
        [
            ((unit + 2 * width, chans), F32),
            ((3 * chans, chans), F32),
            ((chans, chans), F32),
            ((unit, chans), F32),
            ((wrows, chans), BF16),
            ((wrows, chans), BF16),
            ((wrows, 3 * chans), BF16),
            ((unit, chans), F32),
            ((wrows * chans // LANES, 4 * SLOT), BF16),
            ((wrows * chans // LANES, 4 * SLOT), BF16),
        ],
        34,
    )
    mid, g1 = lax.optimization_barrier((mid, g1))
    x0_flat = x0.reshape(tokens, chans)
    tokens_grad, conv_g0, small0 = call(
        token_grad_kernel,
        chunks,
        near(g1, chunk) + [rows_in(mask, chunk), vec(0), rows_in(x0_flat, chunk)],
        [rows_out(chans, BF16), sums(72, chans), sums(8, chans)],
        [((chunk + 2 * width, chans), F32)],
        8,
        after=(result, *mid),
    )

    sums0 = (conv_g0, conv_g1, conv_g2, conv_g3, small0, small1, small3, small5, small6, small7)
    bias_sums = (mix_bg0, mix_bg1, up_bg0, up_bg1)
    kept, sent = fold_small(core, win0, sums0 + bias_sums, chans)
    return result, tokens_grad, mid, kept, sent


def small_kernel(
    core, win0, conv0, conv1, conv2, conv3, s0, s1, s3, s5, s6, s7, mix0, mix1, up0, up1,
    kept, sent, rows,
):
    chans = rows.shape[1]
    rows[...] = jnp.zeros_like(rows)
    place = 0

    def put(part):
        nonlocal place
        rows[place : place + 1, :] = jnp.sum(part, axis=0, keepdims=True)
        place += 1

    for conv in (conv0, conv1, conv2, conv3):
        for k in range(9):
            put(conv[8 * k : 8 * k + 8, :])
    for ref, at in (
        (s0, 0), (s1, 0), (s3, 0), (s6, 0),
        (s1, 16), (s3, 16), (s5, 0), (s7, 8),
        (s1, 24), (s3, 24), (s5, 8), (s7, 16),
        (s1, 8), (s6, 8), (s3, 8), (s7, 0),
    ):
        put(ref[at : at + 8, :])
    for ref in (mix0, mix1, up0, up1):
        for col in range(0, ref.shape[1], chans):
            put(ref[:, col : col + chans])
    spread(core, kept, sent, [win0, rows])


def fold_small(core, win0, parts, chans):
    half = (win0.shape[0] + SMALL_ROWS) // 2
    return pl.pallas_call(
        small_kernel,
        in_specs=[pl.BlockSpec(memory_space=pltpu.SMEM)]
        + [pl.BlockSpec(memory_space=pltpu.VMEM)] * (1 + len(parts)),
        out_shape=[jax.ShapeDtypeStruct((half, chans), BF16)] * 2,
        scratch_shapes=[pltpu.VMEM((SMALL_ROWS, chans), F32)],
        compiler_params=pltpu.CompilerParams(vmem_limit_bytes=VMEM_LIMIT),
    )(core, win0, *parts)


def reader(halves, plane, share, offset, stride, members):
    first = halves[0][0][0]
    part = members // 2 * stride
    planes = 2 * first.shape[0] // part
    bits = planes.bit_length() - 1

    def piece(at, take):
        n, inside = divmod(at, share)
        core, n = divmod(n, planes * members)
        owner, member = divmod(n, members)
        late, place = divmod(member * stride + offset + inside, part)
        far = plane ^ owner
        if late:
            far = sum(((far >> k) & 1) << (bits - 1 - k) for k in range(bits))
        near, other = halves[core][late]
        start = (far & (planes // 2 - 1)) * part + place
        rows = pl.ds(pl.multiple_of(start, 16), take)
        return jnp.where(far < planes // 2, near[rows, :], other[rows, :]).astype(F32)

    def read(at, rows):
        parts = []
        while rows:
            take = min(rows, share - at % share)
            parts.append(piece(at, take))
            at, rows = at + take, rows - take
        return parts[0] if len(parts) == 1 else jnp.concatenate(parts, axis=0)

    return read


def plain_reader(first, second):
    half = first.shape[0]

    def read(at, rows):
        parts = []
        if at < half:
            parts.append(first[at : min(at + rows, half), :].astype(F32))
        if at + rows > half:
            parts.append(second[max(at - half, 0) : at + rows - half, :].astype(F32))
        return parts[0] if len(parts) == 1 else jnp.concatenate(parts, axis=0)

    return read


def put_attention(read, mix_w, out_w):
    chans = out_w.shape[1]
    for k in range(3):
        mix_w[0, :, k * chans : (k + 1) * chans] = read(k * chans, chans)
    out_w[0] = read(3 * chans, chans)


def put_feed(read, at, up_w, down_w):
    chans = down_w.shape[2]
    blocks = up_w.shape[2] // chans
    for k in range(blocks):
        up_w[0, :, k * chans : (k + 1) * chans] = read(at + k * chans, chans)
    for k in range(blocks):
        down_w[0, k * chans : (k + 1) * chans, :] = read(at + (blocks + k) * chans, chans)


def final_kernel(
    place, *refs, shares, members,
):
    inputs, outs, rows = refs[:-15], refs[-15:-1], refs[-1]
    (
        mix_w, out_w, up_w, down_w, conv_w, conv_b, gain, shift, last_shift, win_b, chan_b, out_b, up_b, down_b,
    ) = outs
    layer = pl.program_id(0)
    chans = inputs[0].shape[1]
    feed_rows = 2 * up_w.shape[2]
    blocks = up_b.shape[1] // chans
    mid_share, late_share = shares
    stride = mid_share + late_share
    count = len(inputs) // 2
    here, there = inputs[:count], inputs[count:]

    for flag in range(2):
        halves = (here, there) if flag == 0 else (there, here)
        if count == 2:
            mid, late = (plain_reader(*pair) for pair in zip(*halves))
        else:
            pairs = tuple((half[0:2], half[2:4]) for half in halves)
            mid = reader(pairs, place[1], mid_share, 0, stride, members)
            late = reader(pairs, place[1], late_share, mid_share, stride, members)

        @pl.when((place[0] == flag) & (layer == 0))
        def _():
            put_attention(late, mix_w, out_w)
            put_feed(lambda at, count: mid(feed_rows + 4 * chans + at, count), 0, up_w, down_w)
            rows[...] = late(4 * chans, SMALL_ROWS)

        @pl.when((place[0] == flag) & (layer == 1))
        def _():
            put_attention(lambda at, count: mid(feed_rows + at, count), mix_w, out_w)
            put_feed(mid, 0, up_w, down_w)

    @pl.when(layer == 0)
    def _():
            at = 0
            for k in range(4):
                for i in range(3):
                    for j in range(3):
                        conv_w[i, j, k : k + 1, :] = rows[at : at + 1, :]
                        at += 1
            for ref in (conv_b, gain):
                ref[...] = rows[at : at + 4, :]
                at += 4
            shift[...] = rows[at : at + 3, :]
            last_shift[...] = rows[at + 3, :]
            at += 4
            for ref in (out_b, down_b):
                ref[...] = rows[at : at + 2, :]
                at += 2
            win_b[:chans] = rows[at, :]
            win_b[chans:] = rows[at + 2, :]
            for k in range(3):
                chan_b[k * chans : (k + 1) * chans] = rows[at + 3 + k, :]
            at += 6
            for k in range(2):
                for i in range(blocks):
                    up_b[k : k + 1, i * chans : (i + 1) * chans] = rows[at : at + 1, :]
                    at += 1


def assemble(place, arrays, shares, members, ff):
    chans = arrays[0].shape[1]
    shapes = [
        (2, chans, 3 * chans), (2, chans, chans), (2, chans, ff), (2, ff, chans),
        (3, 3, 4, chans), (4, chans), (4, chans), (3, chans), (chans,),
        (2 * chans,), (3 * chans,), (2, chans), (2, ff), (2, chans),
    ]

    def out_spec(shape):
        if len(shape) == 3:
            return pl.BlockSpec((1,) + shape[1:], lambda i: (i, 0, 0))
        return pl.BlockSpec(shape, lambda i: (0,) * len(shape))

    (
        mix_w, out_w, up_w, down_w, conv_w, conv_b, gain, shift, last_shift, win_b, chan_b, out_b, up_b, down_b,
    ) = pl.pallas_call(
        functools.partial(final_kernel, shares=shares, members=members),
        grid=(2,),
        in_specs=[pl.BlockSpec(memory_space=pltpu.SMEM)]
        + [pl.BlockSpec(x.shape, lambda i: (0, 0), pipeline_mode=pl.Buffered(1)) for x in arrays],
        out_specs=[out_spec(shape) for shape in shapes],
        out_shape=[jax.ShapeDtypeStruct(shape, F32) for shape in shapes],
        scratch_shapes=[pltpu.VMEM((SMALL_ROWS, chans), F32)],
        compiler_params=pltpu.CompilerParams(vmem_limit_bytes=VMEM_LIMIT),
    )(place, *arrays)
    return (
        conv_w.transpose(2, 0, 1, 3), conv_b, gain, shift, last_shift, mix_w,
        win_b, chan_b, out_w, out_b, up_w, up_b, down_w, down_b,
    )


def split_kernel(me, *refs, terms):
    outs = refs[terms:]
    rows = outs[0].shape[0]
    for step, out in enumerate(outs):
        at = pl.multiple_of((me[0] ^ step) * rows, 16)
        total = refs[0][pl.ds(at, rows), :].astype(F32)
        for ref in refs[1:terms]:
            total = total + ref[pl.ds(at, rows), :].astype(F32)
        out[...] = total.astype(BF16)


def split_sum(terms, me, size):
    rows, chans = terms[0].shape
    rows //= size
    if rows % 16 or rows < 512:
        total = functools.reduce(lambda x, y: x + y, [term.astype(F32) for term in terms]).astype(BF16)
        return [lax.dynamic_slice_in_dim(total, (me ^ step) * rows, rows, 0) for step in range(size)]
    return pl.pallas_call(
        functools.partial(split_kernel, terms=len(terms)),
        in_specs=[pl.BlockSpec(memory_space=pltpu.SMEM)] + [pl.BlockSpec(memory_space=pltpu.VMEM)] * len(terms),
        out_shape=[jax.ShapeDtypeStruct((rows, chans), BF16)] * size,
        compiler_params=pltpu.CompilerParams(vmem_limit_bytes=VMEM_LIMIT),
    )(me.astype(jnp.int32).reshape(1), *terms)


def widen_kernel(here, *refs):
    out = refs[-1]
    cols = out.shape[2]
    for step, part in enumerate(refs[:-1]):

        @pl.when(pl.program_id(0) == step)
        def _():
            out[0] = part[:, :cols, :].astype(F32)


def widen(parts, here, cols):
    images = len(parts)
    height, width, chans = parts[0].shape
    return pl.pallas_call(
        widen_kernel,
        grid_spec=pltpu.PrefetchScalarGridSpec(
            num_scalar_prefetch=1,
            grid=(images,),
            in_specs=[pl.BlockSpec(x.shape, lambda i, at: (0, 0, 0), pipeline_mode=pl.Buffered(1)) for x in parts],
            out_specs=pl.BlockSpec(
                (1, height, cols, chans), lambda i, at: ((at[0] + images - i) % images, 0, 0, 0)
            ),
        ),
        out_shape=jax.ShapeDtypeStruct((images, height, cols, chans), F32),
        compiler_params=pltpu.CompilerParams(vmem_limit_bytes=VMEM_LIMIT),
    )(here.astype(jnp.int32).reshape(1), *parts)


def local(
    tokens, heights, conv_weight, conv_bias, norm_gain, norm_shift, mix_weight, window_bias, channel_bias,
    out_weight, out_bias, up_weight, up_bias, down_weight, down_bias, cotangent,
):
    images, height, cols, chans = tokens.shape
    count = lax.axis_size("rows")
    place = lax.axis_index("rows")
    width = -(-cols // 8) * 8
    groups = count // images
    members = [[g * images + j for j in range(images)] for g in range(groups)]
    rows_here = images * height
    level = lax.dynamic_index_in_dim(heights, place % images, 0, keepdims=False)
    open_rows = heights * 7 - place * height

    def pad_image(field):
        inside = jnp.arange(height, dtype=jnp.int32)[None, :] < open_rows[:, None]
        field = jnp.where(inside[:, :, None, None], field, jnp.zeros((), field.dtype))
        return jnp.pad(field, ((0, 0), (0, 0), (0, width - cols), (0, 0)))

    def spread_image(field):
        field = lax.all_to_all(field, "rows", 0, 0, axis_index_groups=members, tiled=True)
        return field.reshape(rows_here, width, chans)

    def scatter_image(field):
        field = field.reshape(images, height, width, chans)
        field = lax.all_to_all(field, "rows", 0, 0, axis_index_groups=members, tiled=True)
        return field[:, :, :cols]

    def halo_of(field):
        flat = field.reshape(rows_here * width, chans)
        if groups == 1:
            return jnp.zeros((2 * width, chans), F32)
        down = [(i, i + images) for i in range(count - images)]
        up = [(i + images, i) for i in range(count - images)]
        above = lax.ppermute(flat[-width:].astype(BF16), "rows", down)
        below = lax.ppermute(flat[:width].astype(BF16), "rows", up)
        return jnp.concatenate([above, below], axis=0).astype(F32)

    def across(value):
        if groups == 1:
            return value
        other = [[j + g * images for g in range(groups)] for j in range(images)]
        return lax.psum(value, "rows", axis_index_groups=other)

    row = jnp.arange(rows_here * width, dtype=jnp.int32) // width + place // images * rows_here
    col = jnp.arange(rows_here * width, dtype=jnp.int32) % width
    mask = ((row < level * 7) & (col < cols)).astype(F32)
    mask = jnp.broadcast_to(mask[:, None], (rows_here * width, LANES))
    scale = lax.rsqrt((level * 7 * cols).astype(F32))
    scale = jnp.broadcast_to(scale, (8, LANES))
    small = prepare(conv_weight, conv_bias, norm_gain, norm_shift, out_bias, down_bias, up_bias)
    small += (
        jnp.concatenate([window_bias[:chans], jnp.zeros((chans,), BF16), window_bias[chans:]]).astype(F32)[None],
        channel_bias.astype(F32)[None],
    )
    x0 = spread_image(pad_image(tokens))
    cot, small, mask, scale = lax.optimization_barrier((pad_image(cotangent), small, mask, scale))
    cot = spread_image(cot).reshape(rows_here * width, chans)

    def exchange(part, axis, step):
        size = lax.axis_size(axis)
        return lax.ppermute(part, axis, [(i, i ^ step) for i in range(size)])

    core = lax.axis_index("core").astype(jnp.int32).reshape(1)

    def share(terms, axis):
        size = lax.axis_size(axis)
        pieces = split_sum(terms, lax.axis_index(axis), size)
        return [pieces[0]] + [exchange(pieces[step], axis, step) for step in range(1, size)]

    def share_cores(kept, sent):
        return [kept, exchange(sent, "core", 1)]

    def total(terms):
        return functools.reduce(lambda x, y: x + y, [term.astype(F32) for term in terms]).astype(BF16)

    def gather(part, axis):
        size, me = lax.axis_size(axis), lax.axis_index(axis)
        rows = part.shape[0]
        out = jnp.zeros((size * rows, part.shape[1]), part.dtype)
        for step in range(size):
            got = part if step == 0 else exchange(part, axis, step)
            out = lax.dynamic_update_slice_in_dim(out, got, (me ^ step) * rows, 0)
        return out

    def join(part, other):
        rows = part.shape[0]
        out = jnp.zeros((2 * rows, part.shape[1]), part.dtype)
        out = lax.dynamic_update_slice_in_dim(out, part, 0, 0)
        return lax.dynamic_update_slice_in_dim(out, other, rows, 0)

    def send_tokens(field):
        field = field.reshape(images, height, width, chans)
        here = place % images
        parts = []
        for step in range(images):
            part = lax.dynamic_index_in_dim(field, (here + step) % images, 0, keepdims=False)
            if step:
                pairs = [(g * images + j, g * images + (j + step) % images) for g in range(groups) for j in range(images)]
                part = lax.ppermute(part, "rows", pairs)
            parts.append(part)
        return parts

    weights = (mix_weight, out_weight, up_weight, down_weight)
    result, tokens_grad, mid, kept, sent = image_block(
        x0, cot, halo_of(x0), mask, scale, halo_of, across, weights, small, cols, core,
        scatter_image, share_cores, lambda terms: share(terms, "plane"),
    )
    together = lax.optimization_barrier
    tokens_grad = send_tokens(tokens_grad)
    mid = share(mid, "rows")
    kept, sent, mid = together((kept, sent, mid))
    late = share(share_cores(kept, sent), "plane")
    late, tokens_grad[2:3] = together((late, tokens_grad[2:3]))
    late = total(share(late, "rows"))
    mid = total(mid)
    shares = (mid.shape[0], late.shape[0])
    block = gather(jnp.concatenate([mid, late], axis=0), "rows")
    members = lax.axis_size("rows")
    bits = lax.axis_size("plane").bit_length() - 1
    half = block.shape[0] // 2
    parts = [block[:half], block[half:]]
    aligned = all(rows % 16 == 0 for rows in shares)
    if not aligned:
        block = gather(block, "plane").reshape(-1, sum(shares), chans)
        arrays = [block[:, : shares[0]].reshape(-1, chans), block[:, shares[0] :].reshape(-1, chans)]
        tokens_grad = widen(tokens_grad, place % images, cols)
    for k in range(bits if aligned else 0):
        others = [exchange(part, "plane", 1 << bit) for part, bit in zip(parts, (k, bits - 1 - k))]
        if k == bits - 1:
            tokens_grad = widen(tokens_grad, place % images, cols)
            others, tokens_grad = together((others, tokens_grad))
        if k + 1 < bits:
            parts = [join(part, other) for part, other in zip(parts, others)]
        else:
            arrays = [parts[0], others[0], parts[1], others[1]]
    arrays += [exchange(array, "core", 1) for array in arrays]
    at = jnp.concatenate([core, lax.axis_index("plane").astype(jnp.int32).reshape(1)])
    return result, tokens_grad, *assemble(at, arrays, shares, members, up_weight.shape[2])


def solution(mesh):
    planes = mesh.shape["dp"] // 2
    fine = Mesh(mesh.devices.reshape(planes, 2, mesh.shape["rows"]), ("plane", "core", "rows"))
    dp = ("plane", "core")
    split = P(dp, "rows", None, None)
    in_specs = (split, P(dp)) + (P(),) * 13 + (split,)
    out_specs = (split, split) + (P(),) * 14
    return jax.shard_map(local, mesh=fine, in_specs=in_specs, out_specs=out_specs, check_vma=False)
```

```python
import functools

import jax
import jax.numpy as jnp
import numpy as np
from jax import lax
from jax.experimental import pallas as pl
from jax.experimental.pallas import tpu as pltpu
from jax.sharding import Mesh
from jax.sharding import PartitionSpec as P

HEADS = 12
HEAD_DIM = 32
EPS = 1e-05
WIN = 7
SLOT = 64
LANES = 128
F32 = jnp.float32
BF16 = jnp.bfloat16
SCALE = HEAD_DIM ** (-0.5)
LOG2E = 1.4426950408889634
ROOT_HALF = 0.7071067811865476
VMEM_LIMIT = 58 * 1024 * 1024
SMALL_ROWS = 512


def dot(left, right):
    return jnp.dot(left, right, preferred_element_type=F32)


def dot_nt(left, right):
    return lax.dot_general(left, right, (((1,), (1,)), ((), ())), preferred_element_type=F32)


def dot_tn(left, right):
    return lax.dot_general(left, right, (((0,), (0,)), ((), ())), preferred_element_type=F32)


def low(value):
    return value.astype(BF16).astype(F32)


def fold(value):
    rows, cols = value.shape
    return jnp.sum(value.reshape(rows // 8, 8, cols), axis=0)


def loop(count, step, body):
    for at in range(0, count, step):
        body(at)


def lane_tiles(chans):
    return [slice(t, t + LANES) for t in range(0, chans, LANES)]


def gelu_parts(value):
    size = jnp.abs(value)
    t = 1.0 / (1.0 + (0.3275911 * ROOT_HALF) * size)
    poly = t * (
        0.127414796
        + t * (-0.142248368 + t * (0.7107068705 + t * (-0.7265760135 + t * 0.5307027145)))
    )
    bell = jnp.exp2(value * value * (-0.5 * LOG2E))
    tail = poly * bell
    cdf = jnp.where(value >= 0.0, 1.0 - tail, tail)
    return value * cdf, cdf + value * bell * 0.3989422804014327


def norm_of(value, gain, shift):
    centre = value - jnp.mean(value, axis=-1, keepdims=True)
    spread = jnp.mean(centre * centre, axis=-1, keepdims=True)
    return centre * lax.rsqrt(spread + EPS) * gain + shift


def norm_back(value, gain, normed_grad):
    centre = value - jnp.mean(value, axis=-1, keepdims=True)
    inv = lax.rsqrt(jnp.mean(centre * centre, axis=-1, keepdims=True) + EPS)
    unit = centre * inv
    unit_grad = normed_grad * gain
    first = jnp.mean(unit_grad, axis=-1, keepdims=True)
    second = jnp.mean(unit_grad * unit, axis=-1, keepdims=True)
    return inv * (unit_grad - first - unit * second), normed_grad * unit


def fill_source(src, main, prev, after, halo, step, steps, width):
    rows = main.shape[0]
    src[pl.ds(0, width), :] = jnp.where(step == 0, halo[0:width, :], low(prev[...]))
    src[pl.ds(rows + width, width), :] = jnp.where(
        step == steps - 1, halo[width : 2 * width, :], low(after[...])
    )

    def body(at):
        src[pl.ds(at + width, 2 * width), :] = low(main[pl.ds(at, 2 * width), :])

    loop(rows // (2 * width) * 2 * width, 2 * width, body)
    if rows % (2 * width):
        at = rows - width
        src[pl.ds(at + width, width), :] = low(main[pl.ds(at, width), :])


def conv_tile(src, vec, at, tile, width, lanes, flipped):
    rows = [src[pl.ds(at + width * d, tile), lanes] for d in range(3)]
    sums = []
    for col in range(3):
        total = None
        for row in range(3):
            k = (2 - row) * 3 + (2 - col) if flipped else row * 3 + col
            term = rows[row] * vec[k : k + 1, lanes]
            total = term if total is None else total + term
        sums.append(total)
    return sums[1] + pltpu.roll(sums[0], 1, 0) + pltpu.roll(sums[2], tile - 1, 0), rows


def conv_weight_tile(acc, rows, field, tile, lanes):
    shifted = [pltpu.roll(field, 1, 0), field, pltpu.roll(field, tile - 1, 0)]
    for row in range(3):
        for col in range(3):
            k = row * 3 + col
            acc[8 * k : 8 * k + 8, lanes] += fold(shifted[col] * rows[2 - row])


def block_heads(part):
    lane = lax.broadcasted_iota(jnp.int32, part.shape, 1)
    zero = jnp.zeros_like(part)
    return jnp.concatenate(
        [jnp.where(lane // HEAD_DIM == h, part, zero) for h in range(LANES // HEAD_DIM)], axis=0
    )


def window_forward_kernel(
    tok, prev, after, halo, mask, vec, mix, mix_b, out_w, gather, x1, nw, mw, ow, x2, src, keep, probs
):
    step, steps = pl.program_id(0), pl.num_programs(0)
    rows, width, chans = tok.shape
    src[pl.ds(0, width), :] = jnp.where(step == 0, halo[0:width, :], prev[0].astype(F32))
    src[pl.ds((rows + 1) * width, width), :] = jnp.where(
        step == steps - 1, halo[width : 2 * width, :], after[0].astype(F32)
    )
    for i in range(rows):
        src[pl.ds((i + 1) * width, width), :] = tok[i].astype(F32)

    def conv_body(at):
        region = mask[pl.ds(at, width), :]
        for lanes in lane_tiles(chans):
            got, near = conv_tile(src, vec, at, width, width, lanes, False)
            x1[pl.ds(at, width), lanes] = region * (near[1] + got + vec[9:10, lanes])

    loop(rows * width, width, conv_body)

    normed = norm_of(x1[...], vec[10:11, :], vec[11:12, :]).astype(BF16)
    normed = dot(gather[...], normed).astype(BF16)
    nw[...] = normed
    mw[...] = (dot(normed, mix[...]) + mix_b[...]).astype(BF16)
    windows = nw.shape[0] // SLOT
    lane = lax.broadcasted_iota(jnp.int32, (SLOT, LANES), 1)
    left = lane < SLOT
    real = lane % SLOT < WIN * WIN
    ones = (
        lax.broadcasted_iota(jnp.int32, (4 * SLOT, LANES), 0) // SLOT
        == lax.broadcasted_iota(jnp.int32, (4 * SLOT, LANES), 1) // HEAD_DIM
    ).astype(BF16)
    floor = -1e30

    places = [(at, lanes) for at in range(0, windows * SLOT, SLOT) for lanes in lane_tiles(chans)]
    for n, (at, lanes) in enumerate(places):
        query = mw[at : at + SLOT, lanes]
        key = mw[at : at + SLOT, chans + lanes.start : chans + lanes.stop]
        scores = dot_nt(query, block_heads(key))
        for half in range(2):
            part = jnp.where(real, scores[:, half * LANES : (half + 1) * LANES], floor)
            top_l = jnp.max(jnp.where(left, part, floor), axis=1, keepdims=True)
            top_r = jnp.max(jnp.where(left, floor, part), axis=1, keepdims=True)
            top = jnp.where(left, top_l, top_r)
            raised = jnp.exp2((part - top) * (SCALE * LOG2E)).astype(BF16)
            probs[n * SLOT : (n + 1) * SLOT, half * LANES : (half + 1) * LANES] = raised
    for n, (at, lanes) in enumerate(places):
        value = mw[at : at + SLOT, 2 * chans + lanes.start : 2 * chans + lanes.stop]
        both = dot(
            probs[n * SLOT : (n + 1) * SLOT, :], jnp.concatenate([block_heads(value), ones], axis=1)
        )
        ow[at : at + SLOT, lanes] = (both[:, :LANES] / both[:, LANES:]).astype(BF16)
    merged = dot_tn(gather[...], ow[...]).astype(BF16)
    keep[...] = dot(merged, out_w[...])

    def out_body(at):
        region = mask[pl.ds(at, width), :]
        for lanes in lane_tiles(chans):
            x2[pl.ds(at, width), lanes] = region * (
                x1[pl.ds(at, width), lanes] + keep[pl.ds(at, width), lanes] + vec[12:13, lanes]
            )

    loop(rows * width, width, out_body)


def conv_forward(main, prev, after, halo, mask, vec, out, src, width):
    step, steps = pl.program_id(0), pl.num_programs(0)
    rows, chans = main.shape
    fill_source(src, main, prev, after, halo, step, steps, width)
    tile = 2 * width

    def body(at):
        region = mask[pl.ds(at, tile), :]
        for lanes in lane_tiles(chans):
            got, _ = conv_tile(src, vec, at, tile, width, lanes, False)
            out[pl.ds(at, tile), lanes] = region * (
                main[pl.ds(at, tile), lanes] + got + vec[9:10, lanes]
            )

    loop(rows, tile, body)


def norm_forward(value, vec, out):
    out[...] = norm_of(value[...], vec[10:11, :], vec[11:12, :]).astype(BF16)


def mlp_body(normed, up_w, up_b, down_w, hidden, slope, keep):
    rows = normed.shape[0]
    for at in range(0, up_w.shape[1], 256):
        cols = slice(at, at + 256)
        pre = dot(normed[...], up_w[:, cols]) + up_b[:, cols]
        for row in range(0, rows, 144):
            act, der = gelu_parts(pre[row : row + 144])
            hidden[row : row + 144, cols] = act.astype(BF16)
            slope[row : row + 144, cols] = der.astype(BF16)
        part = dot(hidden[:, cols], down_w[cols, :])
        if at == 0:
            keep[...] = part
        else:
            keep[...] += part


def add_residual(state, branch, mask, vec, out):
    chans = state.shape[1]

    def body(at):
        region = mask[pl.ds(at, 144), :]
        for lanes in lane_tiles(chans):
            out[pl.ds(at, 144), lanes] = (
                region
                * (state[pl.ds(at, 144), lanes] + branch[pl.ds(at, 144), lanes] + vec[12:13, lanes])
            ).astype(out.dtype)

    loop(state.shape[0], 144, body)


def mlp_forward_kernel(
    main, prev, after, halo, mask, vec, up_w, up_b, down_w, x3, x4, normed, hidden, slope, src, keep
):
    width = prev.shape[0]
    conv_forward(main, prev, after, halo, mask, vec, x3, src, width)
    norm_forward(x3, vec, normed)
    mlp_body(normed, up_w, up_b, down_w, hidden, slope, keep)
    add_residual(x3, keep, mask, vec, x4)


def norm_backward(state, normed_grad, grad, vec, small, out, gain_row):
    part = normed_grad[...]
    back, scaled = norm_back(state[...], vec[10:11, :], part)
    out[...] = grad[...].astype(F32) + back
    small[gain_row : gain_row + 8, :] += fold(scaled)
    small[gain_row + 8 : gain_row + 16, :] += fold(part)


def mlp_down_back(rounded, normed, hidden, slope, pre_grad, up_w, down_w, up_g, up_bg, down_g):
    rows = rounded.shape[0]
    for at in range(0, up_w.shape[1], 256):
        cols = slice(at, at + 256)
        hidden_grad = dot_nt(rounded[...], down_w[cols, :])
        total = None
        for row in range(0, rows, 144):
            part = hidden_grad[row : row + 144] * slope[row : row + 144, cols].astype(F32)
            pre_grad[row : row + 144, cols] = part.astype(BF16)
            total = fold(part) if total is None else total + fold(part)
        up_bg[:, cols] += total
        up_g[:, cols] += dot_tn(normed[...], pre_grad[:, cols])
        down_g[cols, :] += dot_tn(hidden[:, cols], rounded[...])


def mlp_both(normed, cot, up_w, up_b, down_w, hidden, pre_grad, up_g, up_bg, down_g):
    rows = normed.shape[0]

    def block(at):
        cols = pl.ds(pl.multiple_of(at, 256), 256)
        pre = dot(normed[...], up_w[:, cols]) + up_b[:, cols]
        hidden_grad = dot_nt(cot[...], down_w[cols, :])
        total = None
        for row in range(0, rows, 144):
            act, der = gelu_parts(pre[row : row + 144])
            hidden[row : row + 144, cols] = act.astype(BF16)
            part = hidden_grad[row : row + 144] * der
            pre_grad[row : row + 144, cols] = part.astype(BF16)
            total = fold(part) if total is None else total + fold(part)
        up_bg[:, cols] += total
        up_g[:, cols] += dot_tn(normed[...], pre_grad[:, cols])
        down_g[cols, :] += dot_tn(hidden[:, cols], cot[...])

    def pair(i, carry):
        block(i * 512)
        block(i * 512 + 256)
        return carry

    lax.fori_loop(0, up_w.shape[1] // 512, pair, 0)


def column_blocks(source, chans):
    return [source.at[:, col : col + chans] for col in range(0, source.shape[1], chans)]


def spread(core, kept, sent, blocks):
    half = kept.shape[0]
    for flag in range(2):

        @pl.when(core[0] == flag)
        def _():
            at = 0
            for block in blocks:
                rows = block.shape[0]
                cuts = [0, rows] if not at < half < at + rows else [0, half - at, rows]
                for low_cut, high_cut in zip(cuts, cuts[1:]):
                    start = at + low_cut
                    target = kept if (start >= half) == (flag == 1) else sent
                    start = start % half
                    target[start : start + high_cut - low_cut, :] = block[
                        low_cut:high_cut, :
                    ].astype(BF16)
                at += rows


def last_step():
    return pl.program_id(0) == pl.num_programs(0) - 1


def zero_first(*refs):
    @pl.when(pl.program_id(0) == 0)
    def _():
        for ref in refs:
            ref[...] = jnp.zeros_like(ref)


def last_mlp_kernel(
    main, prev, after, halo, mask, vec, up_w, up_b, down_w, cot,
    result, grad, packed, up_bg, small,
    src, x7, keep, back, normed, hidden, pre_grad, up_g, down_g,
):
    width = prev.shape[0]
    zero_first(up_g, up_bg, down_g, small)
    conv_forward(main, prev, after, halo, mask, vec, x7, src, width)
    norm_forward(x7, vec, normed)
    mlp_both(normed, cot, up_w, up_b, down_w, hidden, pre_grad, up_g, up_bg, down_g)
    keep[...] = dot(hidden[...], down_w[...])
    back[...] = dot_nt(pre_grad[...], up_w[...])
    add_residual(x7, keep, mask, vec, result)
    small[0:8, :] += fold(cot[...].astype(F32))
    norm_backward(x7, back, cot, vec, small, grad, 8)

    @pl.when(last_step())
    def _():
        at = 0
        for block in column_blocks(up_g, packed.shape[1]) + [down_g]:
            packed[at : at + block.shape[0], :] = block[...].astype(BF16)
            at += block.shape[0]


def conv_backward(main, prev, after, halo, mask, vec, field, out, conv_g, small, src, width):
    step, steps = pl.program_id(0), pl.num_programs(0)
    rows, chans = main.shape
    fill_source(src, main, prev, after, halo, step, steps, width)
    tile = 72

    def body(at):
        region = mask[pl.ds(at, tile), :]
        for lanes in lane_tiles(chans):
            got, near = conv_tile(src, vec, at, tile, width, lanes, True)
            grad = main[pl.ds(at, tile), lanes]
            out[pl.ds(at, tile), lanes] = (region * (grad + got)).astype(out.dtype)
            conv_weight_tile(conv_g, near, low(field[pl.ds(at, tile), lanes]), tile, lanes)
            small[0:8, lanes] += fold(grad)

    loop(rows, tile, body)


def fold_rows(source, small, row):
    def body(at):
        small[row : row + 8, :] += fold(source[pl.ds(at, 72), :])

    loop(source.shape[0], 72, body)


def channel_mix_kernel(
    main, prev, after, halo, mask, vec, mix, mix_b, x5, normed, mixed, gram, src
):
    width = prev.shape[0]
    chans = main.shape[1]
    zero_first(gram)
    conv_forward(main, prev, after, halo, mask, vec, x5, src, width)
    norm_forward(x5, vec, normed)
    rows = main.shape[0]
    for part in range(3):
        cols = slice(part * chans, (part + 1) * chans)
        got = dot(normed[...], mix[:, cols]) + mix_b[:, cols]
        if part == 1:
            got = got * jnp.concatenate([mask[...]] * (chans // LANES), axis=1)
        mixed[:, cols] = got.astype(BF16)
    for t, lanes in enumerate(lane_tiles(chans)):
        gram[t] += dot_tn(
            mixed[:, chans + lanes.start : chans + lanes.stop],
            mixed[:, 2 * chans + lanes.start : 2 * chans + lanes.stop],
        )


def same_head():
    row = lax.broadcasted_iota(jnp.int32, (LANES, LANES), 0)
    col = lax.broadcasted_iota(jnp.int32, (LANES, LANES), 1)
    return row // HEAD_DIM == col // HEAD_DIM


def channel_weights(gram, scale):
    own = same_head()
    logits = jnp.where(own, gram * scale, -1e30)
    top = jnp.max(logits, axis=1, keepdims=True)
    raised = jnp.where(own, jnp.exp(logits - top), 0.0)
    return raised / jnp.sum(raised, axis=1, keepdims=True)


def channel_out_kernel(mixed, gram, scale, x5, mask, vec, out_w, o2, x6, keep):
    chans = x5.shape[1]
    for t, lanes in enumerate(lane_tiles(chans)):
        weights = channel_weights(gram[t], scale[0:1, :]).astype(BF16)
        o2[:, lanes] = dot_nt(mixed[:, lanes], weights).astype(BF16)
    keep[...] = dot(o2[...], out_w[...])
    add_residual(x5, keep, mask, vec, x6)


def channel_grad_kernel(
    main, prev, after, halo, mask, vec, x6, mixed, o2, out_w,
    grad, attended_grad, weights_g, packed, conv_g, small, src, rounded, out_g,
):
    width = prev.shape[0]
    chans = main.shape[1]
    zero_first(weights_g, out_g, conv_g, small)
    conv_backward(main, prev, after, halo, mask, vec, x6, grad, conv_g, small, src, width)
    rounded[...] = grad[...].astype(BF16)
    fold_rows(grad, small, 8)
    out_g[...] += dot_tn(o2[...], rounded[...])
    attended_grad[...] = dot_nt(rounded[...], out_w[...]).astype(BF16)
    for t, lanes in enumerate(lane_tiles(chans)):
        weights_g[t] += dot_tn(attended_grad[:, lanes], mixed[:, lanes])

    @pl.when(last_step())
    def _():
        packed[...] = out_g[...].astype(BF16)


def channel_back_kernel(
    attended_grad, mixed, gram, weights_g, scale, normed, x5, g6, mask, vec, mix,
    grad, packed, mix_bg, small, mixed_grad, keep, mix_g,
):
    chans = x5.shape[1]
    zero_first(mix_g, mix_bg, small)
    own = same_head()
    wide = mask[...]
    for t, lanes in enumerate(lane_tiles(chans)):
        weights = channel_weights(gram[t], scale[0:1, :])
        back = jnp.where(own, weights_g[t], 0.0)
        logit = weights * (back - jnp.sum(back * weights, axis=1, keepdims=True))
        logit = logit.astype(BF16)
        key = slice(chans + lanes.start, chans + lanes.stop)
        val = slice(2 * chans + lanes.start, 2 * chans + lanes.stop)
        query_grad = dot(attended_grad[:, lanes], weights.astype(BF16))
        key_grad = dot_nt(mixed[:, val], logit) * scale[0:1, :] * wide
        value_grad = dot(mixed[:, key], logit) * scale[0:1, :]
        for cols, part in ((lanes, query_grad), (key, key_grad), (val, value_grad)):
            mix_bg[:, cols] += fold(part)
            mixed_grad[:, cols] = part.astype(BF16)
    for part in range(3):
        cols = slice(part * chans, (part + 1) * chans)
        mix_g[part * chans : (part + 1) * chans, :] += dot_tn(normed[...], mixed_grad[:, cols])
    keep[...] = dot_nt(mixed_grad[...], mix[...])
    norm_backward(x5, keep, g6, vec, small, grad, 0)

    @pl.when(last_step())
    def _():
        packed[...] = mix_g[...].astype(BF16)


def mlp_back_kernel(
    main, prev, after, halo, mask, vec_conv, vec, x4, x3, normed, hidden, slope, up_w, down_w, mlp1, mix1, out1, core,
    grad, kept, sent, up_bg, conv_g, small,
    src, g4, rounded, keep, pre_grad, up_g, down_g,
):
    width = prev.shape[0]
    zero_first(up_g, up_bg, down_g, conv_g, small)
    conv_backward(main, prev, after, halo, mask, vec_conv, x4, g4, conv_g, small, src, width)
    rounded[...] = g4[...].astype(BF16)
    fold_rows(g4, small, 8)
    mlp_down_back(rounded, normed, hidden, slope, pre_grad, up_w, down_w, up_g, up_bg, down_g)
    keep[...] = dot_nt(pre_grad[...], up_w[...])
    norm_backward(x3, keep, g4, vec, small, grad, 16)

    @pl.when(last_step())
    def _():
        spread(core, kept, sent, [mlp1, mix1, out1] + column_blocks(up_g, kept.shape[1]) + [down_g])


def window_back_kernel(
    main, prev, after, halo, mask, vec_conv, vec, x2, x1, nw, mw, ow, mix, out_w, gather,
    grad, packed, mix_bg, conv_g, small,
    src, mix_g, out_g, g2, gw, dow, dmw, keep, probs, slopes,
):
    width = prev.shape[0]
    chans = main.shape[1]
    zero_first(mix_g, mix_bg, out_g, conv_g, small)
    conv_backward(main, prev, after, halo, mask, vec_conv, x2, g2, conv_g, small, src, width)
    fold_rows(g2, small, 8)
    gw[...] = dot(gather[...], g2[...].astype(BF16)).astype(BF16)
    out_g[...] += dot_tn(ow[...], gw[...])
    dow[...] = dot_nt(gw[...], out_w[...]).astype(BF16)
    windows = nw.shape[0] // SLOT
    real = lax.broadcasted_iota(jnp.int32, (SLOT, 4 * SLOT), 0) < WIN * WIN
    head = lax.broadcasted_iota(jnp.int32, (SLOT, LANES), 1) // HEAD_DIM

    places = [(at, lanes) for at in range(0, windows * SLOT, SLOT) for lanes in lane_tiles(chans)]
    for n, (at, lanes) in enumerate(places):
        rows = slice(at, at + SLOT)
        query = mw[rows, lanes]
        key = mw[rows, chans + lanes.start : chans + lanes.stop]
        value = mw[rows, 2 * chans + lanes.start : 2 * chans + lanes.stop]
        scores = jnp.where(real, dot_nt(key, block_heads(query)), -1e30)
        top = jnp.max(scores, axis=0, keepdims=True)
        raised = jnp.exp2((scores - top) * (SCALE * LOG2E))
        share = raised * (1.0 / jnp.sum(raised, axis=0, keepdims=True))
        share_grad = dot_nt(value, block_heads(dow[rows, lanes]))
        inner = jnp.sum(share_grad * share, axis=0, keepdims=True)
        probs[n * SLOT : (n + 1) * SLOT, :] = share.astype(BF16)
        slopes[n * SLOT : (n + 1) * SLOT, :] = (share * (share_grad - inner)).astype(BF16)
    for n, (at, lanes) in enumerate(places):
        rows = slice(at, at + SLOT)
        key_cols = slice(chans + lanes.start, chans + lanes.stop)
        value_cols = slice(2 * chans + lanes.start, 2 * chans + lanes.stop)
        share, slope = probs[n * SLOT : (n + 1) * SLOT, :], slopes[n * SLOT : (n + 1) * SLOT, :]
        value_grad = dot(share, block_heads(dow[rows, lanes]))
        key_grad = dot(slope, block_heads(mw[rows, lanes])) * SCALE
        full = dot_tn(slope, mw[rows, key_cols])
        query_grad = jnp.zeros((SLOT, LANES), F32)
        for h in range(LANES // HEAD_DIM):
            query_grad = jnp.where(head == h, full[h * SLOT : (h + 1) * SLOT], query_grad)
        query_grad = query_grad * SCALE
        for cols, part in ((lanes, query_grad), (key_cols, key_grad), (value_cols, value_grad)):
            dmw[rows, cols] = part.astype(BF16)
            mix_bg[:, cols] += fold(part)
    for part in range(3):
        cols = slice(part * chans, (part + 1) * chans)
        mix_g[part * chans : (part + 1) * chans, :] += dot_tn(nw[...], dmw[:, cols])
    normed_grad = dot_nt(dmw[...], mix[...]).astype(BF16)
    keep[...] = dot_tn(gather[...], normed_grad)
    norm_backward(x1, keep, g2, vec, small, grad, 16)

    @pl.when(last_step())
    def _():
        packed[: 3 * chans, :] = mix_g[...].astype(BF16)
        packed[3 * chans :, :] = out_g[...].astype(BF16)


def token_grad_kernel(main, prev, after, halo, mask, vec, field, core, win0, *refs):
    parts, (out, kept, sent, src, conv_g, small, rows) = refs[:-7], refs[-7:]
    width = prev.shape[0]
    zero_first(conv_g, small)
    conv_backward(main, prev, after, halo, mask, vec, field, out, conv_g, small, src, width)

    @pl.when(last_step())
    def _():
        small_sums(core, win0, conv_g, *parts[:3], small, *parts[3:], kept, sent, rows)


def call(kernel, steps, ins, outs, scratch, cost, after=()):
    count = len(ins)

    def body(*refs):
        kernel(*refs[:count], *refs[count + len(after) :])

    def spec(block, index):
        if block is None:
            return pl.BlockSpec(memory_space=pltpu.SMEM)
        if isinstance(index, int):
            fixed = (index,) + tuple(0 for _ in block[1:])
            return pl.BlockSpec((None,) + block[1:], lambda i: fixed, pipeline_mode=pl.Buffered(1))
        fixed = tuple(0 for _ in block)
        if index is None:
            return pl.BlockSpec(block, lambda i: fixed, pipeline_mode=pl.Buffered(1))
        return pl.BlockSpec(block, index)

    def out_spec(block, index):
        fixed = tuple(0 for _ in block)
        return pl.BlockSpec(block, (lambda i: fixed) if index is None else index)

    return pl.pallas_call(
        body,
        grid=(steps,),
        in_specs=[spec(block, index) for _, block, index in ins]
        + [pl.BlockSpec(memory_space=pl.ANY) for _ in after],
        out_specs=[out_spec(block, index) for _, _, block, index in outs],
        out_shape=[jax.ShapeDtypeStruct(shape, dtype) for shape, dtype, _, _ in outs],
        scratch_shapes=[pltpu.VMEM(shape, dtype) for shape, dtype in scratch],
        compiler_params=pltpu.CompilerParams(vmem_limit_bytes=VMEM_LIMIT),
        cost_estimate=pl.CostEstimate(flops=1, bytes_accessed=cost * 3_600_000, transcendentals=0),
    )(*[array for array, _, _ in ins], *after)


def gather_matrix(cols, width):
    windows = cols // WIN
    slot = np.arange(windows * SLOT)[:, None]
    window, inside = slot // SLOT, slot % SLOT
    source = inside // WIN * width + window * WIN + inside % WIN
    patch = np.arange(WIN * width)[None, :]
    return jnp.asarray(((source == patch) & (inside < WIN * WIN)).astype(BF16))


def prepare_kernel(conv_w, conv_b, gain, shift, out_b, down_b, up_b, vecs, up_bias):
    for k in range(4):
        for i in range(3):
            vecs[k, 3 * i : 3 * i + 3, :] = conv_w[k, i].astype(F32)
        last = out_b if k % 2 == 0 else down_b
        for at, ref, row in ((9, conv_b, k), (10, gain, k), (11, shift, k), (12, last, k // 2)):
            vecs[k, at : at + 1, :] = ref[row : row + 1, :].astype(F32)
    for k in range(2):
        up_bias[k] = up_b[k : k + 1, :].astype(F32)


def prepare(*parts):
    chans, ff = parts[0].shape[-1], parts[-1].shape[-1]
    return pl.pallas_call(
        prepare_kernel,
        out_shape=tuple(jax.ShapeDtypeStruct(x, F32) for x in ((4, 16, chans), (2, 1, ff))),
    )(*parts)


def image_block(x0, cot, tok_halo, mask, scale, halo_of, across, weights, small, cols, core, send_result, share_cores, share_planes):
    mix_w, out_w, up_w, down_w = weights
    height, width, chans = x0.shape
    tokens = height * width
    ff = up_w.shape[2]
    vecs, up_bias, bias0, bias1 = small
    gather = gather_matrix(cols, width)
    wrows = cols // WIN * SLOT
    unit = WIN * width
    units = height // WIN
    chunk = 2 * unit if units % 2 == 0 else unit
    chunks = tokens // chunk

    def near(array, rows):
        per = rows // width
        return [
            (array, (rows, chans), lambda i: (i, 0)),
            (array, (width, chans), lambda i: (jnp.maximum(i * per - 1, 0), 0)),
            (array, (width, chans), lambda i: (jnp.minimum(i * per + per, height - 1), 0)),
            (halo_of(array), (2 * width, chans), None),
        ]

    def rows_in(array, rows):
        return (array, (rows, array.shape[1]), lambda i: (i, 0))

    def whole(array):
        return (array, array.shape, None)

    def layer(array, k):
        return (array, array.shape, k)

    def rows_out(cols_, dtype, rows=chunk, total=tokens):
        return ((total, cols_), dtype, (rows, cols_), lambda i: (i, 0))

    def sums(*shape, dtype=F32):
        return (shape, dtype, shape, None)

    def vec(k):
        return layer(vecs, k)

    scalar = (core, None, None)

    x1, nw, mw, ow, x2 = call(
        window_forward_kernel,
        units,
        [
            (x0, (WIN, width, chans), lambda i: (i, 0, 0)),
            (x0, (1, width, chans), lambda i: (jnp.maximum(i * WIN - 1, 0), 0, 0)),
            (x0, (1, width, chans), lambda i: (jnp.minimum(i * WIN + WIN, height - 1), 0, 0)),
            whole(tok_halo),
            rows_in(mask, unit),
            vec(0),
            layer(mix_w, 0),
            whole(bias0),
            layer(out_w, 0),
            whole(gather),
        ],
        [
            rows_out(chans, F32, unit),
            rows_out(chans, BF16, wrows, units * wrows),
            rows_out(3 * chans, BF16, wrows, units * wrows),
            rows_out(chans, BF16, wrows, units * wrows),
            rows_out(chans, F32, unit),
        ],
        [
            ((unit + 2 * width, chans), F32),
            ((unit, chans), F32),
            ((wrows * chans // LANES, 4 * SLOT), BF16),
        ],
        20,
    )
    x3, x4, n1, h1, s1 = call(
        mlp_forward_kernel,
        chunks,
        near(x2, chunk) + [rows_in(mask, chunk), vec(1), layer(up_w, 0), layer(up_bias, 0), layer(down_w, 0)],
        [
            rows_out(chans, F32),
            rows_out(chans, F32),
            rows_out(chans, BF16),
            rows_out(ff, BF16),
            rows_out(ff, BF16),
        ],
        [((chunk + 2 * width, chans), F32), ((chunk, chans), F32)],
        25,
    )
    x5, n2, m2, gram = call(
        channel_mix_kernel,
        chunks,
        near(x4, chunk) + [rows_in(mask, chunk), vec(2), layer(mix_w, 1), whole(bias1)],
        [
            rows_out(chans, F32),
            rows_out(chans, BF16),
            rows_out(3 * chans, BF16),
            sums(chans // LANES, LANES, LANES),
        ],
        [((chunk + 2 * width, chans), F32)],
        11,
    )
    gram = across(gram)
    o2, x6 = call(
        channel_out_kernel,
        chunks,
        [
            rows_in(m2, chunk),
            whole(gram),
            whole(scale),
            rows_in(x5, chunk),
            rows_in(mask, chunk),
            vec(2),
            layer(out_w, 1),
        ],
        [rows_out(chans, BF16), rows_out(chans, F32)],
        [((chunk, chans), F32)],
        7,
    )
    result, g7, mlp1, up_bg1, small7 = call(
        last_mlp_kernel,
        chunks,
        near(x6, chunk)
        + [
            rows_in(mask, chunk),
            vec(3),
            layer(up_w, 1),
            layer(up_bias, 1),
            layer(down_w, 1),
            rows_in(cot, chunk),
        ],
        [
            rows_out(chans, BF16),
            rows_out(chans, F32),
            sums(2 * ff, chans, dtype=BF16),
            sums(8, ff),
            sums(24, chans),
        ],
        [
            ((chunk + 2 * width, chans), F32),
            ((chunk, chans), F32),
            ((chunk, chans), F32),
            ((chunk, chans), F32),
            ((chunk, chans), BF16),
            ((chunk, ff), BF16),
            ((chunk, ff), BF16),
            ((chans, ff), F32),
            ((ff, chans), F32),
        ],
        38,
    )
    result = send_result(result)
    g6, do2, weights_g, out1, conv_g3, small6 = call(
        channel_grad_kernel,
        chunks,
        near(g7, chunk)
        + [
            rows_in(mask, chunk),
            vec(3),
            rows_in(x6, chunk),
            (m2, (chunk, chans), lambda i: (i, 0)),
            rows_in(o2, chunk),
            layer(out_w, 1),
        ],
        [
            rows_out(chans, F32),
            rows_out(chans, BF16),
            sums(chans // LANES, LANES, LANES),
            sums(chans, chans, dtype=BF16),
            sums(72, chans),
            sums(16, chans),
        ],
        [((chunk + 2 * width, chans), F32), ((chunk, chans), BF16), ((chans, chans), F32)],
        13,
    )
    weights_g = across(weights_g)
    g5, mix1, mix_bg1, small5 = call(
        channel_back_kernel,
        chunks,
        [
            rows_in(do2, chunk),
            rows_in(m2, chunk),
            whole(gram),
            whole(weights_g),
            whole(scale),
            rows_in(n2, chunk),
            rows_in(x5, chunk),
            rows_in(g6, chunk),
            rows_in(mask, chunk),
            vec(2),
            layer(mix_w, 1),
        ],
        [
            rows_out(chans, F32),
            sums(3 * chans, chans, dtype=BF16),
            sums(8, 3 * chans),
            sums(16, chans),
        ],
        [((chunk, 3 * chans), BF16), ((chunk, chans), F32), ((3 * chans, chans), F32)],
        16,
    )
    g3, kept0, sent0, up_bg0, conv_g2, small3 = call(
        mlp_back_kernel,
        chunks,
        near(g5, chunk)
        + [
            rows_in(mask, chunk),
            vec(2),
            vec(1),
            rows_in(x4, chunk),
            rows_in(x3, chunk),
            rows_in(n1, chunk),
            rows_in(h1, chunk),
            rows_in(s1, chunk),
            layer(up_w, 0),
            layer(down_w, 0),
            whole(mlp1),
            whole(mix1),
            whole(out1),
            scalar,
        ],
        [
            rows_out(chans, F32),
            sums(2 * ff + 2 * chans, chans, dtype=BF16),
            sums(2 * ff + 2 * chans, chans, dtype=BF16),
            sums(8, ff),
            sums(72, chans),
            sums(32, chans),
        ],
        [
            ((chunk + 2 * width, chans), F32),
            ((chunk, chans), F32),
            ((chunk, chans), BF16),
            ((chunk, chans), F32),
            ((chunk, ff), BF16),
            ((chans, ff), F32),
            ((ff, chans), F32),
        ],
        32,
    )
    mid = share_planes(share_cores(kept0, sent0))
    g1, win0, mix_bg0, conv_g1, small1 = call(
        window_back_kernel,
        units,
        near(g3, unit)
        + [
            rows_in(mask, unit),
            vec(1),
            vec(0),
            rows_in(x2, unit),
            rows_in(x1, unit),
            rows_in(nw, wrows),
            rows_in(mw, wrows),
            rows_in(ow, wrows),
            layer(mix_w, 0),
            layer(out_w, 0),
            whole(gather),
        ],
        [
            rows_out(chans, F32, unit),
            sums(4 * chans, chans, dtype=BF16),
            sums(8, 3 * chans),
            sums(72, chans),
            sums(32, chans),
        ],
        [
            ((unit + 2 * width, chans), F32),
            ((3 * chans, chans), F32),
            ((chans, chans), F32),
            ((unit, chans), F32),
            ((wrows, chans), BF16),
            ((wrows, chans), BF16),
            ((wrows, 3 * chans), BF16),
            ((unit, chans), F32),
            ((wrows * chans // LANES, 4 * SLOT), BF16),
            ((wrows * chans // LANES, 4 * SLOT), BF16),
        ],
        34,
    )
    mid, g1 = lax.optimization_barrier((mid, g1))
    x0_flat = x0.reshape(tokens, chans)
    sums1 = (conv_g1, conv_g2, conv_g3, small1, small3, small5, small6, small7, mix_bg0, mix_bg1, up_bg0, up_bg1)
    half = (win0.shape[0] + SMALL_ROWS) // 2
    tokens_grad, kept, sent = call(
        token_grad_kernel,
        chunks,
        near(g1, chunk)
        + [rows_in(mask, chunk), vec(0), rows_in(x0_flat, chunk), scalar, whole(win0)]
        + [whole(array) for array in sums1],
        [rows_out(chans, BF16), sums(half, chans, dtype=BF16), sums(half, chans, dtype=BF16)],
        [
            ((chunk + 2 * width, chans), F32),
            ((72, chans), F32),
            ((8, chans), F32),
            ((SMALL_ROWS, chans), F32),
        ],
        10,
        after=(result, *mid),
    )
    return result, tokens_grad, mid, kept, sent


def small_sums(
    core, win0, conv0, conv1, conv2, conv3, s0, s1, s3, s5, s6, s7, mix0, mix1, up0, up1,
    kept, sent, rows,
):
    chans = rows.shape[1]
    rows[...] = jnp.zeros_like(rows)
    place = 0

    def put(part):
        nonlocal place
        rows[place : place + 1, :] = jnp.sum(part, axis=0, keepdims=True)
        place += 1

    for conv in (conv0, conv1, conv2, conv3):
        for k in range(9):
            put(conv[8 * k : 8 * k + 8, :])
    for ref, at in (
        (s0, 0), (s1, 0), (s3, 0), (s6, 0),
        (s1, 16), (s3, 16), (s5, 0), (s7, 8),
        (s1, 24), (s3, 24), (s5, 8), (s7, 16),
        (s1, 8), (s6, 8), (s3, 8), (s7, 0),
    ):
        put(ref[at : at + 8, :])
    for ref in (mix0, mix1, up0, up1):
        for col in range(0, ref.shape[1], chans):
            put(ref[:, col : col + chans])
    spread(core, kept, sent, [win0, rows])


def reader(halves, plane, share, offset, stride, members):
    first = halves[0][0][0]
    part = members // 2 * stride
    planes = 2 * first.shape[0] // part
    bits = planes.bit_length() - 1

    def piece(at, take):
        n, inside = divmod(at, share)
        core, n = divmod(n, planes * members)
        owner, member = divmod(n, members)
        late, place = divmod(member * stride + offset + inside, part)
        far = plane ^ owner
        if late:
            far = sum(((far >> k) & 1) << (bits - 1 - k) for k in range(bits))
        near, other = halves[core][late]
        start = (far & (planes // 2 - 1)) * part + place
        rows = pl.ds(pl.multiple_of(start, 16), take)
        return jnp.where(far < planes // 2, near[rows, :], other[rows, :]).astype(F32)

    def read(at, rows):
        parts = []
        while rows:
            take = min(rows, share - at % share)
            parts.append(piece(at, take))
            at, rows = at + take, rows - take
        return parts[0] if len(parts) == 1 else jnp.concatenate(parts, axis=0)

    return read


def plain_reader(first, second):
    half = first.shape[0]

    def read(at, rows):
        parts = []
        if at < half:
            parts.append(first[at : min(at + rows, half), :].astype(F32))
        if at + rows > half:
            parts.append(second[max(at - half, 0) : at + rows - half, :].astype(F32))
        return parts[0] if len(parts) == 1 else jnp.concatenate(parts, axis=0)

    return read


def put_attention(read, mix_w, out_w):
    chans = out_w.shape[1]
    for k in range(3):
        mix_w[0, :, k * chans : (k + 1) * chans] = read(k * chans, chans)
    out_w[0] = read(3 * chans, chans)


def put_feed(read, at, up_w, down_w):
    chans = down_w.shape[2]
    blocks = up_w.shape[2] // chans
    for k in range(blocks):
        up_w[0, :, k * chans : (k + 1) * chans] = read(at + k * chans, chans)
    for k in range(blocks):
        down_w[0, k * chans : (k + 1) * chans, :] = read(at + (blocks + k) * chans, chans)


def final_kernel(
    place, *refs, shares, members,
):
    inputs, outs, rows = refs[:-15], refs[-15:-1], refs[-1]
    (
        mix_w, out_w, up_w, down_w, conv_w, conv_b, gain, shift, last_shift, win_b, chan_b, out_b, up_b, down_b,
    ) = outs
    layer = pl.program_id(0)
    chans = inputs[0].shape[1]
    feed_rows = 2 * up_w.shape[2]
    blocks = up_b.shape[1] // chans
    mid_share, late_share = shares
    stride = mid_share + late_share
    count = len(inputs) // 2
    here, there = inputs[:count], inputs[count:]

    for flag in range(2):
        halves = (here, there) if flag == 0 else (there, here)
        if count == 2:
            mid, late = (plain_reader(*pair) for pair in zip(*halves))
        else:
            pairs = tuple((half[0:2], half[2:4]) for half in halves)
            mid = reader(pairs, place[1], mid_share, 0, stride, members)
            late = reader(pairs, place[1], late_share, mid_share, stride, members)

        @pl.when((place[0] == flag) & (layer == 0))
        def _():
            put_attention(late, mix_w, out_w)
            put_feed(lambda at, count: mid(feed_rows + 4 * chans + at, count), 0, up_w, down_w)
            rows[...] = late(4 * chans, SMALL_ROWS)

        @pl.when((place[0] == flag) & (layer == 1))
        def _():
            put_attention(lambda at, count: mid(feed_rows + at, count), mix_w, out_w)
            put_feed(mid, 0, up_w, down_w)

    @pl.when(layer == 0)
    def _():
            at = 0
            for k in range(4):
                for i in range(3):
                    for j in range(3):
                        conv_w[i, j, k : k + 1, :] = rows[at : at + 1, :]
                        at += 1
            for ref in (conv_b, gain):
                ref[...] = rows[at : at + 4, :]
                at += 4
            shift[...] = rows[at : at + 3, :]
            last_shift[...] = rows[at + 3, :]
            at += 4
            for ref in (out_b, down_b):
                ref[...] = rows[at : at + 2, :]
                at += 2
            win_b[:chans] = rows[at, :]
            win_b[chans:] = rows[at + 2, :]
            for k in range(3):
                chan_b[k * chans : (k + 1) * chans] = rows[at + 3 + k, :]
            at += 6
            for k in range(2):
                for i in range(blocks):
                    up_b[k : k + 1, i * chans : (i + 1) * chans] = rows[at : at + 1, :]
                    at += 1


def assemble(place, arrays, shares, members, ff):
    chans = arrays[0].shape[1]
    shapes = [
        (2, chans, 3 * chans), (2, chans, chans), (2, chans, ff), (2, ff, chans),
        (3, 3, 4, chans), (4, chans), (4, chans), (3, chans), (chans,),
        (2 * chans,), (3 * chans,), (2, chans), (2, ff), (2, chans),
    ]

    def out_spec(shape):
        if len(shape) == 3:
            return pl.BlockSpec((1,) + shape[1:], lambda i: (i, 0, 0))
        return pl.BlockSpec(shape, lambda i: (0,) * len(shape))

    (
        mix_w, out_w, up_w, down_w, conv_w, conv_b, gain, shift, last_shift, win_b, chan_b, out_b, up_b, down_b,
    ) = pl.pallas_call(
        functools.partial(final_kernel, shares=shares, members=members),
        grid=(2,),
        in_specs=[pl.BlockSpec(memory_space=pltpu.SMEM)]
        + [pl.BlockSpec(x.shape, lambda i: (0, 0), pipeline_mode=pl.Buffered(1)) for x in arrays],
        out_specs=[out_spec(shape) for shape in shapes],
        out_shape=[jax.ShapeDtypeStruct(shape, F32) for shape in shapes],
        scratch_shapes=[pltpu.VMEM((SMALL_ROWS, chans), F32)],
        compiler_params=pltpu.CompilerParams(vmem_limit_bytes=VMEM_LIMIT),
    )(place, *arrays)
    return (
        conv_w.transpose(2, 0, 1, 3), conv_b, gain, shift, last_shift, mix_w,
        win_b, chan_b, out_w, out_b, up_w, up_b, down_w, down_b,
    )


def split_kernel(me, *refs, terms):
    outs = refs[terms:]
    rows = outs[0].shape[0]
    for step, out in enumerate(outs):
        at = pl.multiple_of((me[0] ^ step) * rows, 16)
        total = refs[0][pl.ds(at, rows), :].astype(F32)
        for ref in refs[1:terms]:
            total = total + ref[pl.ds(at, rows), :].astype(F32)
        out[...] = total.astype(BF16)


def split_sum(terms, me, size):
    rows, chans = terms[0].shape
    rows //= size
    if rows % 16 or rows < 512:
        total = functools.reduce(lambda x, y: x + y, [term.astype(F32) for term in terms]).astype(BF16)
        return [lax.dynamic_slice_in_dim(total, (me ^ step) * rows, rows, 0) for step in range(size)]
    return pl.pallas_call(
        functools.partial(split_kernel, terms=len(terms)),
        in_specs=[pl.BlockSpec(memory_space=pltpu.SMEM)] + [pl.BlockSpec(memory_space=pltpu.VMEM)] * len(terms),
        out_shape=[jax.ShapeDtypeStruct((rows, chans), BF16)] * size,
        compiler_params=pltpu.CompilerParams(vmem_limit_bytes=VMEM_LIMIT),
    )(me.astype(jnp.int32).reshape(1), *terms)


def widen_kernel(here, *refs):
    out = refs[-1]
    cols = out.shape[2]
    for step, part in enumerate(refs[:-1]):

        @pl.when(pl.program_id(0) == step)
        def _():
            out[0] = part[:, :cols, :]


def widen(parts, here, cols):
    images = len(parts)
    height, width, chans = parts[0].shape
    return pl.pallas_call(
        widen_kernel,
        grid_spec=pltpu.PrefetchScalarGridSpec(
            num_scalar_prefetch=1,
            grid=(images,),
            in_specs=[pl.BlockSpec(x.shape, lambda i, at: (0, 0, 0), pipeline_mode=pl.Buffered(1)) for x in parts],
            out_specs=pl.BlockSpec(
                (1, height, cols, chans), lambda i, at: ((at[0] + images - i) % images, 0, 0, 0)
            ),
        ),
        out_shape=jax.ShapeDtypeStruct((images, height, cols, chans), BF16),
        compiler_params=pltpu.CompilerParams(vmem_limit_bytes=VMEM_LIMIT),
    )(here.astype(jnp.int32).reshape(1), *parts)


def local(
    tokens, heights, conv_weight, conv_bias, norm_gain, norm_shift, mix_weight, window_bias, channel_bias,
    out_weight, out_bias, up_weight, up_bias, down_weight, down_bias, cotangent,
):
    images, height, cols, chans = tokens.shape
    count = lax.axis_size("rows")
    place = lax.axis_index("rows")
    width = -(-cols // 8) * 8
    groups = count // images
    members = [[g * images + j for j in range(images)] for g in range(groups)]
    rows_here = images * height
    level = lax.dynamic_index_in_dim(heights, place % images, 0, keepdims=False)
    open_rows = heights * 7 - place * height

    def pad_image(field):
        inside = jnp.arange(height, dtype=jnp.int32)[None, :] < open_rows[:, None]
        field = jnp.where(inside[:, :, None, None], field, jnp.zeros((), field.dtype))
        return jnp.pad(field, ((0, 0), (0, 0), (0, width - cols), (0, 0)))

    def spread_image(field):
        field = lax.all_to_all(field, "rows", 0, 0, axis_index_groups=members, tiled=True)
        return field.reshape(rows_here, width, chans)

    def scatter_image(field):
        field = field.reshape(images, height, width, chans)
        field = lax.all_to_all(field, "rows", 0, 0, axis_index_groups=members, tiled=True)
        return field[:, :, :cols]

    def halo_of(field):
        flat = field.reshape(rows_here * width, chans)
        if groups == 1:
            return jnp.zeros((2 * width, chans), F32)
        down = [(i, i + images) for i in range(count - images)]
        up = [(i + images, i) for i in range(count - images)]
        above = lax.ppermute(flat[-width:].astype(BF16), "rows", down)
        below = lax.ppermute(flat[:width].astype(BF16), "rows", up)
        return jnp.concatenate([above, below], axis=0).astype(F32)

    def across(value):
        if groups == 1:
            return value
        other = [[j + g * images for g in range(groups)] for j in range(images)]
        return lax.psum(value, "rows", axis_index_groups=other)

    row = jnp.arange(rows_here * width, dtype=jnp.int32) // width + place // images * rows_here
    col = jnp.arange(rows_here * width, dtype=jnp.int32) % width
    mask = ((row < level * 7) & (col < cols)).astype(F32)
    mask = jnp.broadcast_to(mask[:, None], (rows_here * width, LANES))
    scale = lax.rsqrt((level * 7 * cols).astype(F32))
    scale = jnp.broadcast_to(scale, (8, LANES))
    small = prepare(conv_weight, conv_bias, norm_gain, norm_shift, out_bias, down_bias, up_bias)
    small += (
        jnp.concatenate([window_bias[:chans], jnp.zeros((chans,), BF16), window_bias[chans:]]).astype(F32)[None],
        channel_bias.astype(F32)[None],
    )
    x0 = spread_image(pad_image(tokens))
    cot, small, mask, scale = lax.optimization_barrier((pad_image(cotangent), small, mask, scale))
    cot = spread_image(cot).reshape(rows_here * width, chans)

    def exchange(part, axis, step):
        size = lax.axis_size(axis)
        return lax.ppermute(part, axis, [(i, i ^ step) for i in range(size)])

    core = lax.axis_index("core").astype(jnp.int32).reshape(1)

    def share(terms, axis):
        size = lax.axis_size(axis)
        pieces = split_sum(terms, lax.axis_index(axis), size)
        return [pieces[0]] + [exchange(pieces[step], axis, step) for step in range(1, size)]

    def share_cores(kept, sent):
        return [kept, exchange(sent, "core", 1)]

    def total(terms):
        return functools.reduce(lambda x, y: x + y, [term.astype(F32) for term in terms]).astype(BF16)

    def gather(part, axis):
        size, me = lax.axis_size(axis), lax.axis_index(axis)
        rows = part.shape[0]
        out = jnp.zeros((size * rows, part.shape[1]), part.dtype)
        for step in range(size):
            got = part if step == 0 else exchange(part, axis, step)
            out = lax.dynamic_update_slice_in_dim(out, got, (me ^ step) * rows, 0)
        return out

    def join(part, other):
        rows = part.shape[0]
        out = jnp.zeros((2 * rows, part.shape[1]), part.dtype)
        out = lax.dynamic_update_slice_in_dim(out, part, 0, 0)
        return lax.dynamic_update_slice_in_dim(out, other, rows, 0)

    def send_tokens(field):
        field = field.reshape(images, height, width, chans)
        here = place % images
        parts = []
        for step in range(images):
            part = lax.dynamic_index_in_dim(field, (here + step) % images, 0, keepdims=False)
            if step:
                pairs = [(g * images + j, g * images + (j + step) % images) for g in range(groups) for j in range(images)]
                part = lax.ppermute(part, "rows", pairs)
            parts.append(part)
        return parts

    weights = (mix_weight, out_weight, up_weight, down_weight)
    result, tokens_grad, mid, kept, sent = image_block(
        x0, cot, halo_of(x0), mask, scale, halo_of, across, weights, small, cols, core,
        scatter_image, share_cores, lambda terms: share(terms, "plane"),
    )
    together = lax.optimization_barrier
    tokens_grad = send_tokens(tokens_grad)
    mid = share(mid, "rows")
    kept, sent, mid = together((kept, sent, mid))
    late = share(share_cores(kept, sent), "plane")
    late, tokens_grad[2:3] = together((late, tokens_grad[2:3]))
    late = total(share(late, "rows"))
    mid = total(mid)
    shares = (mid.shape[0], late.shape[0])
    block = gather(jnp.concatenate([mid, late], axis=0), "rows")
    members = lax.axis_size("rows")
    bits = lax.axis_size("plane").bit_length() - 1
    half = block.shape[0] // 2
    parts = [block[:half], block[half:]]
    aligned = all(rows % 16 == 0 for rows in shares)
    if not aligned:
        block = gather(block, "plane").reshape(-1, sum(shares), chans)
        arrays = [block[:, : shares[0]].reshape(-1, chans), block[:, shares[0] :].reshape(-1, chans)]
        tokens_grad = widen(tokens_grad, place % images, cols)
    for k in range(bits if aligned else 0):
        others = [exchange(part, "plane", 1 << bit) for part, bit in zip(parts, (k, bits - 1 - k))]
        if k == bits - 1:
            tokens_grad = widen(tokens_grad, place % images, cols)
            others, tokens_grad = together((others, tokens_grad))
        if k + 1 < bits:
            parts = [join(part, other) for part, other in zip(parts, others)]
        else:
            arrays = [parts[0], others[0], parts[1], others[1]]
    arrays += [exchange(array, "core", 1) for array in arrays]
    at = jnp.concatenate([core, lax.axis_index("plane").astype(jnp.int32).reshape(1)])
    return result, tokens_grad.astype(F32), *assemble(at, arrays, shares, members, up_weight.shape[2])


def solution(mesh):
    planes = mesh.shape["dp"] // 2
    fine = Mesh(mesh.devices.reshape(planes, 2, mesh.shape["rows"]), ("plane", "core", "rows"))
    dp = ("plane", "core")
    split = P(dp, "rows", None, None)
    in_specs = (split, P(dp)) + (P(),) * 13 + (split,)
    out_specs = (split, split) + (P(),) * 14
    return jax.shard_map(local, mesh=fine, in_specs=in_specs, out_specs=out_specs, check_vma=False)
```

```python
import functools

import jax
import jax.numpy as jnp
import numpy as np
from jax import lax
from jax.experimental import pallas as pl
from jax.experimental.pallas import tpu as pltpu
from jax.sharding import Mesh
from jax.sharding import PartitionSpec as P

HEADS = 12
HEAD_DIM = 32
EPS = 1e-05
WIN = 7
SLOT = 64
LANES = 128
F32 = jnp.float32
BF16 = jnp.bfloat16
SCALE = HEAD_DIM ** (-0.5)
LOG2E = 1.4426950408889634
ROOT_HALF = 0.7071067811865476
VMEM_LIMIT = 58 * 1024 * 1024
SMALL_ROWS = 512


def dot(left, right):
    return jnp.dot(left, right, preferred_element_type=F32)


def dot_nt(left, right):
    return lax.dot_general(left, right, (((1,), (1,)), ((), ())), preferred_element_type=F32)


def dot_tn(left, right):
    return lax.dot_general(left, right, (((0,), (0,)), ((), ())), preferred_element_type=F32)


def low(value):
    return value.astype(BF16).astype(F32)


def fold(value):
    rows, cols = value.shape
    return jnp.sum(value.reshape(rows // 8, 8, cols), axis=0)


def loop(count, step, body):
    for at in range(0, count, step):
        body(at)


def lane_tiles(chans):
    return [slice(t, t + LANES) for t in range(0, chans, LANES)]


def gelu_parts(value):
    size = jnp.abs(value)
    t = 1.0 / (1.0 + (0.3275911 * ROOT_HALF) * size)
    poly = t * (
        0.127414796
        + t * (-0.142248368 + t * (0.7107068705 + t * (-0.7265760135 + t * 0.5307027145)))
    )
    bell = jnp.exp2(value * value * (-0.5 * LOG2E))
    tail = poly * bell
    cdf = jnp.where(value >= 0.0, 1.0 - tail, tail)
    return value * cdf, cdf + value * bell * 0.3989422804014327


def norm_of(value, gain, shift):
    centre = value - jnp.mean(value, axis=-1, keepdims=True)
    spread = jnp.mean(centre * centre, axis=-1, keepdims=True)
    return centre * lax.rsqrt(spread + EPS) * gain + shift


def norm_back(value, gain, normed_grad):
    centre = value - jnp.mean(value, axis=-1, keepdims=True)
    inv = lax.rsqrt(jnp.mean(centre * centre, axis=-1, keepdims=True) + EPS)
    unit = centre * inv
    unit_grad = normed_grad * gain
    first = jnp.mean(unit_grad, axis=-1, keepdims=True)
    second = jnp.mean(unit_grad * unit, axis=-1, keepdims=True)
    return inv * (unit_grad - first - unit * second), normed_grad * unit


def fill_source(src, main, prev, after, halo, step, steps, width):
    rows = main.shape[0]
    src[pl.ds(0, width), :] = jnp.where(step == 0, halo[0:width, :], low(prev[...]))
    src[pl.ds(rows + width, width), :] = jnp.where(
        step == steps - 1, halo[width : 2 * width, :], low(after[...])
    )

    def body(at):
        src[pl.ds(at + width, 2 * width), :] = low(main[pl.ds(at, 2 * width), :])

    loop(rows // (2 * width) * 2 * width, 2 * width, body)
    if rows % (2 * width):
        at = rows - width
        src[pl.ds(at + width, width), :] = low(main[pl.ds(at, width), :])


def conv_tile(src, vec, at, tile, width, lanes, flipped):
    rows = [src[pl.ds(at + width * d, tile), lanes] for d in range(3)]
    sums = []
    for col in range(3):
        total = None
        for row in range(3):
            k = (2 - row) * 3 + (2 - col) if flipped else row * 3 + col
            term = rows[row] * vec[k : k + 1, lanes]
            total = term if total is None else total + term
        sums.append(total)
    return sums[1] + pltpu.roll(sums[0], 1, 0) + pltpu.roll(sums[2], tile - 1, 0), rows


def conv_weight_tile(acc, rows, field, tile, lanes):
    shifted = [pltpu.roll(field, 1, 0), field, pltpu.roll(field, tile - 1, 0)]
    for row in range(3):
        for col in range(3):
            k = row * 3 + col
            acc[8 * k : 8 * k + 8, lanes] += fold(shifted[col] * rows[2 - row])


def block_heads(part):
    lane = lax.broadcasted_iota(jnp.int32, part.shape, 1)
    zero = jnp.zeros_like(part)
    return jnp.concatenate(
        [jnp.where(lane // HEAD_DIM == h, part, zero) for h in range(LANES // HEAD_DIM)], axis=0
    )


def window_forward_kernel(
    tok, prev, after, halo, mask, vec, mix, mix_b, out_w, gather, x1, nw, mw, ow, x2, src, keep, probs
):
    step, steps = pl.program_id(0), pl.num_programs(0)
    rows, width, chans = tok.shape
    src[pl.ds(0, width), :] = jnp.where(step == 0, halo[0:width, :], prev[0].astype(F32))
    src[pl.ds((rows + 1) * width, width), :] = jnp.where(
        step == steps - 1, halo[width : 2 * width, :], after[0].astype(F32)
    )
    for i in range(rows):
        src[pl.ds((i + 1) * width, width), :] = tok[i].astype(F32)

    def conv_body(at):
        region = mask[pl.ds(at, width), :]
        for lanes in lane_tiles(chans):
            got, near = conv_tile(src, vec, at, width, width, lanes, False)
            x1[pl.ds(at, width), lanes] = region * (near[1] + got + vec[9:10, lanes])

    loop(rows * width, width, conv_body)

    normed = norm_of(x1[...], vec[10:11, :], vec[11:12, :]).astype(BF16)
    normed = dot(gather[...], normed).astype(BF16)
    nw[...] = normed
    mw[...] = (dot(normed, mix[...]) + mix_b[...]).astype(BF16)
    windows = nw.shape[0] // SLOT
    lane = lax.broadcasted_iota(jnp.int32, (SLOT, LANES), 1)
    left = lane < SLOT
    real = lane % SLOT < WIN * WIN
    ones = (
        lax.broadcasted_iota(jnp.int32, (4 * SLOT, LANES), 0) // SLOT
        == lax.broadcasted_iota(jnp.int32, (4 * SLOT, LANES), 1) // HEAD_DIM
    ).astype(BF16)
    floor = -1e30

    places = [(at, lanes) for at in range(0, windows * SLOT, SLOT) for lanes in lane_tiles(chans)]
    for n, (at, lanes) in enumerate(places):
        query = mw[at : at + SLOT, lanes]
        key = mw[at : at + SLOT, chans + lanes.start : chans + lanes.stop]
        scores = dot_nt(query, block_heads(key))
        for half in range(2):
            part = jnp.where(real, scores[:, half * LANES : (half + 1) * LANES], floor)
            top_l = jnp.max(jnp.where(left, part, floor), axis=1, keepdims=True)
            top_r = jnp.max(jnp.where(left, floor, part), axis=1, keepdims=True)
            top = jnp.where(left, top_l, top_r)
            raised = jnp.exp2((part - top) * (SCALE * LOG2E)).astype(BF16)
            probs[n * SLOT : (n + 1) * SLOT, half * LANES : (half + 1) * LANES] = raised
    for n, (at, lanes) in enumerate(places):
        value = mw[at : at + SLOT, 2 * chans + lanes.start : 2 * chans + lanes.stop]
        both = dot(
            probs[n * SLOT : (n + 1) * SLOT, :], jnp.concatenate([block_heads(value), ones], axis=1)
        )
        ow[at : at + SLOT, lanes] = (both[:, :LANES] / both[:, LANES:]).astype(BF16)
    merged = dot_tn(gather[...], ow[...]).astype(BF16)
    keep[...] = dot(merged, out_w[...])

    def out_body(at):
        region = mask[pl.ds(at, width), :]
        for lanes in lane_tiles(chans):
            x2[pl.ds(at, width), lanes] = region * (
                x1[pl.ds(at, width), lanes] + keep[pl.ds(at, width), lanes] + vec[12:13, lanes]
            )

    loop(rows * width, width, out_body)


def conv_forward(main, prev, after, halo, mask, vec, out, src, width):
    step, steps = pl.program_id(0), pl.num_programs(0)
    rows, chans = main.shape
    fill_source(src, main, prev, after, halo, step, steps, width)
    tile = 2 * width

    def body(at):
        region = mask[pl.ds(at, tile), :]
        for lanes in lane_tiles(chans):
            got, _ = conv_tile(src, vec, at, tile, width, lanes, False)
            out[pl.ds(at, tile), lanes] = region * (
                main[pl.ds(at, tile), lanes] + got + vec[9:10, lanes]
            )

    loop(rows, tile, body)


def norm_forward(value, vec, out):
    out[...] = norm_of(value[...], vec[10:11, :], vec[11:12, :]).astype(BF16)


def column_slices(width):
    return [slice(at, at + 256) for at in range(0, width, 256)]


def mlp_body(normed, up_w, up_b, down_w, hidden, slope, keep):
    rows = normed.shape[0]
    blocks = column_slices(up_w.shape[1])

    def up(cols):
        return dot(normed[...], up_w[:, cols]) + up_b[:, cols]

    after = up(blocks[0])
    for n, cols in enumerate(blocks):
        pre, after = after, up(blocks[n + 1]) if n + 1 < len(blocks) else None
        for row in range(0, rows, 144):
            act, der = gelu_parts(pre[row : row + 144])
            hidden[row : row + 144, cols] = act.astype(BF16)
            slope[row : row + 144, cols] = der.astype(BF16)
        part = dot(hidden[:, cols], down_w[cols, :])
        if n == 0:
            keep[...] = part
        else:
            keep[...] += part


def add_residual(state, branch, mask, vec, out):
    chans = state.shape[1]

    def body(at):
        region = mask[pl.ds(at, 144), :]
        for lanes in lane_tiles(chans):
            out[pl.ds(at, 144), lanes] = (
                region
                * (state[pl.ds(at, 144), lanes] + branch[pl.ds(at, 144), lanes] + vec[12:13, lanes])
            ).astype(out.dtype)

    loop(state.shape[0], 144, body)


def mlp_forward_kernel(
    main, prev, after, halo, mask, vec, up_w, up_b, down_w, x3, x4, normed, hidden, slope, src, keep
):
    width = prev.shape[0]
    conv_forward(main, prev, after, halo, mask, vec, x3, src, width)
    norm_forward(x3, vec, normed)
    mlp_body(normed, up_w, up_b, down_w, hidden, slope, keep)
    add_residual(x3, keep, mask, vec, x4)


def norm_backward(state, normed_grad, grad, vec, small, out, gain_row):
    part = normed_grad[...]
    back, scaled = norm_back(state[...], vec[10:11, :], part)
    out[...] = grad[...].astype(F32) + back
    small[gain_row : gain_row + 8, :] += fold(scaled)
    small[gain_row + 8 : gain_row + 16, :] += fold(part)


def mlp_down_back(rounded, normed, hidden, slope, pre_grad, up_w, down_w, up_g, up_bg, down_g):
    rows = rounded.shape[0]
    blocks = column_slices(up_w.shape[1])

    def down(cols):
        return dot_nt(rounded[...], down_w[cols, :])

    def weights(cols):
        up_g[:, cols] += dot_tn(normed[...], pre_grad[:, cols])
        down_g[cols, :] += dot_tn(hidden[:, cols], rounded[...])

    after = down(blocks[0])
    for n, cols in enumerate(blocks):
        hidden_grad, after = after, down(blocks[n + 1]) if n + 1 < len(blocks) else None
        total = None
        for row in range(0, rows, 144):
            part = hidden_grad[row : row + 144] * slope[row : row + 144, cols].astype(F32)
            pre_grad[row : row + 144, cols] = part.astype(BF16)
            total = fold(part) if total is None else total + fold(part)
        up_bg[:, cols] += total
        if n:
            weights(blocks[n - 1])
    weights(blocks[-1])


def mlp_both(normed, cot, up_w, up_b, down_w, hidden, pre_grad, up_g, up_bg, down_g):
    rows = normed.shape[0]
    blocks = column_slices(up_w.shape[1])

    def inputs(cols):
        return dot(normed[...], up_w[:, cols]) + up_b[:, cols], dot_nt(cot[...], down_w[cols, :])

    def weights(cols):
        up_g[:, cols] += dot_tn(normed[...], pre_grad[:, cols])
        down_g[cols, :] += dot_tn(hidden[:, cols], cot[...])

    after = inputs(blocks[0])
    for n, cols in enumerate(blocks):
        (pre, hidden_grad), after = after, inputs(blocks[n + 1]) if n + 1 < len(blocks) else None
        total = None
        for row in range(0, rows, 144):
            act, der = gelu_parts(pre[row : row + 144])
            hidden[row : row + 144, cols] = act.astype(BF16)
            part = hidden_grad[row : row + 144] * der
            pre_grad[row : row + 144, cols] = part.astype(BF16)
            total = fold(part) if total is None else total + fold(part)
        up_bg[:, cols] += total
        if n:
            weights(blocks[n - 1])
    weights(blocks[-1])


def column_blocks(source, chans):
    return [source.at[:, col : col + chans] for col in range(0, source.shape[1], chans)]


def spread(core, kept, sent, blocks):
    half = kept.shape[0]
    for flag in range(2):

        @pl.when(core[0] == flag)
        def _():
            at = 0
            for block in blocks:
                rows = block.shape[0]
                cuts = [0, rows] if not at < half < at + rows else [0, half - at, rows]
                for low_cut, high_cut in zip(cuts, cuts[1:]):
                    start = at + low_cut
                    target = kept if (start >= half) == (flag == 1) else sent
                    start = start % half
                    target[start : start + high_cut - low_cut, :] = block[
                        low_cut:high_cut, :
                    ].astype(BF16)
                at += rows


def last_step():
    return pl.program_id(0) == pl.num_programs(0) - 1


def zero_first(*refs):
    @pl.when(pl.program_id(0) == 0)
    def _():
        for ref in refs:
            ref[...] = jnp.zeros_like(ref)


def last_mlp_kernel(
    main, prev, after, halo, mask, vec, up_w, up_b, down_w, cot,
    result, grad, packed, up_bg, small,
    src, x7, keep, back, normed, hidden, pre_grad, up_g, down_g,
):
    width = prev.shape[0]
    zero_first(up_g, up_bg, down_g, small)
    conv_forward(main, prev, after, halo, mask, vec, x7, src, width)
    norm_forward(x7, vec, normed)
    mlp_both(normed, cot, up_w, up_b, down_w, hidden, pre_grad, up_g, up_bg, down_g)
    keep[...] = dot(hidden[...], down_w[...])
    back[...] = dot_nt(pre_grad[...], up_w[...])
    add_residual(x7, keep, mask, vec, result)
    small[0:8, :] += fold(cot[...].astype(F32))
    norm_backward(x7, back, cot, vec, small, grad, 8)

    @pl.when(last_step())
    def _():
        at = 0
        for block in column_blocks(up_g, packed.shape[1]) + [down_g]:
            packed[at : at + block.shape[0], :] = block[...].astype(BF16)
            at += block.shape[0]


def conv_backward(main, prev, after, halo, mask, vec, field, out, conv_g, small, src, width):
    step, steps = pl.program_id(0), pl.num_programs(0)
    rows, chans = main.shape
    fill_source(src, main, prev, after, halo, step, steps, width)
    tile = 72

    def body(at):
        region = mask[pl.ds(at, tile), :]
        for lanes in lane_tiles(chans):
            got, near = conv_tile(src, vec, at, tile, width, lanes, True)
            grad = main[pl.ds(at, tile), lanes]
            out[pl.ds(at, tile), lanes] = (region * (grad + got)).astype(out.dtype)
            conv_weight_tile(conv_g, near, low(field[pl.ds(at, tile), lanes]), tile, lanes)
            small[0:8, lanes] += fold(grad)

    loop(rows, tile, body)


def fold_rows(source, small, row):
    def body(at):
        small[row : row + 8, :] += fold(source[pl.ds(at, 72), :])

    loop(source.shape[0], 72, body)


def channel_mix_kernel(
    main, prev, after, halo, mask, vec, mix, mix_b, x5, normed, mixed, gram, src
):
    width = prev.shape[0]
    chans = main.shape[1]
    zero_first(gram)
    conv_forward(main, prev, after, halo, mask, vec, x5, src, width)
    norm_forward(x5, vec, normed)
    rows = main.shape[0]
    for part in range(3):
        cols = slice(part * chans, (part + 1) * chans)
        got = dot(normed[...], mix[:, cols]) + mix_b[:, cols]
        if part == 1:
            got = got * jnp.concatenate([mask[...]] * (chans // LANES), axis=1)
        mixed[:, cols] = got.astype(BF16)
    for t, lanes in enumerate(lane_tiles(chans)):
        gram[t] += dot_tn(
            mixed[:, chans + lanes.start : chans + lanes.stop],
            mixed[:, 2 * chans + lanes.start : 2 * chans + lanes.stop],
        )


def same_head():
    row = lax.broadcasted_iota(jnp.int32, (LANES, LANES), 0)
    col = lax.broadcasted_iota(jnp.int32, (LANES, LANES), 1)
    return row // HEAD_DIM == col // HEAD_DIM


def channel_weights(gram, scale):
    own = same_head()
    logits = jnp.where(own, gram * scale, -1e30)
    top = jnp.max(logits, axis=1, keepdims=True)
    raised = jnp.where(own, jnp.exp(logits - top), 0.0)
    return raised / jnp.sum(raised, axis=1, keepdims=True)


def channel_out_kernel(mixed, gram, scale, x5, mask, vec, out_w, o2, x6, keep):
    chans = x5.shape[1]
    for t, lanes in enumerate(lane_tiles(chans)):
        weights = channel_weights(gram[t], scale[0:1, :]).astype(BF16)
        o2[:, lanes] = dot_nt(mixed[:, lanes], weights).astype(BF16)
    keep[...] = dot(o2[...], out_w[...])
    add_residual(x5, keep, mask, vec, x6)


def channel_grad_kernel(
    main, prev, after, halo, mask, vec, x6, mixed, o2, out_w,
    grad, attended_grad, weights_g, packed, conv_g, small, src, rounded, out_g,
):
    width = prev.shape[0]
    chans = main.shape[1]
    zero_first(weights_g, out_g, conv_g, small)
    conv_backward(main, prev, after, halo, mask, vec, x6, grad, conv_g, small, src, width)
    rounded[...] = grad[...].astype(BF16)
    fold_rows(grad, small, 8)
    out_g[...] += dot_tn(o2[...], rounded[...])
    attended_grad[...] = dot_nt(rounded[...], out_w[...]).astype(BF16)
    for t, lanes in enumerate(lane_tiles(chans)):
        weights_g[t] += dot_tn(attended_grad[:, lanes], mixed[:, lanes])

    @pl.when(last_step())
    def _():
        packed[...] = out_g[...].astype(BF16)


def channel_back_kernel(
    attended_grad, mixed, gram, weights_g, scale, normed, x5, g6, mask, vec, mix,
    grad, packed, mix_bg, small, mixed_grad, keep, mix_g,
):
    chans = x5.shape[1]
    zero_first(mix_g, mix_bg, small)
    own = same_head()
    wide = mask[...]
    for t, lanes in enumerate(lane_tiles(chans)):
        weights = channel_weights(gram[t], scale[0:1, :])
        back = jnp.where(own, weights_g[t], 0.0)
        logit = weights * (back - jnp.sum(back * weights, axis=1, keepdims=True))
        logit = logit.astype(BF16)
        key = slice(chans + lanes.start, chans + lanes.stop)
        val = slice(2 * chans + lanes.start, 2 * chans + lanes.stop)
        query_grad = dot(attended_grad[:, lanes], weights.astype(BF16))
        key_grad = dot_nt(mixed[:, val], logit) * scale[0:1, :] * wide
        value_grad = dot(mixed[:, key], logit) * scale[0:1, :]
        for cols, part in ((lanes, query_grad), (key, key_grad), (val, value_grad)):
            mix_bg[:, cols] += fold(part)
            mixed_grad[:, cols] = part.astype(BF16)
    for part in range(3):
        cols = slice(part * chans, (part + 1) * chans)
        mix_g[part * chans : (part + 1) * chans, :] += dot_tn(normed[...], mixed_grad[:, cols])
    keep[...] = dot_nt(mixed_grad[...], mix[...])
    norm_backward(x5, keep, g6, vec, small, grad, 0)

    @pl.when(last_step())
    def _():
        packed[...] = mix_g[...].astype(BF16)


def mlp_back_kernel(
    main, prev, after, halo, mask, vec_conv, vec, x4, x3, normed, hidden, slope, up_w, down_w, mlp1, mix1, out1, core,
    grad, kept, sent, up_bg, conv_g, small,
    src, g4, rounded, keep, pre_grad, up_g, down_g,
):
    width = prev.shape[0]
    zero_first(up_g, up_bg, down_g, conv_g, small)
    conv_backward(main, prev, after, halo, mask, vec_conv, x4, g4, conv_g, small, src, width)
    rounded[...] = g4[...].astype(BF16)
    fold_rows(g4, small, 8)
    mlp_down_back(rounded, normed, hidden, slope, pre_grad, up_w, down_w, up_g, up_bg, down_g)
    keep[...] = dot_nt(pre_grad[...], up_w[...])
    norm_backward(x3, keep, g4, vec, small, grad, 16)

    @pl.when(last_step())
    def _():
        spread(core, kept, sent, [mlp1, mix1, out1] + column_blocks(up_g, kept.shape[1]) + [down_g])


def window_back_kernel(
    main, prev, after, halo, mask, vec_conv, vec, x2, x1, nw, mw, ow, mix, out_w, gather,
    grad, packed, mix_bg, conv_g, small,
    src, mix_g, out_g, g2, gw, dow, dmw, keep, probs, slopes,
):
    width = prev.shape[0]
    chans = main.shape[1]
    zero_first(mix_g, mix_bg, out_g, conv_g, small)
    conv_backward(main, prev, after, halo, mask, vec_conv, x2, g2, conv_g, small, src, width)
    fold_rows(g2, small, 8)
    gw[...] = dot(gather[...], g2[...].astype(BF16)).astype(BF16)
    out_g[...] += dot_tn(ow[...], gw[...])
    dow[...] = dot_nt(gw[...], out_w[...]).astype(BF16)
    windows = nw.shape[0] // SLOT
    real = lax.broadcasted_iota(jnp.int32, (SLOT, 4 * SLOT), 0) < WIN * WIN
    head = lax.broadcasted_iota(jnp.int32, (SLOT, LANES), 1) // HEAD_DIM

    places = [(at, lanes) for at in range(0, windows * SLOT, SLOT) for lanes in lane_tiles(chans)]
    for n, (at, lanes) in enumerate(places):
        rows = slice(at, at + SLOT)
        query = mw[rows, lanes]
        key = mw[rows, chans + lanes.start : chans + lanes.stop]
        value = mw[rows, 2 * chans + lanes.start : 2 * chans + lanes.stop]
        scores = jnp.where(real, dot_nt(key, block_heads(query)), -1e30)
        top = jnp.max(scores, axis=0, keepdims=True)
        raised = jnp.exp2((scores - top) * (SCALE * LOG2E))
        share = raised * (1.0 / jnp.sum(raised, axis=0, keepdims=True))
        share_grad = dot_nt(value, block_heads(dow[rows, lanes]))
        inner = jnp.sum(share_grad * share, axis=0, keepdims=True)
        probs[n * SLOT : (n + 1) * SLOT, :] = share.astype(BF16)
        slopes[n * SLOT : (n + 1) * SLOT, :] = (share * (share_grad - inner)).astype(BF16)
    for n, (at, lanes) in enumerate(places):
        rows = slice(at, at + SLOT)
        key_cols = slice(chans + lanes.start, chans + lanes.stop)
        value_cols = slice(2 * chans + lanes.start, 2 * chans + lanes.stop)
        share, slope = probs[n * SLOT : (n + 1) * SLOT, :], slopes[n * SLOT : (n + 1) * SLOT, :]
        value_grad = dot(share, block_heads(dow[rows, lanes]))
        key_grad = dot(slope, block_heads(mw[rows, lanes])) * SCALE
        full = dot_tn(slope, mw[rows, key_cols])
        query_grad = jnp.zeros((SLOT, LANES), F32)
        for h in range(LANES // HEAD_DIM):
            query_grad = jnp.where(head == h, full[h * SLOT : (h + 1) * SLOT], query_grad)
        query_grad = query_grad * SCALE
        for cols, part in ((lanes, query_grad), (key_cols, key_grad), (value_cols, value_grad)):
            dmw[rows, cols] = part.astype(BF16)
            mix_bg[:, cols] += fold(part)
    for part in range(3):
        cols = slice(part * chans, (part + 1) * chans)
        mix_g[part * chans : (part + 1) * chans, :] += dot_tn(nw[...], dmw[:, cols])
    normed_grad = dot_nt(dmw[...], mix[...]).astype(BF16)
    keep[...] = dot_tn(gather[...], normed_grad)
    norm_backward(x1, keep, g2, vec, small, grad, 16)

    @pl.when(last_step())
    def _():
        packed[: 3 * chans, :] = mix_g[...].astype(BF16)
        packed[3 * chans :, :] = out_g[...].astype(BF16)


def token_grad_kernel(main, prev, after, halo, mask, vec, field, core, win0, *refs):
    parts, (out, kept, sent, src, conv_g, small, rows) = refs[:-7], refs[-7:]
    width = prev.shape[0]
    zero_first(conv_g, small)
    conv_backward(main, prev, after, halo, mask, vec, field, out, conv_g, small, src, width)

    @pl.when(last_step())
    def _():
        small_sums(core, win0, conv_g, *parts[:3], small, *parts[3:], kept, sent, rows)


def call(kernel, steps, ins, outs, scratch, cost, after=()):
    count = len(ins)

    def body(*refs):
        kernel(*refs[:count], *refs[count + len(after) :])

    def spec(block, index):
        if block is None:
            return pl.BlockSpec(memory_space=pltpu.SMEM)
        if isinstance(index, int):
            fixed = (index,) + tuple(0 for _ in block[1:])
            return pl.BlockSpec((None,) + block[1:], lambda i: fixed, pipeline_mode=pl.Buffered(1))
        fixed = tuple(0 for _ in block)
        if index is None:
            return pl.BlockSpec(block, lambda i: fixed, pipeline_mode=pl.Buffered(1))
        return pl.BlockSpec(block, index)

    def out_spec(block, index):
        fixed = tuple(0 for _ in block)
        return pl.BlockSpec(block, (lambda i: fixed) if index is None else index)

    return pl.pallas_call(
        body,
        grid=(steps,),
        in_specs=[spec(block, index) for _, block, index in ins]
        + [pl.BlockSpec(memory_space=pl.ANY) for _ in after],
        out_specs=[out_spec(block, index) for _, _, block, index in outs],
        out_shape=[jax.ShapeDtypeStruct(shape, dtype) for shape, dtype, _, _ in outs],
        scratch_shapes=[pltpu.VMEM(shape, dtype) for shape, dtype in scratch],
        compiler_params=pltpu.CompilerParams(vmem_limit_bytes=VMEM_LIMIT),
        cost_estimate=pl.CostEstimate(flops=1, bytes_accessed=cost * 3_600_000, transcendentals=0),
    )(*[array for array, _, _ in ins], *after)


def gather_matrix(cols, width):
    windows = cols // WIN
    slot = np.arange(windows * SLOT)[:, None]
    window, inside = slot // SLOT, slot % SLOT
    source = inside // WIN * width + window * WIN + inside % WIN
    patch = np.arange(WIN * width)[None, :]
    return jnp.asarray(((source == patch) & (inside < WIN * WIN)).astype(BF16))


def prepare_kernel(conv_w, conv_b, gain, shift, out_b, down_b, up_b, vecs, up_bias):
    for k in range(4):
        for i in range(3):
            vecs[k, 3 * i : 3 * i + 3, :] = conv_w[k, i].astype(F32)
        last = out_b if k % 2 == 0 else down_b
        for at, ref, row in ((9, conv_b, k), (10, gain, k), (11, shift, k), (12, last, k // 2)):
            vecs[k, at : at + 1, :] = ref[row : row + 1, :].astype(F32)
    for k in range(2):
        up_bias[k] = up_b[k : k + 1, :].astype(F32)


def prepare(*parts):
    chans, ff = parts[0].shape[-1], parts[-1].shape[-1]
    return pl.pallas_call(
        prepare_kernel,
        out_shape=tuple(jax.ShapeDtypeStruct(x, F32) for x in ((4, 16, chans), (2, 1, ff))),
    )(*parts)


def image_block(x0, cot, tok_halo, mask, scale, halo_of, across, weights, small, cols, core, send_result, share_cores, share_planes):
    mix_w, out_w, up_w, down_w = weights
    height, width, chans = x0.shape
    tokens = height * width
    ff = up_w.shape[2]
    vecs, up_bias, bias0, bias1 = small
    gather = gather_matrix(cols, width)
    wrows = cols // WIN * SLOT
    unit = WIN * width
    units = height // WIN
    chunk = 2 * unit if units % 2 == 0 else unit
    chunks = tokens // chunk

    def near(array, rows):
        per = rows // width
        return [
            (array, (rows, chans), lambda i: (i, 0)),
            (array, (width, chans), lambda i: (jnp.maximum(i * per - 1, 0), 0)),
            (array, (width, chans), lambda i: (jnp.minimum(i * per + per, height - 1), 0)),
            (halo_of(array), (2 * width, chans), None),
        ]

    def rows_in(array, rows):
        return (array, (rows, array.shape[1]), lambda i: (i, 0))

    def whole(array):
        return (array, array.shape, None)

    def layer(array, k):
        return (array, array.shape, k)

    def rows_out(cols_, dtype, rows=chunk, total=tokens):
        return ((total, cols_), dtype, (rows, cols_), lambda i: (i, 0))

    def sums(*shape, dtype=F32):
        return (shape, dtype, shape, None)

    def vec(k):
        return layer(vecs, k)

    scalar = (core, None, None)

    x1, nw, mw, ow, x2 = call(
        window_forward_kernel,
        units,
        [
            (x0, (WIN, width, chans), lambda i: (i, 0, 0)),
            (x0, (1, width, chans), lambda i: (jnp.maximum(i * WIN - 1, 0), 0, 0)),
            (x0, (1, width, chans), lambda i: (jnp.minimum(i * WIN + WIN, height - 1), 0, 0)),
            whole(tok_halo),
            rows_in(mask, unit),
            vec(0),
            layer(mix_w, 0),
            whole(bias0),
            layer(out_w, 0),
            whole(gather),
        ],
        [
            rows_out(chans, F32, unit),
            rows_out(chans, BF16, wrows, units * wrows),
            rows_out(3 * chans, BF16, wrows, units * wrows),
            rows_out(chans, BF16, wrows, units * wrows),
            rows_out(chans, F32, unit),
        ],
        [
            ((unit + 2 * width, chans), F32),
            ((unit, chans), F32),
            ((wrows * chans // LANES, 4 * SLOT), BF16),
        ],
        20,
    )
    x3, x4, n1, h1, s1 = call(
        mlp_forward_kernel,
        chunks,
        near(x2, chunk) + [rows_in(mask, chunk), vec(1), layer(up_w, 0), layer(up_bias, 0), layer(down_w, 0)],
        [
            rows_out(chans, F32),
            rows_out(chans, F32),
            rows_out(chans, BF16),
            rows_out(ff, BF16),
            rows_out(ff, BF16),
        ],
        [((chunk + 2 * width, chans), F32), ((chunk, chans), F32)],
        25,
    )
    x5, n2, m2, gram = call(
        channel_mix_kernel,
        chunks,
        near(x4, chunk) + [rows_in(mask, chunk), vec(2), layer(mix_w, 1), whole(bias1)],
        [
            rows_out(chans, F32),
            rows_out(chans, BF16),
            rows_out(3 * chans, BF16),
            sums(chans // LANES, LANES, LANES),
        ],
        [((chunk + 2 * width, chans), F32)],
        11,
    )
    gram = across(gram)
    o2, x6 = call(
        channel_out_kernel,
        chunks,
        [
            rows_in(m2, chunk),
            whole(gram),
            whole(scale),
            rows_in(x5, chunk),
            rows_in(mask, chunk),
            vec(2),
            layer(out_w, 1),
        ],
        [rows_out(chans, BF16), rows_out(chans, F32)],
        [((chunk, chans), F32)],
        7,
    )
    result, g7, mlp1, up_bg1, small7 = call(
        last_mlp_kernel,
        chunks,
        near(x6, chunk)
        + [
            rows_in(mask, chunk),
            vec(3),
            layer(up_w, 1),
            layer(up_bias, 1),
            layer(down_w, 1),
            rows_in(cot, chunk),
        ],
        [
            rows_out(chans, BF16),
            rows_out(chans, F32),
            sums(2 * ff, chans, dtype=BF16),
            sums(8, ff),
            sums(24, chans),
        ],
        [
            ((chunk + 2 * width, chans), F32),
            ((chunk, chans), F32),
            ((chunk, chans), F32),
            ((chunk, chans), F32),
            ((chunk, chans), BF16),
            ((chunk, ff), BF16),
            ((chunk, ff), BF16),
            ((chans, ff), F32),
            ((ff, chans), F32),
        ],
        38,
    )
    result = send_result(result)
    g6, do2, weights_g, out1, conv_g3, small6 = call(
        channel_grad_kernel,
        chunks,
        near(g7, chunk)
        + [
            rows_in(mask, chunk),
            vec(3),
            rows_in(x6, chunk),
            (m2, (chunk, chans), lambda i: (i, 0)),
            rows_in(o2, chunk),
            layer(out_w, 1),
        ],
        [
            rows_out(chans, F32),
            rows_out(chans, BF16),
            sums(chans // LANES, LANES, LANES),
            sums(chans, chans, dtype=BF16),
            sums(72, chans),
            sums(16, chans),
        ],
        [((chunk + 2 * width, chans), F32), ((chunk, chans), BF16), ((chans, chans), F32)],
        13,
    )
    weights_g = across(weights_g)
    g5, mix1, mix_bg1, small5 = call(
        channel_back_kernel,
        chunks,
        [
            rows_in(do2, chunk),
            rows_in(m2, chunk),
            whole(gram),
            whole(weights_g),
            whole(scale),
            rows_in(n2, chunk),
            rows_in(x5, chunk),
            rows_in(g6, chunk),
            rows_in(mask, chunk),
            vec(2),
            layer(mix_w, 1),
        ],
        [
            rows_out(chans, F32),
            sums(3 * chans, chans, dtype=BF16),
            sums(8, 3 * chans),
            sums(16, chans),
        ],
        [((chunk, 3 * chans), BF16), ((chunk, chans), F32), ((3 * chans, chans), F32)],
        16,
    )
    g3, kept0, sent0, up_bg0, conv_g2, small3 = call(
        mlp_back_kernel,
        chunks,
        near(g5, chunk)
        + [
            rows_in(mask, chunk),
            vec(2),
            vec(1),
            rows_in(x4, chunk),
            rows_in(x3, chunk),
            rows_in(n1, chunk),
            rows_in(h1, chunk),
            rows_in(s1, chunk),
            layer(up_w, 0),
            layer(down_w, 0),
            whole(mlp1),
            whole(mix1),
            whole(out1),
            scalar,
        ],
        [
            rows_out(chans, F32),
            sums(2 * ff + 2 * chans, chans, dtype=BF16),
            sums(2 * ff + 2 * chans, chans, dtype=BF16),
            sums(8, ff),
            sums(72, chans),
            sums(32, chans),
        ],
        [
            ((chunk + 2 * width, chans), F32),
            ((chunk, chans), F32),
            ((chunk, chans), BF16),
            ((chunk, chans), F32),
            ((chunk, ff), BF16),
            ((chans, ff), F32),
            ((ff, chans), F32),
        ],
        32,
    )
    mid = share_planes(share_cores(kept0, sent0))
    g1, win0, mix_bg0, conv_g1, small1 = call(
        window_back_kernel,
        units,
        near(g3, unit)
        + [
            rows_in(mask, unit),
            vec(1),
            vec(0),
            rows_in(x2, unit),
            rows_in(x1, unit),
            rows_in(nw, wrows),
            rows_in(mw, wrows),
            rows_in(ow, wrows),
            layer(mix_w, 0),
            layer(out_w, 0),
            whole(gather),
        ],
        [
            rows_out(chans, F32, unit),
            sums(4 * chans, chans, dtype=BF16),
            sums(8, 3 * chans),
            sums(72, chans),
            sums(32, chans),
        ],
        [
            ((unit + 2 * width, chans), F32),
            ((3 * chans, chans), F32),
            ((chans, chans), F32),
            ((unit, chans), F32),
            ((wrows, chans), BF16),
            ((wrows, chans), BF16),
            ((wrows, 3 * chans), BF16),
            ((unit, chans), F32),
            ((wrows * chans // LANES, 4 * SLOT), BF16),
            ((wrows * chans // LANES, 4 * SLOT), BF16),
        ],
        34,
    )
    mid, g1 = lax.optimization_barrier((mid, g1))
    x0_flat = x0.reshape(tokens, chans)
    sums1 = (conv_g1, conv_g2, conv_g3, small1, small3, small5, small6, small7, mix_bg0, mix_bg1, up_bg0, up_bg1)
    half = (win0.shape[0] + SMALL_ROWS) // 2
    tokens_grad, kept, sent = call(
        token_grad_kernel,
        chunks,
        near(g1, chunk)
        + [rows_in(mask, chunk), vec(0), rows_in(x0_flat, chunk), scalar, whole(win0)]
        + [whole(array) for array in sums1],
        [rows_out(chans, BF16), sums(half, chans, dtype=BF16), sums(half, chans, dtype=BF16)],
        [
            ((chunk + 2 * width, chans), F32),
            ((72, chans), F32),
            ((8, chans), F32),
            ((SMALL_ROWS, chans), F32),
        ],
        10,
        after=(result, *mid),
    )
    return result, tokens_grad, mid, kept, sent


def small_sums(
    core, win0, conv0, conv1, conv2, conv3, s0, s1, s3, s5, s6, s7, mix0, mix1, up0, up1,
    kept, sent, rows,
):
    chans = rows.shape[1]
    rows[...] = jnp.zeros_like(rows)
    place = 0

    def put(part):
        nonlocal place
        rows[place : place + 1, :] = jnp.sum(part, axis=0, keepdims=True)
        place += 1

    for conv in (conv0, conv1, conv2, conv3):
        for k in range(9):
            put(conv[8 * k : 8 * k + 8, :])
    for ref, at in (
        (s0, 0), (s1, 0), (s3, 0), (s6, 0),
        (s1, 16), (s3, 16), (s5, 0), (s7, 8),
        (s1, 24), (s3, 24), (s5, 8), (s7, 16),
        (s1, 8), (s6, 8), (s3, 8), (s7, 0),
    ):
        put(ref[at : at + 8, :])
    for ref in (mix0, mix1, up0, up1):
        for col in range(0, ref.shape[1], chans):
            put(ref[:, col : col + chans])
    spread(core, kept, sent, [win0, rows])


def reader(halves, plane, share, offset, stride, members):
    first = halves[0][0][0]
    part = members // 2 * stride
    planes = 2 * first.shape[0] // part
    bits = planes.bit_length() - 1

    def piece(at, take):
        n, inside = divmod(at, share)
        core, n = divmod(n, planes * members)
        owner, member = divmod(n, members)
        late, place = divmod(member * stride + offset + inside, part)
        far = plane ^ owner
        if late:
            far = sum(((far >> k) & 1) << (bits - 1 - k) for k in range(bits))
        near, other = halves[core][late]
        start = (far & (planes // 2 - 1)) * part + place
        rows = pl.ds(pl.multiple_of(start, 16), take)
        return jnp.where(far < planes // 2, near[rows, :], other[rows, :]).astype(F32)

    def read(at, rows):
        parts = []
        while rows:
            take = min(rows, share - at % share)
            parts.append(piece(at, take))
            at, rows = at + take, rows - take
        return parts[0] if len(parts) == 1 else jnp.concatenate(parts, axis=0)

    return read


def plain_reader(first, second):
    half = first.shape[0]

    def read(at, rows):
        parts = []
        if at < half:
            parts.append(first[at : min(at + rows, half), :].astype(F32))
        if at + rows > half:
            parts.append(second[max(at - half, 0) : at + rows - half, :].astype(F32))
        return parts[0] if len(parts) == 1 else jnp.concatenate(parts, axis=0)

    return read


def put_attention(read, mix_w, out_w):
    chans = out_w.shape[1]
    for k in range(3):
        mix_w[0, :, k * chans : (k + 1) * chans] = read(k * chans, chans)
    out_w[0] = read(3 * chans, chans)


def put_feed(read, at, up_w, down_w):
    chans = down_w.shape[2]
    blocks = up_w.shape[2] // chans
    for k in range(blocks):
        up_w[0, :, k * chans : (k + 1) * chans] = read(at + k * chans, chans)
    for k in range(blocks):
        down_w[0, k * chans : (k + 1) * chans, :] = read(at + (blocks + k) * chans, chans)


def final_kernel(
    core, plane, *refs, shares, members,
):
    inputs, outs, rows = refs[:-15], refs[-15:-1], refs[-1]
    (
        mix_w, out_w, up_w, down_w, conv_w, conv_b, gain, shift, last_shift, win_b, chan_b, out_b, up_b, down_b,
    ) = outs
    layer = pl.program_id(0)
    chans = inputs[0].shape[1]
    feed_rows = 2 * up_w.shape[2]
    blocks = up_b.shape[1] // chans
    mid_share, late_share = shares
    stride = mid_share + late_share
    count = len(inputs) // 2
    here, there = inputs[:count], inputs[count:]

    for flag in range(2):
        halves = (here, there) if flag == 0 else (there, here)
        if count == 2:
            mid, late = (plain_reader(*pair) for pair in zip(*halves))
        else:
            pairs = tuple((half[0:2], half[2:4]) for half in halves)
            mid = reader(pairs, plane[0], mid_share, 0, stride, members)
            late = reader(pairs, plane[0], late_share, mid_share, stride, members)

        @pl.when((core[0] == flag) & (layer == 0))
        def _():
            put_attention(late, mix_w, out_w)
            put_feed(lambda at, count: mid(feed_rows + 4 * chans + at, count), 0, up_w, down_w)
            rows[...] = late(4 * chans, SMALL_ROWS)

        @pl.when((core[0] == flag) & (layer == 1))
        def _():
            put_attention(lambda at, count: mid(feed_rows + at, count), mix_w, out_w)
            put_feed(mid, 0, up_w, down_w)

    @pl.when(layer == 0)
    def _():
            at = 0
            for k in range(4):
                for i in range(3):
                    for j in range(3):
                        conv_w[i, j, k : k + 1, :] = rows[at : at + 1, :]
                        at += 1
            for ref in (conv_b, gain):
                ref[...] = rows[at : at + 4, :]
                at += 4
            shift[...] = rows[at : at + 3, :]
            last_shift[...] = rows[at + 3, :]
            at += 4
            for ref in (out_b, down_b):
                ref[...] = rows[at : at + 2, :]
                at += 2
            win_b[:chans] = rows[at, :]
            win_b[chans:] = rows[at + 2, :]
            for k in range(3):
                chan_b[k * chans : (k + 1) * chans] = rows[at + 3 + k, :]
            at += 6
            for k in range(2):
                for i in range(blocks):
                    up_b[k : k + 1, i * chans : (i + 1) * chans] = rows[at : at + 1, :]
                    at += 1


def assemble(core, plane, arrays, shares, members, ff):
    chans = arrays[0].shape[1]
    shapes = [
        (2, chans, 3 * chans), (2, chans, chans), (2, chans, ff), (2, ff, chans),
        (3, 3, 4, chans), (4, chans), (4, chans), (3, chans), (chans,),
        (2 * chans,), (3 * chans,), (2, chans), (2, ff), (2, chans),
    ]

    def out_spec(shape):
        if len(shape) == 3:
            return pl.BlockSpec((1,) + shape[1:], lambda i: (i, 0, 0))
        return pl.BlockSpec(shape, lambda i: (0,) * len(shape))

    (
        mix_w, out_w, up_w, down_w, conv_w, conv_b, gain, shift, last_shift, win_b, chan_b, out_b, up_b, down_b,
    ) = pl.pallas_call(
        functools.partial(final_kernel, shares=shares, members=members),
        grid=(2,),
        in_specs=[pl.BlockSpec(memory_space=pltpu.SMEM)] * 2
        + [pl.BlockSpec(x.shape, lambda i: (0, 0), pipeline_mode=pl.Buffered(1)) for x in arrays],
        out_specs=[out_spec(shape) for shape in shapes],
        out_shape=[jax.ShapeDtypeStruct(shape, F32) for shape in shapes],
        scratch_shapes=[pltpu.VMEM((SMALL_ROWS, chans), F32)],
        compiler_params=pltpu.CompilerParams(vmem_limit_bytes=VMEM_LIMIT),
    )(core, plane, *arrays)
    return (
        conv_w.transpose(2, 0, 1, 3), conv_b, gain, shift, last_shift, mix_w,
        win_b, chan_b, out_w, out_b, up_w, up_b, down_w, down_b,
    )


def split_kernel(me, *refs, terms):
    outs = refs[terms:]
    rows = outs[0].shape[0]
    for step, out in enumerate(outs):
        at = pl.multiple_of((me[0] ^ step) * rows, 16)
        total = refs[0][pl.ds(at, rows), :].astype(F32)
        for ref in refs[1:terms]:
            total = total + ref[pl.ds(at, rows), :].astype(F32)
        out[...] = total.astype(BF16)


def split_sum(terms, me, size):
    rows, chans = terms[0].shape
    rows //= size
    if rows % 16 or rows < 512:
        total = functools.reduce(lambda x, y: x + y, [term.astype(F32) for term in terms]).astype(BF16)
        return [lax.dynamic_slice_in_dim(total, (me ^ step) * rows, rows, 0) for step in range(size)]
    return pl.pallas_call(
        functools.partial(split_kernel, terms=len(terms)),
        in_specs=[pl.BlockSpec(memory_space=pltpu.SMEM)] + [pl.BlockSpec(memory_space=pltpu.VMEM)] * len(terms),
        out_shape=[jax.ShapeDtypeStruct((rows, chans), BF16)] * size,
        compiler_params=pltpu.CompilerParams(vmem_limit_bytes=VMEM_LIMIT),
    )(me.astype(jnp.int32).reshape(1), *terms)


def widen_kernel(here, *refs):
    out = refs[-1]
    cols = out.shape[2]
    for step, part in enumerate(refs[:-1]):

        @pl.when(pl.program_id(0) == step)
        def _():
            out[0] = part[:, :cols, :]


def widen(parts, here, cols):
    images = len(parts)
    height, width, chans = parts[0].shape
    return pl.pallas_call(
        widen_kernel,
        grid_spec=pltpu.PrefetchScalarGridSpec(
            num_scalar_prefetch=1,
            grid=(images,),
            in_specs=[pl.BlockSpec(x.shape, lambda i, at: (0, 0, 0), pipeline_mode=pl.Buffered(1)) for x in parts],
            out_specs=pl.BlockSpec(
                (1, height, cols, chans), lambda i, at: ((at[0] + images - i) % images, 0, 0, 0)
            ),
        ),
        out_shape=jax.ShapeDtypeStruct((images, height, cols, chans), BF16),
        compiler_params=pltpu.CompilerParams(vmem_limit_bytes=VMEM_LIMIT),
    )(here.astype(jnp.int32).reshape(1), *parts)


def local(
    tokens, heights, conv_weight, conv_bias, norm_gain, norm_shift, mix_weight, window_bias, channel_bias,
    out_weight, out_bias, up_weight, up_bias, down_weight, down_bias, cotangent,
):
    images, height, cols, chans = tokens.shape
    count = lax.axis_size("rows")
    place = lax.axis_index("rows")
    width = -(-cols // 8) * 8
    groups = count // images
    members = [[g * images + j for j in range(images)] for g in range(groups)]
    rows_here = images * height
    level = lax.dynamic_index_in_dim(heights, place % images, 0, keepdims=False)
    open_rows = heights * 7 - place * height

    def pad_image(field):
        inside = jnp.arange(height, dtype=jnp.int32)[None, :] < open_rows[:, None]
        field = jnp.where(inside[:, :, None, None], field, jnp.zeros((), field.dtype))
        return jnp.pad(field, ((0, 0), (0, 0), (0, width - cols), (0, 0)))

    def spread_image(field):
        field = lax.all_to_all(field, "rows", 0, 0, axis_index_groups=members, tiled=True)
        return field.reshape(rows_here, width, chans)

    def scatter_image(field):
        field = field.reshape(images, height, width, chans)
        field = lax.all_to_all(field, "rows", 0, 0, axis_index_groups=members, tiled=True)
        return field[:, :, :cols]

    def halo_of(field):
        flat = field.reshape(rows_here * width, chans)
        if groups == 1:
            return jnp.zeros((2 * width, chans), F32)
        down = [(i, i + images) for i in range(count - images)]
        up = [(i + images, i) for i in range(count - images)]
        above = lax.ppermute(flat[-width:].astype(BF16), "rows", down)
        below = lax.ppermute(flat[:width].astype(BF16), "rows", up)
        return jnp.concatenate([above, below], axis=0).astype(F32)

    def across(value):
        if groups == 1:
            return value
        other = [[j + g * images for g in range(groups)] for j in range(images)]
        return lax.psum(value, "rows", axis_index_groups=other)

    row = jnp.arange(rows_here * width, dtype=jnp.int32) // width + place // images * rows_here
    col = jnp.arange(rows_here * width, dtype=jnp.int32) % width
    mask = ((row < level * 7) & (col < cols)).astype(F32)
    mask = jnp.broadcast_to(mask[:, None], (rows_here * width, LANES))
    scale = lax.rsqrt((level * 7 * cols).astype(F32))
    scale = jnp.broadcast_to(scale, (8, LANES))
    small = prepare(conv_weight, conv_bias, norm_gain, norm_shift, out_bias, down_bias, up_bias)
    small += (
        jnp.concatenate([window_bias[:chans], jnp.zeros((chans,), BF16), window_bias[chans:]]).astype(F32)[None],
        channel_bias.astype(F32)[None],
    )
    field, cotangent = lax.optimization_barrier((pad_image(tokens), cotangent))
    x0 = spread_image(field)
    cot, small, mask, scale = lax.optimization_barrier((pad_image(cotangent), small, mask, scale))
    cot = spread_image(cot).reshape(rows_here * width, chans)

    def exchange(part, axis, step):
        size = lax.axis_size(axis)
        return lax.ppermute(part, axis, [(i, i ^ step) for i in range(size)])

    core = lax.axis_index("core").astype(jnp.int32).reshape(1)

    def share(terms, axis):
        size = lax.axis_size(axis)
        pieces = split_sum(terms, lax.axis_index(axis), size)
        return [pieces[0]] + [exchange(pieces[step], axis, step) for step in range(1, size)]

    def share_cores(kept, sent):
        return [kept, exchange(sent, "core", 1)]

    def total(terms):
        return functools.reduce(lambda x, y: x + y, [term.astype(F32) for term in terms]).astype(BF16)

    def gather(part, axis):
        size, me = lax.axis_size(axis), lax.axis_index(axis)
        rows = part.shape[0]
        out = jnp.zeros((size * rows, part.shape[1]), part.dtype)
        for step in range(size):
            got = part if step == 0 else exchange(part, axis, step)
            out = lax.dynamic_update_slice_in_dim(out, got, (me ^ step) * rows, 0)
        return out

    def join(part, other):
        rows = part.shape[0]
        out = jnp.zeros((2 * rows, part.shape[1]), part.dtype)
        out = lax.dynamic_update_slice_in_dim(out, part, 0, 0)
        return lax.dynamic_update_slice_in_dim(out, other, rows, 0)

    def send_tokens(field):
        field = field.reshape(images, height, width, chans)
        here = place % images
        parts = []
        for step in range(images):
            part = lax.dynamic_index_in_dim(field, (here + step) % images, 0, keepdims=False)
            if step:
                pairs = [(g * images + j, g * images + (j + step) % images) for g in range(groups) for j in range(images)]
                part = lax.ppermute(part, "rows", pairs)
            parts.append(part)
        return parts

    weights = (mix_weight, out_weight, up_weight, down_weight)
    result, tokens_grad, mid, kept, sent = image_block(
        x0, cot, halo_of(x0), mask, scale, halo_of, across, weights, small, cols, core,
        scatter_image, share_cores, lambda terms: share(terms, "plane"),
    )
    together = lax.optimization_barrier
    tokens_grad = send_tokens(tokens_grad)
    mid = share(mid, "rows")
    kept, sent, mid = together((kept, sent, mid))
    late = share(share_cores(kept, sent), "plane")
    late, tokens_grad[2:3] = together((late, tokens_grad[2:3]))
    late = total(share(late, "rows"))
    mid = total(mid)
    shares = (mid.shape[0], late.shape[0])
    block = gather(jnp.concatenate([mid, late], axis=0), "rows")
    members = lax.axis_size("rows")
    bits = lax.axis_size("plane").bit_length() - 1
    half = block.shape[0] // 2
    parts = [block[:half], block[half:]]
    aligned = all(rows % 16 == 0 for rows in shares)
    if not aligned:
        block = gather(block, "plane").reshape(-1, sum(shares), chans)
        arrays = [block[:, : shares[0]].reshape(-1, chans), block[:, shares[0] :].reshape(-1, chans)]
        tokens_grad = widen(tokens_grad, place % images, cols)
    for k in range(bits if aligned else 0):
        others = [exchange(part, "plane", 1 << bit) for part, bit in zip(parts, (k, bits - 1 - k))]
        if k == bits - 1:
            tokens_grad = widen(tokens_grad, place % images, cols)
            others, tokens_grad = together((others, tokens_grad))
        if k + 1 < bits:
            parts = [join(part, other) for part, other in zip(parts, others)]
        else:
            arrays = [parts[0], others[0], parts[1], others[1]]
    arrays += [exchange(array, "core", 1) for array in arrays]
    plane = lax.axis_index("plane").astype(jnp.int32).reshape(1)
    return result, tokens_grad.astype(F32), *assemble(core, plane, arrays, shares, members, up_weight.shape[2])


def solution(mesh):
    planes = mesh.shape["dp"] // 2
    fine = Mesh(mesh.devices.reshape(planes, 2, mesh.shape["rows"]), ("plane", "core", "rows"))
    dp = ("plane", "core")
    split = P(dp, "rows", None, None)
    in_specs = (split, P(dp)) + (P(),) * 13 + (split,)
    out_specs = (split, split) + (P(),) * 14
    return jax.shard_map(local, mesh=fine, in_specs=in_specs, out_specs=out_specs, check_vma=False)
```
